32 devices in a mesh: dp: 4 (over x, core), tensor: 8 (over z, y).
Axes of the slice: x: 2, y: 2, z: 4, core: 2. Of those that a mesh axis runs over, the one named last changes fastest.
Arguments:
- inputs: bfloat16 [2, 11776, 1152], P(None, ('dp', 'tensor')), may hold values from -6 to 6
- pad_mask: int32 [2, 16, 736], P(None, 'dp'), may hold values from 0 to 1, as said below
- cotangent: bfloat16 [2, 11776, 1152], P(None, ('dp', 'tensor')), may hold values from -6 to 6
- attn_norm_gain: float32 [1152], replicated, may hold values from 0.5 to 1.5
- attn_norm_shift: float32 [1152], replicated, may hold values from -1.5 to 1.5
- w_query: bfloat16 [1152, 1152], P('dp', 'tensor'), may hold values from -0.1875 to 0.1875
- b_query: float32 [1152], replicated, may hold values from -1.5 to 1.5
- w_key: bfloat16 [1152, 1152], P('dp', 'tensor'), may hold values from -0.1875 to 0.1875
- w_value: bfloat16 [1152, 1152], P('dp', 'tensor'), may hold values from -0.1875 to 0.1875
- b_value: float32 [1152], replicated, may hold values from -1.5 to 1.5
- w_out: bfloat16 [1152, 1152], P('tensor', 'dp'), may hold values from -3 to 3
- b_out: float32 [1152], replicated, may hold values from -1.5 to 1.5
- mlp_norm_gain: float32 [1152], replicated, may hold values from 0.5 to 1.5
- mlp_norm_shift: float32 [1152], replicated, may hold values from -1.5 to 1.5
- w_up: bfloat16 [1152, 4304], P('dp', 'tensor'), may hold values from -0.1875 to 0.1875
- b_up: float32 [4304], replicated, may hold values from -1.5 to 1.5
- w_down: bfloat16 [4304, 1152], P('tensor', 'dp'), may hold values from -0.09375 to 0.09375
- b_down: float32 [1152], replicated, may hold values from -1.5 to 1.5
Outputs:
- layer_out: bfloat16 [2, 11776, 1152], P(None, ('dp', 'tensor'))
- input_grad: float32 [2, 11776, 1152], P(None, ('dp', 'tensor'))
- grad_attn_norm_gain: float32 [1152], replicated
- grad_attn_norm_shift: float32 [1152], replicated
- grad_w_query: float32 [1152, 1152], P('dp', 'tensor')
- grad_b_query: float32 [1152], P('tensor')
- grad_w_key: float32 [1152, 1152], P('dp', 'tensor')
- grad_w_value: float32 [1152, 1152], P('dp', 'tensor')
- grad_b_value: float32 [1152], P('tensor')
- grad_w_out: float32 [1152, 1152], P('tensor', 'dp')
- grad_b_out: float32 [1152], replicated
- grad_mlp_norm_gain: float32 [1152], replicated
- grad_mlp_norm_shift: float32 [1152], replicated
- grad_w_up: float32 [1152, 4304], P('dp', 'tensor')
- grad_b_up: float32 [4304], replicated
- grad_w_down: float32 [4304, 1152], P('tensor', 'dp')
- grad_b_down: float32 [1152], replicated
The draws below stay inside these ranges and needn't reach their ends.
Inputs may be any that keep to these rules, and one draw needn't show every extreme that they name: `pad_mask`: each slot's ones form a prefix of 368 to 729 positions, so its last 7 positions are 0; numbering slots m * 16 + j, slots 0, 4, 8 and so on have 736 - 7 ones and slots 1, 5, 9 and so on have 736 // 2.
All inputs are finite; a program needn't handle non-finite values.
Results may differ from the reference program's by a relative error of at most 0.015.
Values may be sent and summed in bfloat16 or wider, within the bound.
No kernel may reach another device: no remote copies, remote signals or barrier semaphores. Data moves between devices by JAX's collectives and lax.ppermute only.
A program may use at most 384 MiB of HBM per device.

```python
from functools import partial
import jax
import jax.numpy as jnp
from jax import lax

D = 1152
HEADS = 16
HEAD_DIM = 72
FF = 4304
LEN = 736
PAD = 7
MICRO = 2
GROUP_SLOTS = 16
SLOTS = 32


def draw_pad_mask(key, part):
    lengths = jax.random.randint(key, (SLOTS,), LEN // 2, LEN - PAD + 1)
    slot_ids = jnp.arange(SLOTS)
    lengths = jnp.where(slot_ids % 4 == 0, LEN - PAD, lengths)
    lengths = jnp.where(slot_ids % 4 == 1, LEN // 2, lengths)
    positions = jnp.arange(LEN)
    filled = (positions[None, :] < lengths[:, None]).astype(jnp.int32)
    return filled.reshape(MICRO, GROUP_SLOTS, LEN)


def shard_levels(key, dims, split, smallest, largest):
    def one(dim, parts):
        draws = jax.random.uniform(jax.random.fold_in(jax.random.fold_in(key, 6), dim), (parts,), jnp.float32, smallest / len(split), largest / len(split))
        return jnp.repeat(jnp.exp(draws), dims[dim] // parts).reshape((-1,) + (1,) * (len(dims) - dim - 1))

    gain = one(*split[0])
    for cut in split[1:]:
        gain = gain * one(*cut)
    return gain


def normal_values(key, dims, deviation, limit, cuts=(), dtype=jnp.bfloat16):
    drawn = jax.random.normal(key, dims, jnp.float32) * deviation
    if len(cuts) > 0:
        drawn = shard_levels(key, dims, cuts, -0.22, 0.18) * drawn
    return jnp.clip(drawn, min=-limit, max=limit).astype(dtype)


def setup_inputs(seed: int = 0) -> dict:
    arg_keys = jax.random.split(jax.random.key(seed), 19)
    inputs = normal_values(arg_keys[0], (MICRO, GROUP_SLOTS * LEN, D), 1.0, 6.0, ((1, 32),))
    pad_mask = draw_pad_mask(jax.random.fold_in(arg_keys[18], 71), 0)
    cotangent = normal_values(arg_keys[2], (MICRO, GROUP_SLOTS * LEN, D), 1.0, 6.0, ((1, 32),))
    attn_norm_gain = jnp.clip(1.0 + 0.1 * jax.random.normal(arg_keys[3], (D,), jnp.float32), 0.5, 1.5)
    attn_norm_shift = normal_values(arg_keys[4], (D,), 0.3, 1.5, (), jnp.float32)
    w_query = normal_values(arg_keys[5], (D, D), D ** -0.5, 0.1875, ((0, 4), (1, 8)))
    b_query = normal_values(arg_keys[6], (D,), 0.3, 1.5, (), jnp.float32)
    w_key = normal_values(arg_keys[7], (D, D), D ** -0.5, 0.1875, ((0, 4), (1, 8)))
    w_value = normal_values(arg_keys[8], (D, D), D ** -0.5, 0.1875, ((0, 4), (1, 8)))
    b_value = normal_values(arg_keys[9], (D,), 0.3, 1.5, (), jnp.float32)
    w_out = normal_values(arg_keys[10], (D, D), (max(D // 288, 1)) ** -0.5, 3.0, ((0, 8), (1, 4)))
    b_out = normal_values(arg_keys[11], (D,), 0.3, 1.5, (), jnp.float32)
    mlp_norm_gain = jnp.clip(1.0 + 0.1 * jax.random.normal(arg_keys[12], (D,), jnp.float32), 0.5, 1.5)
    mlp_norm_shift = normal_values(arg_keys[13], (D,), 0.3, 1.5, (), jnp.float32)
    w_up = normal_values(arg_keys[14], (D, FF), D ** -0.5, 0.1875, ((0, 4), (1, 8)))
    b_up = normal_values(arg_keys[15], (FF,), 0.3, 1.5, (), jnp.float32)
    w_down = normal_values(arg_keys[16], (FF, D), FF ** -0.5, 0.09375, ((0, 8), (1, 4)))
    b_down = normal_values(arg_keys[17], (D,), 0.3, 1.5, (), jnp.float32)
    return {"inputs": inputs, "pad_mask": pad_mask, "cotangent": cotangent, "attn_norm_gain": attn_norm_gain, "attn_norm_shift": attn_norm_shift, "w_query": w_query, "b_query": b_query, "w_key": w_key, "w_value": w_value, "b_value": b_value, "w_out": w_out, "b_out": b_out, "mlp_norm_gain": mlp_norm_gain, "mlp_norm_shift": mlp_norm_shift, "w_up": w_up, "b_up": b_up, "w_down": w_down, "b_down": b_down}


norm_eps = 1e-06
masked_score = -1000000000.0

@jax.custom_vjp
def low(v):
    return lax.optimization_barrier(v.astype(jnp.bfloat16)).astype(jnp.float32)

@jax.custom_vjp
def low_back(v):
    return v

def low_keep(v):
    return (low(v), None)

def low_pass(kept, grad):
    return (grad,)

def back_keep(v):
    return (v, None)

def back_low(kept, grad):
    return (low(grad),)
low.defvjp(low_keep, low_pass)
low_back.defvjp(back_keep, back_low)

def product(left_side, right_side):
    return jnp.dot(left_side, right_side, precision=lax.Precision.HIGHEST, preferred_element_type=jnp.float32)

def layer_norm(values, norm_gain, norm_shift):
    row_mean = lax.optimization_barrier(jnp.mean(values, axis=-1, keepdims=True))
    centred = values - row_mean
    variance = lax.optimization_barrier(jnp.mean(centred * centred, axis=-1, keepdims=True))
    return centred * lax.rsqrt(variance + norm_eps) * norm_gain + norm_shift

def attend_pairs(members):
    queries, keys_low, values_low, key_valid = members
    raw_scores = low_back(jnp.einsum('slhe,smhe->shlm', queries, keys_low, precision=lax.Precision.HIGHEST))
    scores = jnp.where(key_valid[:, None, None, :] > 0, raw_scores * HEAD_DIM ** (-0.5), masked_score)
    attn_probs = low(jax.nn.softmax(scores, axis=-1))
    return jnp.einsum('shlm,smhe->slhe', attn_probs, values_low, precision=lax.Precision.HIGHEST)

def layer_forward(pad_mask, inputs, attn_norm_gain, attn_norm_shift, w_query, b_query, w_key, w_value, b_value, w_out, b_out, mlp_norm_gain, mlp_norm_shift, w_up, b_up, w_down, b_down):
    flat_rows = inputs.reshape(-1, D)
    normed_first = low(layer_norm(flat_rows, attn_norm_gain, attn_norm_shift))
    queries = low_back(low(product(normed_first, w_query) + b_query))
    keys_low = low_back(low(product(normed_first, w_key)))
    values_low = low_back(low(product(normed_first, w_value) + b_value))
    pair_shape = (SLOTS // 2, 2, LEN, HEADS, HEAD_DIM)
    attended = lax.map(jax.checkpoint(attend_pairs), (queries.reshape(pair_shape), keys_low.reshape(pair_shape), values_low.reshape(pair_shape), pad_mask.reshape(SLOTS // 2, 2, LEN)))
    attended = low_back(low(attended.reshape(-1, D)))
    branch = low_back(product(attended, w_out) + b_out)
    middle = flat_rows + branch
    normed_second = low(layer_norm(middle, mlp_norm_gain, mlp_norm_shift))
    pre_act = low_back(product(normed_second, w_up) + b_up)
    active = low(jax.nn.gelu(pre_act, approximate=True))
    mlp_branch = low_back(product(active, w_down) + b_down)
    return (middle + mlp_branch).reshape(MICRO, GROUP_SLOTS * LEN, D)

def reference(inputs, pad_mask, cotangent, attn_norm_gain, attn_norm_shift, w_query, b_query, w_key, w_value, b_value, w_out, b_out, mlp_norm_gain, mlp_norm_shift, w_up, b_up, w_down, b_down):
    as_float = jnp.float32
    result, pullback = jax.vjp(partial(layer_forward, pad_mask), inputs.astype(as_float), attn_norm_gain.astype(as_float), attn_norm_shift.astype(as_float), w_query.astype(as_float), b_query.astype(as_float), w_key.astype(as_float), w_value.astype(as_float), b_value.astype(as_float), w_out.astype(as_float), b_out.astype(as_float), mlp_norm_gain.astype(as_float), mlp_norm_shift.astype(as_float), w_up.astype(as_float), b_up.astype(as_float), w_down.astype(as_float), b_down.astype(as_float))
    gradients = pullback(cotangent.astype(as_float))
    return (result.astype(jnp.bfloat16), gradients[0], gradients[1], gradients[2], gradients[3], gradients[4], gradients[5], gradients[6], gradients[7], gradients[8], gradients[9], gradients[10], gradients[11], gradients[12], gradients[13], gradients[14], gradients[15])
```

```python
from functools import partial

import jax
import jax.numpy as jnp
from jax import lax
from jax.experimental import pallas as pl
from jax.experimental.pallas import tpu as pltpu
from jax.sharding import PartitionSpec as P

HEAD_DIM = 72
norm_eps = 1e-06
masked_score = -1000000000.0
low = jnp.bfloat16
wide = jnp.float32
score_scale = HEAD_DIM**-0.5
log2_e = 1.4426950408889634
gelu_scale = 0.7978845608028654
gelu_cube = 0.044715
everyone = ("dp", "tensor")


def product(left, right, left_dim, right_dim):
    return lax.dot_general(
        left, right, (((left_dim,), (right_dim,)), ((), ())), preferred_element_type=wide
    )


def norm_stats(values):
    row_mean = jnp.mean(values, axis=-1, keepdims=True)
    centred = values - row_mean
    inv_scale = lax.rsqrt(jnp.mean(centred * centred, axis=-1, keepdims=True) + norm_eps)
    return centred * inv_scale, inv_scale


def norm_backward(grad_rows, unit_rows, inv_scale, norm_gain):
    grad_unit = grad_rows * norm_gain
    mean_grad = jnp.mean(grad_unit, axis=-1, keepdims=True)
    mean_along = jnp.mean(grad_unit * unit_rows, axis=-1, keepdims=True)
    grad_values = inv_scale * (grad_unit - mean_grad - unit_rows * mean_along)
    return (grad_values, jnp.sum(grad_rows * unit_rows, axis=0), jnp.sum(grad_rows, axis=0))


def attend_kernel(heads, query_ref, key_ref, value_ref, bias_ref, out_ref, total_ref):
    for head in range(heads):
        rows = slice(head * HEAD_DIM, (head + 1) * HEAD_DIM)
        scores = product(key_ref[rows, :], query_ref[rows, :], 0, 0) * (score_scale * log2_e)
        scores = scores + bias_ref[...]
        top = jnp.max(scores, axis=0, keepdims=True)
        weights = jnp.exp2(scores - top)
        total = jnp.sum(weights, axis=0, keepdims=True)
        mixed = product(value_ref[rows, :], weights.astype(low), 1, 0)
        out_ref[rows, :] = (mixed * (1.0 / total)).astype(low)
        total_ref[head] = top + jnp.log2(total)


def attend_back_kernel(
    heads,
    query_ref,
    key_ref,
    value_ref,
    bias_ref,
    out_ref,
    total_ref,
    grad_ref,
    grad_query_ref,
    grad_key_ref,
    grad_value_ref,
):
    for head in range(heads):
        rows = slice(head * HEAD_DIM, (head + 1) * HEAD_DIM)
        query, key, value, grad = (
            query_ref[rows, :],
            key_ref[rows, :],
            value_ref[rows, :],
            grad_ref[rows, :],
        )
        scores = product(key, query, 0, 0) * (score_scale * log2_e) + bias_ref[...]
        probs = jnp.exp2(scores - total_ref[head])
        grad_probs = product(value, grad, 0, 0)
        along = jnp.sum(
            grad.astype(wide) * out_ref[rows, :].astype(wide), axis=0, keepdims=True
        )
        grad_raw = (probs * (grad_probs - along)).astype(low)
        grad_value_ref[rows, :] = product(grad, probs.astype(low), 1, 1).astype(low)
        grad_query_ref[rows, :] = (product(key, grad_raw, 1, 0) * score_scale).astype(low)
        grad_key_ref[rows, :] = (product(query, grad_raw, 1, 1) * score_scale).astype(low)


def attend(projected, bias, heads, step_heads):
    tokens = projected.shape[1]
    steps = heads // step_heads
    part = lambda place: pl.BlockSpec(
        (HEAD_DIM * step_heads, tokens), lambda i, place=place: (place * steps + i, 0)
    )
    return pl.pallas_call(
        partial(attend_kernel, step_heads),
        grid=(steps,),
        in_specs=[part(0), part(1), part(2), pl.BlockSpec((tokens, 1), lambda i: (0, 0))],
        out_specs=[part(0), pl.BlockSpec((step_heads, 1, tokens), lambda i: (i, 0, 0))],
        out_shape=[
            jax.ShapeDtypeStruct((heads * HEAD_DIM, tokens), low),
            jax.ShapeDtypeStruct((heads, 1, tokens), wide),
        ],
        compiler_params=pltpu.CompilerParams(vmem_limit_bytes=48 * 2**20),
        cost_estimate=pl.CostEstimate(
            flops=heads * tokens * tokens * 1024, bytes_accessed=16 * 2**20, transcendentals=0
        ),
        name="attend",
    )(projected, projected, projected, bias)


def attend_back(projected, bias, attended, total, grad, heads, step_heads):
    tokens = projected.shape[1]
    steps = heads // step_heads
    part = lambda place: pl.BlockSpec(
        (HEAD_DIM * step_heads, tokens), lambda i, place=place: (place * steps + i, 0)
    )
    return pl.pallas_call(
        partial(attend_back_kernel, step_heads),
        grid=(steps,),
        in_specs=[
            part(0),
            part(1),
            part(2),
            pl.BlockSpec((tokens, 1), lambda i: (0, 0)),
            part(0),
            pl.BlockSpec((step_heads, 1, tokens), lambda i: (i, 0, 0)),
            part(0),
        ],
        out_specs=[part(0)] * 3,
        out_shape=[jax.ShapeDtypeStruct((heads * HEAD_DIM, tokens), low)] * 3,
        compiler_params=pltpu.CompilerParams(vmem_limit_bytes=48 * 2**20),
        cost_estimate=pl.CostEstimate(
            flops=heads * tokens * tokens * 2048, bytes_accessed=16 * 2**20, transcendentals=0
        ),
        name="attend_back",
    )(projected, projected, projected, bias, attended, total, grad)


def mlp_kernel(
    normed_ref,
    grad_ref,
    up_ref,
    down_ref,
    bias_ref,
    out_ref,
    grad_normed_ref,
    grad_up_ref,
    grad_down_ref,
    grad_bias_ref,
):
    step = pl.program_id(0)
    normed, grad = normed_ref[...], grad_ref[...]
    up, down = up_ref[...], down_ref[...]
    pre_act = product(up, normed, 1, 1) + bias_ref[...]
    square = pre_act * pre_act
    bent = jnp.tanh(gelu_scale * (pre_act + gelu_cube * square * pre_act))
    half = 0.5 * (1.0 + bent)
    active = (pre_act * half).astype(low)
    slope = half + 0.5 * pre_act * (1.0 - bent * bent) * (
        gelu_scale * (1.0 + 3.0 * gelu_cube * square)
    )
    grad_wide = product(down, grad, 1, 1) * slope
    grad_pre = grad_wide.astype(low)
    grad_bias_ref[...] = jnp.sum(grad_wide, axis=1, keepdims=True)
    grad_down_ref[...] = product(active, grad, 1, 0).astype(low)
    grad_up_ref[...] = product(grad_pre, normed, 1, 0).astype(low)
    out_term = product(active, down, 0, 0)
    normed_term = product(grad_pre, up, 0, 0)

    @pl.when(step == 0)
    def first():
        out_ref[...] = out_term
        grad_normed_ref[...] = normed_term

    @pl.when(step > 0)
    def later():
        out_ref[...] += out_term
        grad_normed_ref[...] += normed_term


def mlp(normed, grad, up, down, bias, block):
    tokens, width = normed.shape
    units = up.shape[0]
    whole = pl.BlockSpec((tokens, width), lambda i: (0, 0))
    rows = pl.BlockSpec((block, width), lambda i: (i, 0))
    column = pl.BlockSpec((block, 1), lambda i: (i, 0))
    return pl.pallas_call(
        mlp_kernel,
        grid=(units // block,),
        in_specs=[whole, whole, rows, rows, column],
        out_specs=[whole, whole, rows, rows, column],
        out_shape=[
            jax.ShapeDtypeStruct((tokens, width), wide),
            jax.ShapeDtypeStruct((tokens, width), wide),
            jax.ShapeDtypeStruct((units, width), low),
            jax.ShapeDtypeStruct((units, width), low),
            jax.ShapeDtypeStruct((units, 1), wide),
        ],
        compiler_params=pltpu.CompilerParams(vmem_limit_bytes=60 * 2**20),
        cost_estimate=pl.CostEstimate(
            flops=16 * tokens * width * units, bytes_accessed=64 * 2**20, transcendentals=0
        ),
        name="mlp",
    )(normed, grad, up, down, bias)


def gather_slab(pieces, dp_count):
    rows, part = pieces.shape
    owned = lax.all_to_all(
        pieces.reshape(dp_count, rows // dp_count, part), "dp", 0, 2, tiled=True
    )
    return lax.all_gather(owned[0], everyone, axis=0, tiled=True)


def scatter_slab(terms, dp_count):
    owned = lax.psum_scatter(terms, everyone, scatter_dimension=0, tiled=True)
    rows, width = owned.shape
    back = lax.all_to_all(owned[None], "dp", 2, 0, tiled=True)
    return back.reshape(dp_count * rows, width // dp_count).astype(wide)


def shards(
    dp_count,
    tensor_count,
    inputs,
    pad_mask,
    cotangent,
    attn_norm_gain,
    attn_norm_shift,
    w_query,
    b_query,
    w_key,
    w_value,
    b_value,
    w_out,
    b_out,
    mlp_norm_gain,
    mlp_norm_shift,
    w_up,
    b_up,
    w_down,
    b_down,
):
    half_rows, width = inputs.shape[1:]
    head_cols = w_query.shape[1]
    unit_cols = w_up.shape[1]
    heads = head_cols * tensor_count // HEAD_DIM
    quantum = 8 * dp_count
    slab_units = -(-unit_cols // quantum) * quantum
    tensor_place = lax.axis_index("tensor")
    col_start = tensor_place * head_cols
    side = tensor_place % 2
    pairs = [(place, place ^ 1) for place in range(tensor_count)]

    def swap(values):
        return lax.ppermute(values, "tensor", pairs)

    def one_slot(values):
        kept = lax.dynamic_index_in_dim(values, side, 0, keepdims=False)
        sent = lax.dynamic_index_in_dim(values, 1 - side, 0, keepdims=False)
        return jnp.concatenate([kept, swap(sent)], axis=0)

    def both_micros(values):
        kept = values[:half_rows]
        other = swap(values[half_rows:].astype(low)).astype(values.dtype)
        return jnp.where(side == 0, jnp.stack([kept, other]), jnp.stack([other, kept]))

    def slab_order(values):
        padded = jnp.pad(
            values.reshape(tensor_count, unit_cols), ((0, 0), (0, slab_units - unit_cols))
        )
        return padded.reshape(tensor_count, dp_count, -1).transpose(1, 0, 2).reshape(-1)

    def unit_order(values):
        slabs = values.reshape(dp_count, tensor_count, -1).transpose(1, 0, 2)
        return slabs.reshape(tensor_count, slab_units)[:, :unit_cols].reshape(-1)

    x_slot = one_slot(inputs).astype(wide)
    grad_out = one_slot(cotangent)
    mask_row = lax.dynamic_slice(
        pad_mask, (side, tensor_place // 2, 0), (1, 1, 2 * half_rows)
    ).reshape(2, half_rows)
    mask_row = jnp.where(side == 0, mask_row, mask_row[::-1]).reshape(2 * half_rows, 1)
    bias_col = jnp.where(mask_row > 0, 0.0, masked_score).astype(wide)

    attn_rows = gather_slab(
        jnp.concatenate([w_query.T, w_key.T, w_value.T, w_out], axis=0), dp_count
    )
    kinds = attn_rows.reshape(4, dp_count // 4, tensor_count, -1, width)
    kinds = kinds.transpose(0, 2, 1, 3, 4).reshape(4, -1, width)
    qkv_rows = kinds[:3].reshape(-1, width)
    out_rows = kinds[3]
    unit_pad = ((0, slab_units - unit_cols), (0, 0))
    up_rows = gather_slab(jnp.pad(w_up.T, unit_pad), dp_count)
    down_rows = gather_slab(jnp.pad(w_down, unit_pad), dp_count)

    unit_first, scale_first = norm_stats(x_slot)
    normed_first = (unit_first * attn_norm_gain + attn_norm_shift).astype(low)
    qkv_bias = jnp.concatenate([b_query, jnp.zeros_like(b_query), b_value])
    projected = (product(qkv_rows, normed_first, 1, 1) + qkv_bias[:, None]).astype(low)
    attended, total = attend(projected, bias_col, heads, 4)
    middle = x_slot + (product(attended, out_rows, 0, 0) + b_out)
    unit_second, scale_second = norm_stats(middle)
    normed_second = (unit_second * mlp_norm_gain + mlp_norm_shift).astype(low)
    down_out, grad_normed_second, grad_up, grad_down, grad_up_bias = mlp(
        normed_second,
        grad_out,
        up_rows,
        down_rows,
        slab_order(b_up)[:, None],
        8 * (slab_units // 8),
    )
    layer_out = both_micros((middle + (down_out + b_down)).astype(low))
    grad_w_up = scatter_slab(grad_up, dp_count)[:unit_cols].T
    grad_w_down = scatter_slab(grad_down, dp_count)[:unit_cols]

    grad_mid_norm, gain_second, shift_second = norm_backward(
        grad_normed_second, unit_second, scale_second, mlp_norm_gain
    )
    grad_wide = grad_out.astype(wide)
    grad_middle = grad_wide + grad_mid_norm
    grad_branch = grad_middle.astype(low)
    grad_attended = product(out_rows, grad_branch, 1, 1).astype(low)
    grad_out_rows = product(attended, grad_branch, 1, 0).astype(low)
    grad_query, grad_key, grad_value = attend_back(
        projected, bias_col, attended, total, grad_attended, heads, 4
    )
    grad_projected = jnp.concatenate([grad_query, grad_key, grad_value], axis=0)
    grad_qkv_rows = product(grad_projected, normed_first, 1, 0).astype(low)
    grad_normed_first = product(grad_projected, qkv_rows, 0, 0)
    grad_in_norm, gain_first, shift_first = norm_backward(
        grad_normed_first, unit_first, scale_first, attn_norm_gain
    )
    input_grad = both_micros(grad_middle + grad_in_norm)
    grad_kinds = jnp.concatenate([grad_qkv_rows, grad_out_rows], axis=0)
    grad_kinds = grad_kinds.reshape(4, tensor_count, dp_count // 4, -1, width)
    grad_kinds = grad_kinds.transpose(0, 2, 1, 3, 4).reshape(-1, width)
    attn_owned = scatter_slab(grad_kinds, dp_count).reshape(4, head_cols, -1)

    vectors = [
        gain_first,
        shift_first,
        jnp.sum(grad_query, axis=1, dtype=wide),
        jnp.sum(grad_value, axis=1, dtype=wide),
        jnp.sum(grad_branch, axis=0, dtype=wide),
        gain_second,
        shift_second,
        jnp.sum(grad_wide, axis=0),
        grad_up_bias[:, 0],
    ]
    summed = lax.psum(jnp.concatenate(vectors), everyone)
    small = [summed[i * width : (i + 1) * width] for i in range(8)]
    return (
        layer_out,
        input_grad,
        small[0],
        small[1],
        attn_owned[0].T,
        lax.dynamic_slice_in_dim(small[2], col_start, head_cols),
        attn_owned[1].T,
        attn_owned[2].T,
        lax.dynamic_slice_in_dim(small[3], col_start, head_cols),
        attn_owned[3],
        small[4],
        small[5],
        small[6],
        grad_w_up,
        unit_order(summed[8 * width :]),
        grad_w_down,
        small[7],
    )


def solution(mesh):
    tokens = P(None, ("dp", "tensor"), None)
    columns = P("dp", "tensor")
    rows = P("tensor", "dp")
    return jax.shard_map(
        partial(shards, mesh.shape["dp"], mesh.shape["tensor"]),
        mesh=mesh,
        in_specs=(
            tokens,
            P(None, "dp", None),
            tokens,
            P(),
            P(),
            columns,
            P(),
            columns,
            columns,
            P(),
            rows,
            P(),
            P(),
            P(),
            columns,
            P(),
            rows,
            P(),
        ),
        out_specs=(
            tokens,
            tokens,
            P(),
            P(),
            columns,
            P("tensor"),
            columns,
            columns,
            P("tensor"),
            rows,
            P(),
            P(),
            P(),
            columns,
            P(),
            rows,
            P(),
        ),
        check_vma=False,
    )
```

```python
from functools import partial

import jax
import jax.numpy as jnp
from jax import lax
from jax.experimental import pallas as pl
from jax.experimental.pallas import tpu as pltpu
from jax.sharding import PartitionSpec as P

HEAD_DIM = 72
norm_eps = 1e-06
masked_score = -1000000000.0
low = jnp.bfloat16
wide = jnp.float32
score_scale = HEAD_DIM**-0.5
log2_e = 1.4426950408889634
gelu_scale = 0.7978845608028654
gelu_cube = 0.044715
everyone = ("dp", "tensor")


def product(left, right, left_dim, right_dim):
    return lax.dot_general(
        left, right, (((left_dim,), (right_dim,)), ((), ())), preferred_element_type=wide
    )


def norm_stats(values):
    row_mean = jnp.mean(values, axis=-1, keepdims=True)
    centred = values - row_mean
    inv_scale = lax.rsqrt(jnp.mean(centred * centred, axis=-1, keepdims=True) + norm_eps)
    return centred * inv_scale, inv_scale


def norm_backward(grad_rows, unit_rows, inv_scale, norm_gain):
    grad_unit = grad_rows * norm_gain
    mean_grad = jnp.mean(grad_unit, axis=-1, keepdims=True)
    mean_along = jnp.mean(grad_unit * unit_rows, axis=-1, keepdims=True)
    grad_values = inv_scale * (grad_unit - mean_grad - unit_rows * mean_along)
    return (grad_values, jnp.sum(grad_rows * unit_rows, axis=0), jnp.sum(grad_rows, axis=0))


def attend_kernel(heads, query_ref, key_ref, value_ref, bias_ref, out_ref, total_ref):
    for head in range(heads):
        rows = slice(head * HEAD_DIM, (head + 1) * HEAD_DIM)
        scores = product(key_ref[rows, :], query_ref[rows, :], 0, 0) * (score_scale * log2_e)
        scores = scores + bias_ref[...]
        top = jnp.max(scores, axis=0, keepdims=True)
        weights = jnp.exp2(scores - top)
        total = jnp.sum(weights, axis=0, keepdims=True)
        mixed = product(value_ref[rows, :], weights.astype(low), 1, 0)
        out_ref[rows, :] = (mixed * (1.0 / total)).astype(low)
        total_ref[head] = top + jnp.log2(total)


def attend_back_kernel(
    heads,
    query_ref,
    key_ref,
    value_ref,
    bias_ref,
    out_ref,
    total_ref,
    grad_ref,
    grads_ref,
):
    for head in range(heads):
        rows = slice(head * HEAD_DIM, (head + 1) * HEAD_DIM)
        query, key, value, grad = (
            query_ref[rows, :],
            key_ref[rows, :],
            value_ref[rows, :],
            grad_ref[rows, :],
        )
        scores = product(key, query, 0, 0) * (score_scale * log2_e) + bias_ref[...]
        probs = jnp.exp2(scores - total_ref[head])
        grad_probs = product(value, grad, 0, 0)
        along = jnp.sum(
            grad.astype(wide) * out_ref[rows, :].astype(wide), axis=0, keepdims=True
        )
        grad_raw = (probs * (grad_probs - along)).astype(low)
        grads_ref[2, rows, :] = product(grad, probs.astype(low), 1, 1).astype(low)
        grads_ref[0, rows, :] = (product(key, grad_raw, 1, 0) * score_scale).astype(low)
        grads_ref[1, rows, :] = (product(query, grad_raw, 1, 1) * score_scale).astype(low)


def attend(projected, bias, heads, step_heads):
    tokens = projected.shape[1]
    steps = heads // step_heads
    part = lambda place: pl.BlockSpec(
        (HEAD_DIM * step_heads, tokens), lambda i, place=place: (place * steps + i, 0)
    )
    return pl.pallas_call(
        partial(attend_kernel, step_heads),
        grid=(steps,),
        in_specs=[part(0), part(1), part(2), pl.BlockSpec((tokens, 1), lambda i: (0, 0))],
        out_specs=[part(0), pl.BlockSpec((step_heads, 1, tokens), lambda i: (i, 0, 0))],
        out_shape=[
            jax.ShapeDtypeStruct((heads * HEAD_DIM, tokens), low),
            jax.ShapeDtypeStruct((heads, 1, tokens), wide),
        ],
        compiler_params=pltpu.CompilerParams(vmem_limit_bytes=48 * 2**20),
        cost_estimate=pl.CostEstimate(
            flops=heads * tokens * tokens * 1024, bytes_accessed=16 * 2**20, transcendentals=0
        ),
        name="attend",
    )(projected, projected, projected, bias)


def attend_back(projected, bias, attended, total, grad, heads, step_heads):
    tokens = projected.shape[1]
    steps = heads // step_heads
    part = lambda place: pl.BlockSpec(
        (HEAD_DIM * step_heads, tokens), lambda i, place=place: (place * steps + i, 0)
    )
    return pl.pallas_call(
        partial(attend_back_kernel, step_heads),
        grid=(steps,),
        in_specs=[
            part(0),
            part(1),
            part(2),
            pl.BlockSpec((tokens, 1), lambda i: (0, 0)),
            part(0),
            pl.BlockSpec((step_heads, 1, tokens), lambda i: (i, 0, 0)),
            part(0),
        ],
        out_specs=pl.BlockSpec((3, HEAD_DIM * step_heads, tokens), lambda i: (0, i, 0)),
        out_shape=jax.ShapeDtypeStruct((3, heads * HEAD_DIM, tokens), low),
        compiler_params=pltpu.CompilerParams(vmem_limit_bytes=48 * 2**20),
        cost_estimate=pl.CostEstimate(
            flops=heads * tokens * tokens * 2048, bytes_accessed=16 * 2**20, transcendentals=0
        ),
        name="attend_back",
    )(projected, projected, projected, bias, attended, total, grad)


def mlp_kernel(
    joined,
    carried,
    normed_ref,
    grad_ref,
    up_ref,
    down_ref,
    bias_ref,
    *refs,
):
    if carried:
        out_before, normed_before = refs[:2]
        refs = refs[2:]
    if joined:
        out_ref, grad_normed_ref, grad_rows_ref, grad_bias_ref = refs
        grad_up_ref, grad_down_ref = grad_rows_ref.at[0], grad_rows_ref.at[1]
    else:
        out_ref, grad_normed_ref, grad_up_ref, grad_down_ref, grad_bias_ref = refs
    step = pl.program_id(0)
    normed, grad = normed_ref[...], grad_ref[...]
    up, down = up_ref[...], down_ref[...]
    pre_act = product(up, normed, 1, 1) + bias_ref[...]
    square = pre_act * pre_act
    bent = jnp.tanh(gelu_scale * (pre_act + gelu_cube * square * pre_act))
    half = 0.5 * (1.0 + bent)
    active = (pre_act * half).astype(low)
    slope = half + 0.5 * pre_act * (1.0 - bent * bent) * (
        gelu_scale * (1.0 + 3.0 * gelu_cube * square)
    )
    grad_wide = product(down, grad, 1, 1) * slope
    grad_pre = grad_wide.astype(low)
    grad_bias_ref[...] = jnp.sum(grad_wide, axis=1, keepdims=True)
    grad_down_ref[...] = product(active, grad, 1, 0).astype(low)
    grad_up_ref[...] = product(grad_pre, normed, 1, 0).astype(low)
    out_term = product(active, down, 0, 0)
    normed_term = product(grad_pre, up, 0, 0)

    @pl.when(step == 0)
    def first():
        if carried:
            out_ref[...] = out_before[...] + out_term
            grad_normed_ref[...] = normed_before[...] + normed_term
        else:
            out_ref[...] = out_term
            grad_normed_ref[...] = normed_term

    @pl.when(step > 0)
    def later():
        out_ref[...] += out_term
        grad_normed_ref[...] += normed_term


def mlp(normed, grad, up, down, bias, block, before=None):
    tokens, width = normed.shape
    joined = down is None
    units = up.shape[0] // 2 if joined else up.shape[0]
    steps = units // block
    whole = pl.BlockSpec((tokens, width), lambda i: (0, 0))
    rows = pl.BlockSpec((block, width), lambda i: (i, 0))
    lower = pl.BlockSpec((block, width), lambda i: (steps + i, 0)) if joined else rows
    column = pl.BlockSpec((block, 1), lambda i: (i, 0))
    sums = [jax.ShapeDtypeStruct((tokens, width), wide)] * 2
    if joined:
        grad_specs = [pl.BlockSpec((2, block, width), lambda i: (0, i, 0))]
        grad_shapes = [jax.ShapeDtypeStruct((2, units, width), low)]
    else:
        grad_specs = [rows, rows]
        grad_shapes = [jax.ShapeDtypeStruct((units, width), low)] * 2
    earlier = [] if before is None else list(before)
    return pl.pallas_call(
        partial(mlp_kernel, joined, before is not None),
        grid=(steps,),
        in_specs=[whole, whole, rows, lower, column] + [whole] * len(earlier),
        out_specs=[whole, whole] + grad_specs + [column],
        out_shape=sums + grad_shapes + [jax.ShapeDtypeStruct((units, 1), wide)],
        input_output_aliases={5: 0, 6: 1} if earlier else {},
        compiler_params=pltpu.CompilerParams(vmem_limit_bytes=60 * 2**20),
        cost_estimate=pl.CostEstimate(
            flops=16 * tokens * width * units, bytes_accessed=64 * 2**20, transcendentals=0
        ),
        name="mlp",
    )(normed, grad, up, up if joined else down, bias, *earlier)


def place_kernel(kind_ref, *refs):
    pieces, out_ref, sems = refs[:8], refs[8], refs[9]
    kind = kind_ref[0]
    quarter = out_ref.shape[1] // 4
    copies = []
    for core in range(2):
        near, near_y, far, far_x = pieces[4 * core : 4 * core + 4]
        same, across = kind ^ core, kind ^ (core + 2)
        moves = (
            (near.at[pl.ds(0, quarter)], same, 0),
            (near.at[pl.ds(quarter, quarter)], across, 0),
            (near_y.at[pl.ds(0, quarter)], same, 1),
            (near_y.at[pl.ds(quarter, quarter)], across, 1),
            (far, same, 2),
            (far_x, across, 2),
        )
        for source, target, start in moves:
            copies.append(
                pltpu.make_async_copy(
                    source,
                    out_ref.at[target, pl.ds(start * quarter, source.shape[0])],
                    sems.at[len(copies)],
                )
            )
    for copy in copies:
        copy.start()
    for copy in copies:
        copy.wait()


def place(kind, pieces):
    rows, width = pieces[0].shape
    anywhere = pl.BlockSpec(memory_space=pl.ANY)
    return pl.pallas_call(
        place_kernel,
        in_specs=[pl.BlockSpec(memory_space=pltpu.SMEM)] + [anywhere] * 8,
        out_specs=anywhere,
        out_shape=jax.ShapeDtypeStruct((4, 2 * rows, width), low),
        scratch_shapes=[pltpu.SemaphoreType.DMA((12,))],
        cost_estimate=pl.CostEstimate(
            flops=0, bytes_accessed=32 * rows * width, transcendentals=0
        ),
        name="place",
    )(kind, *pieces)


def kinds_kernel(kind_ref, grads_ref, attended_ref, normed_ref, branch_ref, out_ref):
    kind = pl.program_id(0)

    @pl.when(kind < 3)
    def projections():
        out_ref[0] = product(grads_ref[0], normed_ref[...], 1, 0).astype(low)

    @pl.when(kind == 3)
    def output():
        out_ref[0] = product(attended_ref[...], branch_ref[...], 1, 0).astype(low)


def kinds_grad(kind, grads, attended, normed, branch, block):
    _, rows, tokens = grads.shape
    width = normed.shape[1]
    whole = pl.BlockSpec((tokens, width), lambda k, i, ref: (0, 0))

    def spot(k, i, ref):
        other = k ^ ref[0]
        return ((other & 1) * 2 + (other >> 1), i, 0)

    return pl.pallas_call(
        kinds_kernel,
        grid_spec=pltpu.PrefetchScalarGridSpec(
            num_scalar_prefetch=1,
            grid=(4, rows // block),
            in_specs=[
                pl.BlockSpec((1, block, tokens), lambda k, i, ref: (jnp.minimum(k, 2), i, 0)),
                pl.BlockSpec((block, tokens), lambda k, i, ref: (i, 0)),
                whole,
                whole,
            ],
            out_specs=pl.BlockSpec((1, block, width), spot),
        ),
        out_shape=jax.ShapeDtypeStruct((4, rows, width), low),
        compiler_params=pltpu.CompilerParams(vmem_limit_bytes=40 * 2**20),
        cost_estimate=pl.CostEstimate(
            flops=12 * rows * width * tokens, bytes_accessed=24 * 2**20, transcendentals=0
        ),
        name="kinds_grad",
    )(kind, grads, attended, normed, branch)


def gather_rows(owned):
    return lax.all_gather(owned, everyone, axis=0, tiled=True)


def scatter_rows(terms):
    return lax.psum_scatter(terms, everyone, scatter_dimension=0, tiled=True)


def to_rows(pieces, dp_count):
    rows, part = pieces.shape
    return lax.all_to_all(
        pieces.reshape(dp_count, rows // dp_count, part), "dp", 0, 2, tiled=True
    )[0]


def to_columns(owned, dp_count):
    rows, width = owned.shape
    back = lax.all_to_all(owned[None], "dp", 2, 0, tiled=True)
    return back.reshape(dp_count * rows, width // dp_count).astype(wide)


class Hops:
    def __init__(self, dp_count, tensor_count):
        self.count = dp_count * tensor_count
        self.y, self.z = 1, (2, 4, 6)
        self.core, self.x = tensor_count, 2 * tensor_count
        z1, z2, z3 = self.z
        self.near = (0, z1)
        self.far = (z2, z3)

    def send(self, values, distance):
        pairs = [(place, place ^ distance) for place in range(self.count)]
        return lax.ppermute(values, everyone, pairs)

    def order(self):
        x, y = self.x, self.y
        near = [n ^ p ^ q for q in (0, y) for p in (0, x) for n in self.near]
        far = [n ^ p ^ q for q in (0, x) for p in (0, y) for n in self.far]
        return near + far

    def gather_kinds(self, block):
        z1, z2, z3 = [self.send(block, z) for z in self.z]
        near = jnp.concatenate([block, z1], axis=0)
        far = jnp.concatenate([z2, z3], axis=0)
        near = jnp.concatenate([near, self.send(near, self.x)], axis=0)
        far = jnp.concatenate([far, self.send(far, self.y)], axis=0)
        near_y, far_x = self.send(near, self.y), self.send(far, self.x)
        pieces = [near, near_y, far, far_x]
        return pieces + [self.send(piece, self.core) for piece in pieces]

    def gather_units(self, block):
        half = block.shape[0] // 2

        def join(*blocks):
            return jnp.concatenate(
                [b[: b.shape[0] // 2] for b in blocks] + [b[b.shape[0] // 2 :] for b in blocks],
                axis=0,
            )

        z1, z2, z3 = [self.send(block, z) for z in self.z]
        near, far = join(block, z1), join(z2, z3)
        near, far = join(near, self.send(near, self.x)), join(far, self.send(far, self.y))
        own = join(near, self.send(near, self.y), far, self.send(far, self.x))
        return own, self.send(own, self.core)

    def add(self, *terms):
        total = terms[0].astype(wide)
        for term in terms[1:]:
            total = total + term.astype(wide)
        return total.astype(low)

    def reduce_last(self, near, far, axis):
        take = lambda values, place: lax.index_in_dim(values, place, axis, keepdims=False)
        near = self.add(take(near, 0), self.send(take(near, 1), self.x))
        far = self.add(take(far, 0), self.send(take(far, 1), self.y))
        return self.add(
            take(near, 0),
            self.send(take(near, 1), self.z[0]),
            self.send(take(far, 0), self.z[1]),
            self.send(take(far, 1), self.z[2]),
        )

    def reduce_kinds(self, terms):
        rows = terms.shape[1] // 8
        width = terms.shape[2]
        terms = terms.reshape(2, 2, 8, rows, width)
        sent = self.send(terms[1], self.core)
        near_y = self.add(terms[0, :, 2:4], sent[:, 2:4])
        far_x = self.add(terms[0, 1, 4:8], sent[1, 4:8])
        near_y, far_x = self.send(near_y, self.y), self.send(far_x, self.x)
        near = self.add(terms[0, :, 0:2], sent[:, 0:2], near_y)
        far = self.add(terms[0, 0, 4:8], sent[0, 4:8], far_x)
        near = near.reshape(2, 2, rows, width)
        far = far.reshape(2, 2, rows, width)
        return self.reduce_last(near, far, 0)

    def reduce_units(self, own, sibling):
        width = own.shape[2]
        sent = self.send(sibling, self.core).reshape(2, 4, -1, width)
        own = own.reshape(2, 4, -1, width)
        near_y = self.send(self.add(own[:, 1], sent[:, 1]), self.y)
        far_x = self.send(self.add(own[:, 3], sent[:, 3]), self.x)
        near = self.add(own[:, 0], sent[:, 0], near_y).reshape(2, 2, 2, -1, width)
        far = self.add(own[:, 2], sent[:, 2], far_x).reshape(2, 2, 2, -1, width)
        near = self.add(near[:, 0], self.send(near[:, 1], self.x))
        far = self.add(far[:, 0], self.send(far[:, 1], self.y))
        return self.add(
            near[:, 0],
            self.send(near[:, 1], self.z[0]),
            self.send(far[:, 0], self.z[1]),
            self.send(far[:, 1], self.z[2]),
        )

    def sum_all(self, values):
        for distance in (self.core, self.x, self.y, self.z[0], self.z[1]):
            values = values + self.send(values, distance)
        return values


def shards(
    dp_count,
    tensor_count,
    inputs,
    pad_mask,
    cotangent,
    attn_norm_gain,
    attn_norm_shift,
    w_query,
    b_query,
    w_key,
    w_value,
    b_value,
    w_out,
    b_out,
    mlp_norm_gain,
    mlp_norm_shift,
    w_up,
    b_up,
    w_down,
    b_down,
):
    half_rows, width = inputs.shape[1:]
    head_cols = w_query.shape[1]
    unit_cols = w_up.shape[1]
    heads = head_cols * tensor_count // HEAD_DIM
    quantum = 8 * dp_count
    slab_units = -(-unit_cols // quantum) * quantum
    by_hops = (dp_count, tensor_count) == (4, 8)
    hop_units = 4 * 56 if by_hops else 0
    bulk_units = slab_units - hop_units
    dp_place, tensor_place = lax.axis_index("dp"), lax.axis_index("tensor")
    here = dp_place * tensor_count + tensor_place
    devices = dp_count * tensor_count
    col_start = tensor_place * head_cols
    side = tensor_place % 2
    pairs = [(place, place ^ 1) for place in range(tensor_count)]
    hops = Hops(dp_count, tensor_count)
    kind = dp_place.reshape(1).astype(jnp.int32)

    def swap(values):
        return lax.ppermute(values, "tensor", pairs)

    def one_slot(values):
        kept = lax.dynamic_index_in_dim(values, side, 0, keepdims=False)
        sent = lax.dynamic_index_in_dim(values, 1 - side, 0, keepdims=False)
        return jnp.concatenate([kept, swap(sent)], axis=0)

    def both_micros(values):
        kept = values[:half_rows]
        other = swap(values[half_rows:].astype(low)).astype(values.dtype)
        return jnp.where(side == 0, jnp.stack([kept, other]), jnp.stack([other, kept]))

    if by_hops:
        head_places = tensor_place ^ jnp.array(
            [n ^ q for group in (hops.near, hops.far) for q in (0, hops.y) for n in group]
        )
        hop_order = hops.order()
        hop_order = hop_order + [place ^ hops.core for place in hop_order]
        hop_places = here ^ jnp.array(hop_order)
        hop_find = [hop_order.index(place) for place in range(devices)]

    def to_heads(values):
        if not by_hops:
            return values
        return values.reshape(tensor_count, head_cols)[head_places].reshape(-1)

    def from_heads(values):
        if not by_hops:
            return values
        blocks = values.reshape(tensor_count, head_cols)
        return jnp.zeros_like(blocks).at[head_places].set(blocks).reshape(-1)

    def in_slabs(values, start, stop):
        part = values[:, start:stop].reshape(tensor_count, dp_count, -1)
        return part.transpose(1, 0, 2)

    def from_slabs(values):
        return (
            values.reshape(dp_count, tensor_count, -1).transpose(1, 0, 2).reshape(tensor_count, -1)
        )

    x_slot = one_slot(inputs).astype(wide)
    attn_block = to_rows(
        jnp.concatenate([w_query.T, w_key.T, w_value.T, w_out], axis=0), dp_count
    )
    grad_out = one_slot(cotangent)
    mask_row = lax.dynamic_slice(
        pad_mask, (side, tensor_place // 2, 0), (1, 1, 2 * half_rows)
    ).reshape(2, half_rows)
    mask_row = jnp.where(side == 0, mask_row, mask_row[::-1]).reshape(2 * half_rows, 1)
    bias_col = jnp.where(mask_row > 0, 0.0, masked_score).astype(wide)

    unit_pad = ((0, slab_units - unit_cols), (0, 0))
    up_cols, down_cols = jnp.pad(w_up.T, unit_pad), jnp.pad(w_down, unit_pad)
    bulk_rows = bulk_units // dp_count
    hop_rows = hop_units // dp_count
    split = lambda values: (
        values[:bulk_units].reshape(dp_count, bulk_rows, values.shape[1]),
        values[bulk_units:].reshape(dp_count, hop_rows, values.shape[1]),
    )
    (up_bulk, up_hop), (down_bulk, down_hop) = split(up_cols), split(down_cols)
    mlp_owned = to_rows(
        jnp.concatenate([up_bulk, down_bulk, up_hop, down_hop], axis=1).reshape(
            2 * slab_units, -1
        ),
        dp_count,
    )
    if by_hops:
        kinds = place(kind, hops.gather_kinds(attn_block))
        up_rows = gather_rows(mlp_owned[:bulk_rows])
        down_rows = gather_rows(mlp_owned[bulk_rows : 2 * bulk_rows])
        hop_own, hop_sibling = hops.gather_units(mlp_owned[2 * bulk_rows :])
    else:
        attn_rows = gather_rows(attn_block)
        kinds = attn_rows.reshape(4, dp_count // 4, tensor_count, -1, width)
        kinds = kinds.transpose(0, 2, 1, 3, 4).reshape(4, -1, width)
        up_rows = gather_rows(mlp_owned[:bulk_rows])
        down_rows = gather_rows(mlp_owned[bulk_rows:])
    qkv_rows = kinds[:3].reshape(-1, width)
    out_rows = kinds[3]
    slab_bias = jnp.pad(
        b_up.reshape(tensor_count, unit_cols), ((0, 0), (0, slab_units - unit_cols))
    )

    unit_first, scale_first = norm_stats(x_slot)
    normed_first = (unit_first * attn_norm_gain + attn_norm_shift).astype(low)
    qkv_bias = jnp.concatenate([to_heads(b_query), jnp.zeros_like(b_query), to_heads(b_value)])
    projected = (product(qkv_rows, normed_first, 1, 1) + qkv_bias[:, None]).astype(low)
    attended, total = attend(projected, bias_col, heads, 4)
    middle = x_slot + (product(attended, out_rows, 0, 0) + b_out)
    unit_second, scale_second = norm_stats(middle)
    normed_second = (unit_second * mlp_norm_gain + mlp_norm_shift).astype(low)
    bulk_bias = in_slabs(slab_bias, 0, bulk_units).reshape(-1, 1)
    bulk_block = 512 if by_hops else bulk_units
    *sums, grad_up, grad_down, bulk_grad = mlp(
        normed_second, grad_out, up_rows, down_rows, bulk_bias, bulk_block
    )
    up_owned, down_owned = scatter_rows(grad_up), scatter_rows(grad_down)
    bulk_grad = bulk_grad[:, 0]
    if by_hops:
        hop_bias = in_slabs(slab_bias, bulk_units, slab_units).reshape(devices, hop_rows)
        hop_bias = hop_bias[hop_places].reshape(2, -1, 1)
        *sums, grad_sibling, sibling_bias = mlp(
            normed_second, grad_out, hop_sibling, None, hop_bias[1], 448, sums
        )
        *sums, grad_own, own_bias = mlp(
            normed_second, grad_out, hop_own, None, hop_bias[0], 448, sums
        )
        hop_owned = hops.reduce_units(grad_own, grad_sibling)
        hop_grad = jnp.concatenate([own_bias[:, 0], sibling_bias[:, 0]]).reshape(devices, -1)
        hop_grad = hop_grad[jnp.array(hop_find)][here ^ jnp.arange(devices)].reshape(-1)
        up_grad = jnp.concatenate([bulk_grad, hop_grad])
        mlp_grads = jnp.concatenate([up_owned, down_owned, hop_owned[0], hop_owned[1]], axis=0)
    else:
        up_grad = bulk_grad
        mlp_grads = jnp.concatenate([up_owned, down_owned], axis=0)
    down_out, grad_normed_second = sums
    layer_out = both_micros((middle + (down_out + b_down)).astype(low))

    grad_mid_norm, gain_second, shift_second = norm_backward(
        grad_normed_second, unit_second, scale_second, mlp_norm_gain
    )
    grad_wide = grad_out.astype(wide)
    grad_middle = grad_wide + grad_mid_norm
    grad_branch = grad_middle.astype(low)
    grad_attended = product(out_rows, grad_branch, 1, 1).astype(low)
    grad_projected = attend_back(
        projected, bias_col, attended, total, grad_attended, heads, 4
    )
    grad_flat = grad_projected.reshape(-1, 2 * half_rows)
    grad_normed_first = product(grad_flat, qkv_rows, 0, 0)
    if by_hops:
        grad_kinds = kinds_grad(
            kind, grad_projected, attended, normed_first, grad_branch, heads * HEAD_DIM // 4
        )
        attn_owned = hops.reduce_kinds(grad_kinds)
    else:
        grad_qkv_rows = product(grad_flat, normed_first, 1, 0).astype(low)
        grad_out_rows = product(attended, grad_branch, 1, 0).astype(low)
        grad_kinds = jnp.concatenate([grad_qkv_rows, grad_out_rows], axis=0)
        grad_kinds = grad_kinds.reshape(4, tensor_count, dp_count // 4, -1, width)
        attn_owned = scatter_rows(grad_kinds.transpose(0, 2, 1, 3, 4).reshape(-1, width))
    grad_in_norm, gain_first, shift_first = norm_backward(
        grad_normed_first, unit_first, scale_first, attn_norm_gain
    )
    input_grad = both_micros(grad_middle + grad_in_norm)

    mlp_cols = to_columns(mlp_grads, dp_count).reshape(dp_count, 2 * slab_units // dp_count, -1)
    cuts = (0, bulk_rows, 2 * bulk_rows, 2 * bulk_rows + hop_rows, 2 * bulk_rows + 2 * hop_rows)
    parts = [
        mlp_cols[:, cuts[i] : cuts[i + 1]].reshape(-1, mlp_cols.shape[2]) for i in range(4)
    ]
    grad_w_up = jnp.concatenate([parts[0], parts[2]], axis=0)[:unit_cols].T
    grad_w_down = jnp.concatenate([parts[1], parts[3]], axis=0)[:unit_cols]
    attn_cols = to_columns(attn_owned, dp_count).reshape(4, head_cols, -1)

    early = [
        jnp.sum(grad_branch, axis=0, dtype=wide),
        gain_second,
        shift_second,
        jnp.sum(grad_wide, axis=0),
        up_grad,
    ]
    late = [
        gain_first,
        shift_first,
        from_heads(jnp.sum(grad_projected[0], axis=1, dtype=wide)),
        from_heads(jnp.sum(grad_projected[2], axis=1, dtype=wide)),
    ]
    if by_hops:
        early = hops.sum_all(jnp.concatenate(early).reshape(-1, 128)).reshape(-1)
        late = hops.sum_all(jnp.concatenate(late).reshape(-1, 128)).reshape(-1)
    else:
        early = lax.psum(jnp.concatenate(early), everyone)
        late = lax.psum(jnp.concatenate(late), everyone)
    early_part = lambda place: early[place * width : (place + 1) * width]
    late_part = lambda place: late[place * width : (place + 1) * width]
    up_all = early[4 * width :]
    bulk_count = tensor_count * bulk_units
    up_all = jnp.concatenate(
        [from_slabs(up_all[:bulk_count])]
        + ([from_slabs(up_all[bulk_count:])] if by_hops else []),
        axis=1,
    )
    return (
        layer_out,
        input_grad,
        late_part(0),
        late_part(1),
        attn_cols[0].T,
        lax.dynamic_slice_in_dim(late_part(2), col_start, head_cols),
        attn_cols[1].T,
        attn_cols[2].T,
        lax.dynamic_slice_in_dim(late_part(3), col_start, head_cols),
        attn_cols[3],
        early_part(0),
        early_part(1),
        early_part(2),
        grad_w_up,
        up_all[:, :unit_cols].reshape(-1),
        grad_w_down,
        early_part(3),
    )


def solution(mesh):
    tokens = P(None, ("dp", "tensor"), None)
    columns = P("dp", "tensor")
    rows = P("tensor", "dp")
    return jax.shard_map(
        partial(shards, mesh.shape["dp"], mesh.shape["tensor"]),
        mesh=mesh,
        in_specs=(
            tokens,
            P(None, "dp", None),
            tokens,
            P(),
            P(),
            columns,
            P(),
            columns,
            columns,
            P(),
            rows,
            P(),
            P(),
            P(),
            columns,
            P(),
            rows,
            P(),
        ),
        out_specs=(
            tokens,
            tokens,
            P(),
            P(),
            columns,
            P("tensor"),
            columns,
            columns,
            P("tensor"),
            rows,
            P(),
            P(),
            P(),
            columns,
            P(),
            rows,
            P(),
        ),
        check_vma=False,
    )
```

```python
from functools import partial

import jax
import jax.numpy as jnp
from jax import lax
from jax.experimental import pallas as pl
from jax.experimental.pallas import tpu as pltpu
from jax.sharding import PartitionSpec as P

HEAD_DIM = 72
norm_eps = 1e-06
masked_score = -1000000000.0
low = jnp.bfloat16
wide = jnp.float32
score_scale = HEAD_DIM**-0.5
log2_e = 1.4426950408889634
gelu_scale = 0.7978845608028654
gelu_cube = 0.044715
everyone = ("dp", "tensor")


def product(left, right, left_dim, right_dim):
    return lax.dot_general(
        left, right, (((left_dim,), (right_dim,)), ((), ())), preferred_element_type=wide
    )


def attend_kernel(heads, query_ref, key_ref, value_ref, bias_ref, out_ref, total_ref):
    for head in range(heads):
        rows = slice(head * HEAD_DIM, (head + 1) * HEAD_DIM)
        scores = product(key_ref[rows, :], query_ref[rows, :], 0, 0) * (score_scale * log2_e)
        scores = scores + bias_ref[...]
        top = jnp.max(scores, axis=0, keepdims=True)
        weights = jnp.exp2(scores - top)
        total = jnp.sum(weights, axis=0, keepdims=True)
        mixed = product(value_ref[rows, :], weights.astype(low), 1, 0)
        out_ref[rows, :] = (mixed * (1.0 / total)).astype(low)
        total_ref[head] = top + jnp.log2(total)


def attend_back_kernel(
    heads,
    query_ref,
    key_ref,
    value_ref,
    bias_ref,
    out_ref,
    total_ref,
    grad_ref,
    grads_ref,
):
    for head in range(heads):
        rows = slice(head * HEAD_DIM, (head + 1) * HEAD_DIM)
        query, key, value, grad = (
            query_ref[rows, :],
            key_ref[rows, :],
            value_ref[rows, :],
            grad_ref[rows, :],
        )
        scores = product(key, query, 0, 0) * (score_scale * log2_e) + bias_ref[...]
        probs = jnp.exp2(scores - total_ref[head])
        grad_probs = product(value, grad, 0, 0)
        along = jnp.sum(
            grad.astype(wide) * out_ref[rows, :].astype(wide), axis=0, keepdims=True
        )
        grad_raw = (probs * (grad_probs - along)).astype(low)
        grads_ref[2, rows, :] = product(grad, probs.astype(low), 1, 1).astype(low)
        grads_ref[0, rows, :] = (product(key, grad_raw, 1, 0) * score_scale).astype(low)
        grads_ref[1, rows, :] = (product(query, grad_raw, 1, 1) * score_scale).astype(low)


def attend(projected, bias, heads, step_heads):
    tokens = projected.shape[1]
    steps = heads // step_heads
    part = lambda place: pl.BlockSpec(
        (HEAD_DIM * step_heads, tokens), lambda i, place=place: (place * steps + i, 0)
    )
    return pl.pallas_call(
        partial(attend_kernel, step_heads),
        grid=(steps,),
        in_specs=[part(0), part(1), part(2), pl.BlockSpec((tokens, 1), lambda i: (0, 0))],
        out_specs=[part(0), pl.BlockSpec((step_heads, 1, tokens), lambda i: (i, 0, 0))],
        out_shape=[
            jax.ShapeDtypeStruct((heads * HEAD_DIM, tokens), low),
            jax.ShapeDtypeStruct((heads, 1, tokens), wide),
        ],
        compiler_params=pltpu.CompilerParams(vmem_limit_bytes=48 * 2**20),
        cost_estimate=pl.CostEstimate(
            flops=heads * tokens * tokens * 1024, bytes_accessed=16 * 2**20, transcendentals=0
        ),
        name="attend",
    )(projected, projected, projected, bias)


def attend_back(projected, bias, attended, total, grad, heads, step_heads):
    tokens = projected.shape[1]
    steps = heads // step_heads
    part = lambda place: pl.BlockSpec(
        (HEAD_DIM * step_heads, tokens), lambda i, place=place: (place * steps + i, 0)
    )
    return pl.pallas_call(
        partial(attend_back_kernel, step_heads),
        grid=(steps,),
        in_specs=[
            part(0),
            part(1),
            part(2),
            pl.BlockSpec((tokens, 1), lambda i: (0, 0)),
            part(0),
            pl.BlockSpec((step_heads, 1, tokens), lambda i: (i, 0, 0)),
            part(0),
        ],
        out_specs=pl.BlockSpec((3, HEAD_DIM * step_heads, tokens), lambda i: (0, i, 0)),
        out_shape=jax.ShapeDtypeStruct((3, heads * HEAD_DIM, tokens), low),
        compiler_params=pltpu.CompilerParams(vmem_limit_bytes=48 * 2**20),
        cost_estimate=pl.CostEstimate(
            flops=heads * tokens * tokens * 2048, bytes_accessed=16 * 2**20, transcendentals=0
        ),
        name="attend_back",
    )(projected, projected, projected, bias, attended, total, grad)


def kinds_kernel(kind_ref, grads_ref, attended_ref, normed_ref, branch_ref, out_ref):
    kind = pl.program_id(0)

    @pl.when(kind < 3)
    def projections():
        out_ref[0] = product(grads_ref[0], normed_ref[...], 1, 0).astype(low)

    @pl.when(kind == 3)
    def output():
        out_ref[0] = product(attended_ref[...], branch_ref[...], 1, 0).astype(low)


def kinds_grad(kind, grads, attended, normed, branch, block):
    _, rows, tokens = grads.shape
    width = normed.shape[1]
    whole = pl.BlockSpec((tokens, width), lambda k, i, ref: (0, 0))

    def spot(k, i, ref):
        other = k ^ ref[0]
        return ((other & 1) * 2 + (other >> 1), i, 0)

    return pl.pallas_call(
        kinds_kernel,
        grid_spec=pltpu.PrefetchScalarGridSpec(
            num_scalar_prefetch=1,
            grid=(4, rows // block),
            in_specs=[
                pl.BlockSpec((1, block, tokens), lambda k, i, ref: (jnp.minimum(k, 2), i, 0)),
                pl.BlockSpec((block, tokens), lambda k, i, ref: (i, 0)),
                whole,
                whole,
            ],
            out_specs=pl.BlockSpec((1, block, width), spot),
        ),
        out_shape=jax.ShapeDtypeStruct((4, rows, width), low),
        compiler_params=pltpu.CompilerParams(vmem_limit_bytes=40 * 2**20),
        cost_estimate=pl.CostEstimate(
            flops=12 * rows * width * tokens, bytes_accessed=24 * 2**20, transcendentals=0
        ),
        name="kinds_grad",
    )(kind, grads, attended, normed, branch)


def norm_forward(values, gain, shift):
    row_mean = jnp.mean(values, axis=-1, keepdims=True)
    centred = values - row_mean
    inv_scale = lax.rsqrt(jnp.mean(centred * centred, axis=-1, keepdims=True) + norm_eps)
    return (centred * inv_scale * gain + shift).astype(low)


def norm_back_kernel(values_ref, grad_ref, gain_ref, base_ref, full_ref, low_ref, sums_ref):
    values = values_ref[...].astype(wide)
    centred = values - jnp.mean(values, axis=-1, keepdims=True)
    inv_scale = lax.rsqrt(jnp.mean(centred * centred, axis=-1, keepdims=True) + norm_eps)
    unit = centred * inv_scale
    grad = grad_ref[...]
    scaled = grad * gain_ref[...]
    mean_grad = jnp.mean(scaled, axis=-1, keepdims=True)
    mean_along = jnp.mean(scaled * unit, axis=-1, keepdims=True)
    base = base_ref[...].astype(wide)
    full = base + inv_scale * (scaled - mean_grad - unit * mean_along)
    rounded = full.astype(low)
    full_ref[...] = full
    low_ref[...] = rounded
    total = lambda rows: jnp.sum(rows, axis=0, keepdims=True)
    sums = jnp.concatenate(
        [total(grad * unit), total(grad), total(rounded.astype(wide)), total(base)], axis=0
    )

    @pl.when(pl.program_id(0) == 0)
    def first():
        sums_ref[...] = sums

    @pl.when(pl.program_id(0) > 0)
    def later():
        sums_ref[...] += sums


def norm_back(values, grad, gain, base):
    tokens, width = values.shape
    block = tokens // 4
    rows = pl.BlockSpec((block, width), lambda i: (i, 0))
    return pl.pallas_call(
        norm_back_kernel,
        grid=(4,),
        in_specs=[rows, rows, pl.BlockSpec((1, width), lambda i: (0, 0)), rows],
        out_specs=[rows, rows, pl.BlockSpec((4, width), lambda i: (0, 0))],
        out_shape=[
            jax.ShapeDtypeStruct((tokens, width), wide),
            jax.ShapeDtypeStruct((tokens, width), low),
            jax.ShapeDtypeStruct((4, width), wide),
        ],
        compiler_params=pltpu.CompilerParams(vmem_limit_bytes=40 * 2**20),
        cost_estimate=pl.CostEstimate(
            flops=32 * tokens * width, bytes_accessed=16 * tokens * width, transcendentals=0
        ),
        name="norm_back",
    )(values, grad, gain.reshape(1, width), base)


def mlp_kernel(carried, normed_ref, grad_ref, bias_ref, *refs):
    pieces, refs = refs[:8], refs[8:]
    if carried:
        out_before, normed_before = refs[:2]
        refs = refs[2:]
    out_ref, grad_normed_ref, first_ref, last_ref, grad_bias_ref, ups, downs, sems = refs
    step = pl.program_id(0)
    slot = step % 2
    rows = ups.shape[1] // 2

    def copies(at):
        moves = []
        for half in range(2):
            piece = pieces[2 * at + half]
            for kind, target in enumerate((ups, downs)):
                moves.append(
                    pltpu.make_async_copy(
                        piece.at[pl.ds(kind * rows, rows)],
                        target.at[at % 2, pl.ds(half * rows, rows)],
                        sems.at[at % 2, 2 * half + kind],
                    )
                )
        return moves

    for at in range(4):

        @pl.when(step + 1 == at if at else step == 0)
        def fetch():
            for move in copies(at):
                move.start()

    for at in range(4):

        @pl.when(step == at)
        def arrive():
            for move in copies(at):
                move.wait()

    normed, grad = normed_ref[...], grad_ref[...]
    up, down = ups[slot], downs[slot]
    pre_act = product(up, normed, 1, 1) + bias_ref[...]
    square = pre_act * pre_act
    bent = jnp.tanh(gelu_scale * (pre_act + gelu_cube * square * pre_act))
    half = 0.5 * (1.0 + bent)
    active = (pre_act * half).astype(low)
    slope = half + 0.5 * pre_act * (1.0 - bent * bent) * (
        gelu_scale * (1.0 + 3.0 * gelu_cube * square)
    )
    grad_wide = product(down, grad, 1, 1) * slope
    grad_pre = grad_wide.astype(low)
    grad_bias_ref[...] = jnp.sum(grad_wide, axis=1, keepdims=True)
    grad_down = product(active, grad, 1, 0).astype(low)
    grad_up = product(grad_pre, normed, 1, 0).astype(low)

    def keep(ref):
        for place in range(2):
            ref[place, 0] = grad_up[place * rows : (place + 1) * rows]
            ref[place, 1] = grad_down[place * rows : (place + 1) * rows]

    pl.when(step < 2)(lambda: keep(first_ref))
    pl.when(step >= 2)(lambda: keep(last_ref))
    out_term = product(active, down, 0, 0)
    normed_term = product(grad_pre, up, 0, 0)

    @pl.when(step == 0)
    def first():
        if carried:
            out_ref[...] = out_before[...] + out_term
            grad_normed_ref[...] = normed_before[...] + normed_term
        else:
            out_ref[...] = out_term
            grad_normed_ref[...] = normed_term

    @pl.when(step > 0)
    def later():
        out_ref[...] += out_term
        grad_normed_ref[...] += normed_term


def mlp(normed, grad, bias, pieces, before=None):
    tokens, width = normed.shape
    rows = pieces[0].shape[0] // 2
    whole = pl.BlockSpec((tokens, width), lambda i: (0, 0))
    column = pl.BlockSpec((2 * rows, 1), lambda i: (i, 0))
    grads = jax.ShapeDtypeStruct((4, 2, rows, width), low)
    earlier = [] if before is None else list(before)
    return pl.pallas_call(
        partial(mlp_kernel, before is not None),
        grid=(4,),
        in_specs=[whole, whole, column]
        + [pl.BlockSpec(memory_space=pl.ANY)] * 8
        + [whole] * len(earlier),
        out_specs=[
            whole,
            whole,
            pl.BlockSpec((2, 2, rows, width), lambda i: (jnp.minimum(i, 1), 0, 0, 0)),
            pl.BlockSpec((2, 2, rows, width), lambda i: (jnp.maximum(i - 2, 0), 0, 0, 0)),
            column,
        ],
        out_shape=[jax.ShapeDtypeStruct((tokens, width), wide)] * 2
        + [grads, grads, jax.ShapeDtypeStruct((8 * rows, 1), wide)],
        scratch_shapes=[
            pltpu.VMEM((2, 2 * rows, width), low),
            pltpu.VMEM((2, 2 * rows, width), low),
            pltpu.SemaphoreType.DMA((2, 4)),
        ],
        input_output_aliases={11: 0, 12: 1} if earlier else {},
        compiler_params=pltpu.CompilerParams(vmem_limit_bytes=60 * 2**20),
        cost_estimate=pl.CostEstimate(
            flops=16 * tokens * width * 8 * rows, bytes_accessed=40 * 2**20, transcendentals=0
        ),
        name="mlp",
    )(normed, grad, bias, *pieces, *earlier)


def place_kernel(kind_ref, *refs):
    pieces, out_ref = refs[:8], refs[8]
    kind = kind_ref[0]
    quarter = out_ref.shape[1] // 4
    for core in range(2):
        near, near_y, far, far_x = pieces[4 * core : 4 * core + 4]
        same, across = kind ^ core, kind ^ (core + 2)
        out_ref[same, :quarter] = near[:quarter]
        out_ref[across, :quarter] = near[quarter:]
        out_ref[same, quarter : 2 * quarter] = near_y[:quarter]
        out_ref[across, quarter : 2 * quarter] = near_y[quarter:]
        out_ref[same, 2 * quarter :] = far[...]
        out_ref[across, 2 * quarter :] = far_x[...]


def place(kind, pieces):
    rows, width = pieces[0].shape
    local = pl.BlockSpec(memory_space=pltpu.VMEM)
    return pl.pallas_call(
        place_kernel,
        in_specs=[pl.BlockSpec(memory_space=pltpu.SMEM)] + [local] * 8,
        out_specs=local,
        out_shape=jax.ShapeDtypeStruct((4, 2 * rows, width), low),
        compiler_params=pltpu.CompilerParams(vmem_limit_bytes=40 * 2**20),
        cost_estimate=pl.CostEstimate(
            flops=0, bytes_accessed=32 * rows * width, transcendentals=0
        ),
        name="place",
    )(kind, *pieces)


def unite_kernel(kind_ref, *refs):
    outs = refs[4:]
    part = refs[0].shape[1]
    for distance in range(4):
        source = kind_ref[0] ^ distance
        for column in range(4):

            @pl.when(source == column)
            def put():
                start = 0
                for out in outs:
                    rows = out.shape[0]
                    out[:, column * part : (column + 1) * part] = refs[distance][
                        start : start + rows, :
                    ]
                    start += rows


def unite(kind, blocks, cuts):
    part = blocks[0].shape[1]
    local = pl.BlockSpec(memory_space=pltpu.VMEM)
    return pl.pallas_call(
        unite_kernel,
        in_specs=[pl.BlockSpec(memory_space=pltpu.SMEM)] + [local] * 4,
        out_specs=[local] * len(cuts),
        out_shape=[jax.ShapeDtypeStruct((rows, 4 * part), low) for rows in cuts],
        name="unite",
    )(kind, *blocks)


def divide_kernel(kind_ref, *refs):
    ins, outs = refs[:-4], refs[-4:]
    part = outs[0].shape[1]
    for distance in range(4):
        target = kind_ref[0] ^ distance
        for column in range(4):

            @pl.when(target == column)
            def put():
                start = 0
                for ref in ins:
                    rows = ref.shape[0]
                    outs[distance][start : start + rows, :] = ref[
                        :, column * part : (column + 1) * part
                    ]
                    start += rows


def divide(kind, owned):
    rows = sum(values.shape[0] for values in owned)
    part = owned[0].shape[1] // 4
    local = pl.BlockSpec(memory_space=pltpu.VMEM)
    return pl.pallas_call(
        divide_kernel,
        in_specs=[pl.BlockSpec(memory_space=pltpu.SMEM)] + [local] * len(owned),
        out_specs=[local] * 4,
        out_shape=[jax.ShapeDtypeStruct((rows, part), low)] * 4,
        name="divide",
    )(kind, *owned)


def settle_kernel(kind_ref, *refs):
    for distance in range(4):
        refs[4][kind_ref[0] ^ distance] = refs[distance][...].astype(wide)


def settle(kind, blocks):
    rows, part = blocks[0].shape
    local = pl.BlockSpec(memory_space=pltpu.VMEM)
    return pl.pallas_call(
        settle_kernel,
        in_specs=[pl.BlockSpec(memory_space=pltpu.SMEM)] + [local] * 4,
        out_specs=local,
        out_shape=jax.ShapeDtypeStruct((4, rows, part), wide),
        name="settle",
    )(kind, *blocks)


def after(values, *earlier):
    return lax.optimization_barrier((values, earlier))[0]


def add_low(*terms):
    total = terms[0].astype(wide)
    for term in terms[1:]:
        total = total + term.astype(wide)
    return total.astype(low)


def join(kinds, *blocks):
    width = blocks[0].shape[-1]
    parts = [block.reshape(kinds, -1, width) for block in blocks]
    return jnp.concatenate(parts, axis=1).reshape(-1, width)


class Hops:
    def __init__(self, dp_count, tensor_count):
        self.count = dp_count * tensor_count
        self.y, self.z = 1, (2, 4, 6)
        self.core, self.x = tensor_count, 2 * tensor_count
        self.near, self.far = (0, 2), (4, 6)

    def send(self, values, distance):
        pairs = [(place, place ^ distance) for place in range(self.count)]
        return lax.ppermute(values, everyone, pairs)

    def order(self):
        x, y = self.x, self.y
        near = [n ^ p ^ q for q in (0, y) for p in (0, x) for n in self.near]
        far = [n ^ p ^ q for q in (0, x) for p in (0, y) for n in self.far]
        return near + far

    def along_z(self, block):
        return [self.send(block, z) for z in self.z]

    def second(self, kinds, block, arrived):
        z1, z2, z3 = arrived
        near, far = join(kinds, block, z1), join(kinds, z2, z3)
        return near, far, self.send(near, self.x), self.send(far, self.y)

    def third(self, kinds, near, far, near_x, far_y):
        near, far = join(kinds, near, near_x), join(kinds, far, far_y)
        return near, self.send(near, self.y), far, self.send(far, self.x)

    def sibling(self, *pieces):
        return [self.send(piece, self.core) for piece in pieces]

    def sum_all(self, values):
        for distance in (self.core, self.x, self.y, self.z[0], self.z[1]):
            values = values + self.send(values, distance)
        return values

    def across_dp(self, blocks):
        return [blocks[0]] + [self.send(blocks[j], j * self.core) for j in (1, 2, 3)]


class Reduction:
    def __init__(self, hops, own, sibling, joined):
        self.hops, self.own, self.joined = hops, own, joined
        self.arrived = hops.send(sibling, hops.core)
        self.width = own.shape[-1]

    def part(self, place):
        terms = (self.own, self.arrived)
        if self.joined:
            return tuple(term[place] for term in terms)
        cuts = (
            lambda term: term[:, 0:2],
            lambda term: term[:, 2:4],
            lambda term: term[0, 4:8],
            lambda term: term[1, 4:8],
        )
        return tuple(cuts[place](term) for term in terms)

    def halves(self, values):
        axis = 1 if self.joined else 0
        shape = (2, 2, 2, -1, self.width) if self.joined else (2, 2, -1, self.width)
        values = values.reshape(shape)
        return [lax.index_in_dim(values, place, axis, keepdims=False) for place in (0, 1)]

    def blocks(self, values):
        axis = 1 if self.joined else 0
        return [lax.index_in_dim(values, place, axis, keepdims=False) for place in (0, 1)]

    def ready_third(self):
        self.operands = add_low(*self.part(1)), add_low(*self.part(3))
        return self.operands

    def third(self, *earlier):
        near, far = after(self.operands, *earlier)
        near, far = self.hops.send(near, self.hops.y), self.hops.send(far, self.hops.x)
        near, far = add_low(*self.part(0), near), add_low(*self.part(2), far)
        self.near, self.far = self.halves(near), self.halves(far)
        self.operands = self.near[1], self.far[1]
        return self.operands

    def second(self, *earlier):
        near, far = after(self.operands, *earlier)
        near, far = self.hops.send(near, self.hops.x), self.hops.send(far, self.hops.y)
        near, far = add_low(self.near[0], near), add_low(self.far[0], far)
        self.near, self.far = self.blocks(near), self.blocks(far)
        self.operands = self.near[1], self.far[0], self.far[1]
        return self.operands

    def along_z(self, *earlier):
        operands = after(self.operands, *earlier)
        arrived = [self.hops.send(v, z) for v, z in zip(operands, self.hops.z, strict=True)]
        return add_low(self.near[0], *arrived)


def shards(
    dp_count,
    tensor_count,
    inputs,
    pad_mask,
    cotangent,
    attn_norm_gain,
    attn_norm_shift,
    w_query,
    b_query,
    w_key,
    w_value,
    b_value,
    w_out,
    b_out,
    mlp_norm_gain,
    mlp_norm_shift,
    w_up,
    b_up,
    w_down,
    b_down,
):
    half_rows, width = inputs.shape[1:]
    tokens = 2 * half_rows
    head_cols = w_query.shape[1]
    unit_cols = w_up.shape[1]
    quantum = 8 * dp_count
    slab_units = -(-unit_cols // quantum) * quantum
    by_hops = (dp_count, tensor_count) == (4, 8)
    dp_place, tensor_place = lax.axis_index("dp"), lax.axis_index("tensor")
    devices = dp_count * tensor_count
    here = dp_place * tensor_count + tensor_place
    col_start = tensor_place * head_cols
    side = tensor_place % 2
    pairs = [(place, place ^ 1) for place in range(tensor_count)]
    hops = Hops(dp_count, tensor_count)
    kind = dp_place.reshape(1).astype(jnp.int32)
    heads = head_cols * tensor_count // HEAD_DIM // 2
    piece_rows = heads * HEAD_DIM

    def swap(values):
        return lax.ppermute(values, "tensor", pairs)

    def one_slot(values, *earlier):
        kept = lax.dynamic_index_in_dim(values, side, 0, keepdims=False)
        sent = lax.dynamic_index_in_dim(values, 1 - side, 0, keepdims=False)
        if earlier:
            sent = after(sent, *earlier)
        return jnp.concatenate([kept, swap(sent)], axis=0)

    def both_micros(kept, other):
        return jnp.where(side == 0, jnp.stack([kept, other]), jnp.stack([other, kept]))

    unit_pad = ((0, slab_units - unit_cols), (0, 0))
    up_cols, down_cols = jnp.pad(w_up.T, unit_pad), jnp.pad(w_down, unit_pad)
    attn_cols = jnp.concatenate([w_query.T, w_key.T, w_value.T, w_out], axis=0)
    if by_hops:
        unit_cuts = (72, slab_units // 4 - 72)
        first_units = 4 * unit_cuts[0]
        share = lambda values, low_end, high_end: values[low_end:high_end].reshape(
            4, -1, values.shape[1]
        )
        mlp_cols = jnp.concatenate(
            [
                share(up_cols, 0, first_units),
                share(down_cols, 0, first_units),
                share(up_cols, first_units, slab_units),
                share(down_cols, first_units, slab_units),
            ],
            axis=1,
        )
        attn_cols = attn_cols.reshape(4, head_cols, -1)
        pick = lambda values, j: lax.dynamic_index_in_dim(
            values, dp_place ^ j, 0, keepdims=False
        )
        attn_blocks = hops.across_dp([pick(attn_cols, j) for j in range(4)])
        a_one, a_two = unite(kind, attn_blocks, (HEAD_DIM, HEAD_DIM))
        x_slot = one_slot(inputs)
        mlp_cols = after(mlp_cols, *attn_blocks[1:])
        mlp_blocks = hops.across_dp([pick(mlp_cols, j) for j in range(4)])
        m_one, m_two = unite(kind, mlp_blocks, [2 * rows for rows in unit_cuts])

        a_one_z = hops.along_z(a_one)
        a_one_two = hops.second(1, a_one, a_one_z)
        a_two_z = hops.along_z(after(a_two, *a_one_z))
        a_one_three = hops.third(1, *a_one_two)
        m_one_z = hops.along_z(after(m_one, *a_two_z))
        a_two, a_two_z = after((a_two, a_two_z), *a_one_three)
        kinds_one = place(kind, list(a_one_three) + hops.sibling(*a_one_three))
        a_two_two = hops.second(1, a_two, a_two_z)
        a_two_three = hops.third(1, *a_two_two)
        grad_out = one_slot(cotangent, *a_two_two[2:])
        m_two_z = hops.along_z(after(m_two, *m_one_z))
        m_one, m_one_z = after((m_one, m_one_z), *a_two_three)
        kinds_two = place(kind, list(a_two_three) + hops.sibling(*a_two_three))
        m_one_two = hops.second(2, m_one, m_one_z)
        m_one_three = hops.third(2, *m_one_two)
        m_one_sibling = hops.sibling(*m_one_three)
        m_two, m_two_z = after((m_two, m_two_z), *m_one_three)
        m_two_two = hops.second(2, m_two, m_two_z)
        m_two_three = hops.third(2, *m_two_two)
        m_two_sibling = hops.sibling(*m_two_three)
        kinds = [kinds_one, kinds_two]
        unit_pieces = [
            m_one_sibling + list(m_one_three),
            m_two_sibling + list(m_two_three),
        ]
        order = hops.order()
        order = [place ^ hops.core for place in order] + order
        unit_places = here ^ jnp.array(order)
        unit_find = jnp.array([order.index(place) for place in range(devices)])
        head_places = tensor_place ^ jnp.array(
            [n ^ q for group in (hops.near, hops.far) for q in (0, hops.y) for n in group]
        )
    else:
        x_slot, grad_out = one_slot(inputs), one_slot(cotangent)
        unit_cuts = (slab_units // dp_count,)

        def gathered(values):
            owned = lax.all_to_all(
                values.reshape(dp_count, -1, values.shape[1]), "dp", 0, 2, tiled=True
            )
            return lax.all_gather(owned[0], everyone, axis=0, tiled=True)

        attn_rows = gathered(attn_cols)
        attn_rows = attn_rows.reshape(4, dp_count // 4, tensor_count, -1, width)
        attn_rows = attn_rows.transpose(0, 2, 1, 3, 4).reshape(4, -1, width)
        kinds = [attn_rows[:, :piece_rows], attn_rows[:, piece_rows:]]
        up_rows = gathered(up_cols).reshape(4, 8, -1, width)
        down_rows = gathered(down_cols).reshape(4, 8, -1, width)
        unit_pieces = [
            [jnp.concatenate([up_rows[part, i], down_rows[part, i]]) for i in range(8)]
            for part in range(4)
        ]

    def head_bias(values, part):
        if by_hops:
            blocks = values.reshape(tensor_count, 2, HEAD_DIM)[:, part]
            return blocks[head_places].reshape(-1)
        return values[part * piece_rows : (part + 1) * piece_rows]

    def head_grads(one, two):
        if by_hops:
            blocks = jnp.stack([one.reshape(-1, HEAD_DIM), two.reshape(-1, HEAD_DIM)], axis=1)
            return jnp.zeros_like(blocks).at[head_places].set(blocks).reshape(-1)
        return jnp.concatenate([one, two])

    slab_bias = jnp.pad(
        b_up.reshape(tensor_count, unit_cols), ((0, 0), (0, slab_units - unit_cols))
    )
    unit_starts = [dp_count * sum(unit_cuts[:i]) for i in range(len(unit_cuts) + 1)]

    def unit_bias(part):
        if not by_hops:
            values = slab_bias.reshape(tensor_count, dp_count, -1).transpose(1, 0, 2)
            return values.reshape(4, -1, 1)[part]
        values = slab_bias[:, unit_starts[part] : unit_starts[part + 1]]
        values = values.reshape(tensor_count, dp_count, -1).transpose(1, 0, 2)
        return values.reshape(devices, -1)[unit_places].reshape(-1, 1)

    def unit_grads(values):
        slabs = []
        for part in values if by_hops else [jnp.concatenate(values)]:
            part = part.reshape(devices, -1)
            if by_hops:
                part = part[unit_find][here ^ jnp.arange(devices)]
            part = part.reshape(dp_count, tensor_count, -1).transpose(1, 0, 2)
            slabs.append(part.reshape(tensor_count, -1))
        return jnp.concatenate(slabs, axis=1)

    mask_row = lax.dynamic_slice(pad_mask, (side, tensor_place // 2, 0), (1, 1, tokens))
    mask_row = mask_row.reshape(2, half_rows)
    mask_row = jnp.where(side == 0, mask_row, mask_row[::-1]).reshape(tokens, 1)
    bias_col = jnp.where(mask_row > 0, 0.0, masked_score).astype(wide)

    normed_first = norm_forward(x_slot.astype(wide), attn_norm_gain, attn_norm_shift)
    projected, attended, totals = [], [], []
    branch = b_out
    for part in range(2):
        zeros = jnp.zeros((piece_rows,), wide)
        bias = jnp.concatenate([head_bias(b_query, part), zeros, head_bias(b_value, part)])
        rows = kinds[part][:3].reshape(-1, width)
        projected.append((product(rows, normed_first, 1, 1) + bias[:, None]).astype(low))
        mixed, total = attend(projected[part], bias_col, heads, 4)
        attended.append(mixed)
        totals.append(total)
        branch = product(mixed, kinds[part][3], 0, 0) + branch
    middle = x_slot.astype(wide) + branch
    normed_second = norm_forward(middle, mlp_norm_gain, mlp_norm_shift)
    sums, grad_siblings, grad_owns, up_sums = None, [], [], []
    for part, pieces in enumerate(unit_pieces):
        *sums, grad_sibling, grad_own, up_sum = mlp(
            normed_second, grad_out, unit_bias(part), pieces, sums
        )
        grad_siblings.append(grad_sibling)
        grad_owns.append(grad_own)
        up_sums.append(up_sum[:, 0])
    down_out, grad_normed_second = sums
    out_low = (middle + (down_out + b_down)).astype(low)

    if by_hops:
        m_one, m_two = [
            Reduction(hops, own, sibling, True)
            for own, sibling in zip(grad_owns, grad_siblings, strict=True)
        ]
        grad_normed_second = after(grad_normed_second, *m_one.ready_third())
    grad_middle, grad_branch, second_sums = norm_back(
        middle, grad_normed_second, mlp_norm_gain, grad_out
    )
    grad_attended = [product(kinds[part][3], grad_branch, 1, 1).astype(low) for part in range(2)]
    first_terms, projection_grads, kind_grads = 0.0, [], []
    for part in range(2):
        grads = attend_back(
            projected[part],
            bias_col,
            attended[part],
            totals[part],
            grad_attended[part],
            heads,
            4,
        )
        if by_hops:
            if part == 0:
                grads = after(grads, *m_one.third(), *m_two.ready_third())
            else:
                m_one_second = m_one.second()
                grads = after(grads, *m_one_second)
        projection_grads.append(grads)
        kind_grads.append(
            kinds_grad(kind, grads, attended[part], normed_first, grad_branch, piece_rows // 2)
        )
        if by_hops and part == 0:
            terms = kind_grads[0].reshape(2, 2, 8, HEAD_DIM, width)
            a_one = Reduction(hops, terms[0], terms[1], False)
    if by_hops:
        m_two_third = m_two.third(*m_one_second)
        terms = kind_grads[1].reshape(2, 2, 8, HEAD_DIM, width)
        a_two = Reduction(hops, terms[0], terms[1], False)
    for part in range(2):
        rows = kinds[part][:3].reshape(-1, width)
        terms = projection_grads[part].reshape(-1, tokens)
        if by_hops and part == 1:
            terms = after(terms, *a_one.ready_third())
        first_terms = product(terms, rows, 0, 0) + first_terms
    input_full, input_low, first_sums = norm_back(
        x_slot, first_terms, attn_norm_gain, grad_middle
    )
    layer_out = both_micros(out_low[:half_rows], swap(out_low[half_rows:]))
    input_grad = both_micros(
        input_full[:half_rows], swap(input_low[half_rows:]).astype(wide)
    )

    if by_hops:
        m_one_owned = m_one.along_z()
        m_two_second = m_two.second(m_two_third, input_low)
        a_two.ready_third()
        a_one_third = a_one.third(*m_two_third)
        m_two_owned = m_two.along_z(m_one_owned)
        a_one_second = a_one.second(*a_one_third)
        a_two_third = a_two.third(*a_one_third)
        a_one_owned = a_one.along_z(m_two_owned)
        a_two.second(*a_two_third)
        a_two_owned = a_two.along_z()
        mlp_owned = [m_one_owned[0], m_one_owned[1], m_two_owned[0], m_two_owned[1]]
        attn_owned = [a_one_owned, a_two_owned]
        mlp_back = settle(kind, hops.across_dp(divide(kind, mlp_owned)))
        attn_back = settle(kind, hops.across_dp(divide(kind, attn_owned)))
        bounds = [0]
        for rows in (unit_cuts[0], unit_cuts[0], unit_cuts[1], unit_cuts[1]):
            bounds.append(bounds[-1] + rows)
        parts = [
            mlp_back[:, bounds[i] : bounds[i + 1]].reshape(-1, mlp_back.shape[2])
            for i in range(4)
        ]
        grad_w_up = jnp.concatenate([parts[0], parts[2]], axis=0)
        grad_w_down = jnp.concatenate([parts[1], parts[3]], axis=0)
    else:

        def scattered(values):
            owned = lax.psum_scatter(values, everyone, scatter_dimension=0, tiled=True)
            back = lax.all_to_all(owned[None], "dp", 2, 0, tiled=True)
            return back.reshape(-1, width // dp_count).astype(wide)

        both = jnp.concatenate(
            [half for pair in zip(grad_siblings, grad_owns, strict=True) for half in pair], axis=0
        )
        grad_w_up = scattered(both[:, 0].reshape(-1, width))
        grad_w_down = scattered(both[:, 1].reshape(-1, width))
        terms = jnp.concatenate(kind_grads, axis=1)
        terms = terms.reshape(4, tensor_count, dp_count // 4, -1, width)
        terms = terms.transpose(0, 2, 1, 3, 4).reshape(-1, width)
        attn_back = scattered(terms).reshape(4, head_cols, -1)

    total_over = lambda i: jnp.concatenate(
        [jnp.sum(grads[i], axis=1, dtype=wide) for grads in projection_grads]
    )
    split_heads = lambda values: head_grads(values[:piece_rows], values[piece_rows:])
    early = jnp.concatenate([second_sums.reshape(-1), unit_grads(up_sums).reshape(-1)])
    late = jnp.concatenate(
        [
            first_sums[:2].reshape(-1),
            split_heads(total_over(0)),
            split_heads(total_over(2)),
        ]
    )
    if by_hops:
        early = hops.sum_all(early.reshape(-1, 128)).reshape(-1)
        late = hops.sum_all(late.reshape(-1, 128)).reshape(-1)
    else:
        early, late = lax.psum(early, everyone), lax.psum(late, everyone)
    early_part = lambda i: early[i * width : (i + 1) * width]
    late_part = lambda i: late[i * width : (i + 1) * width]
    up_all = early[4 * width :].reshape(tensor_count, slab_units)
    return (
        layer_out,
        input_grad,
        late_part(0),
        late_part(1),
        attn_back[0].T,
        lax.dynamic_slice_in_dim(late_part(2), col_start, head_cols),
        attn_back[1].T,
        attn_back[2].T,
        lax.dynamic_slice_in_dim(late_part(3), col_start, head_cols),
        attn_back[3],
        early_part(2),
        early_part(0),
        early_part(1),
        grad_w_up[:unit_cols].T,
        up_all[:, :unit_cols].reshape(-1),
        grad_w_down[:unit_cols],
        early_part(3),
    )


def solution(mesh):
    tokens = P(None, ("dp", "tensor"), None)
    columns = P("dp", "tensor")
    rows = P("tensor", "dp")
    return jax.shard_map(
        partial(shards, mesh.shape["dp"], mesh.shape["tensor"]),
        mesh=mesh,
        in_specs=(
            tokens,
            P(None, "dp", None),
            tokens,
            P(),
            P(),
            columns,
            P(),
            columns,
            columns,
            P(),
            rows,
            P(),
            P(),
            P(),
            columns,
            P(),
            rows,
            P(),
        ),
        out_specs=(
            tokens,
            tokens,
            P(),
            P(),
            columns,
            P("tensor"),
            columns,
            columns,
            P("tensor"),
            rows,
            P(),
            P(),
            P(),
            columns,
            P(),
            rows,
            P(),
        ),
        check_vma=False,
    )
```

```python
from functools import partial

import jax
import jax.numpy as jnp
from jax import lax
from jax.experimental import pallas as pl
from jax.experimental.pallas import tpu as pltpu
from jax.sharding import PartitionSpec as P

HEAD_DIM = 72
norm_eps = 1e-06
masked_score = -1000000000.0
low = jnp.bfloat16
wide = jnp.float32
score_scale = HEAD_DIM**-0.5
log2_e = 1.4426950408889634
gelu_scale = 0.7978845608028654
gelu_cube = 0.044715
everyone = ("dp", "tensor")


def product(left, right, left_dim, right_dim):
    return lax.dot_general(
        left, right, (((left_dim,), (right_dim,)), ((), ())), preferred_element_type=wide
    )


def attend_kernel(heads, query_ref, key_ref, value_ref, bias_ref, out_ref, total_ref):
    for head in range(heads):
        rows = slice(head * HEAD_DIM, (head + 1) * HEAD_DIM)
        scores = product(key_ref[rows, :], query_ref[rows, :], 0, 0) * (score_scale * log2_e)
        scores = scores + bias_ref[...]
        top = jnp.max(scores, axis=0, keepdims=True)
        weights = jnp.exp2(scores - top)
        total = jnp.sum(weights, axis=0, keepdims=True)
        mixed = product(value_ref[rows, :], weights.astype(low), 1, 0)
        out_ref[rows, :] = (mixed * (1.0 / total)).astype(low)
        total_ref[head] = top + jnp.log2(total)


def attend_back_kernel(
    heads,
    query_ref,
    key_ref,
    value_ref,
    bias_ref,
    out_ref,
    total_ref,
    weights_ref,
    branch_ref,
    grads_ref,
):
    grad_rows = product(weights_ref[...], branch_ref[...], 1, 1).astype(low)
    for head in range(heads):
        rows = slice(head * HEAD_DIM, (head + 1) * HEAD_DIM)
        query, key, value, grad = (
            query_ref[rows, :],
            key_ref[rows, :],
            value_ref[rows, :],
            grad_rows[rows, :],
        )
        scores = product(key, query, 0, 0) * (score_scale * log2_e) + bias_ref[...]
        probs = jnp.exp2(scores - total_ref[head])
        grad_probs = product(value, grad, 0, 0)
        along = jnp.sum(
            grad.astype(wide) * out_ref[rows, :].astype(wide), axis=0, keepdims=True
        )
        grad_raw = (probs * (grad_probs - along)).astype(low)
        grads_ref[2, rows, :] = product(grad, probs.astype(low), 1, 1).astype(low)
        grads_ref[0, rows, :] = (product(key, grad_raw, 1, 0) * score_scale).astype(low)
        grads_ref[1, rows, :] = (product(query, grad_raw, 1, 1) * score_scale).astype(low)


def attend(projected, bias, heads, step_heads):
    tokens = projected.shape[1]
    steps = heads // step_heads
    part = lambda place: pl.BlockSpec(
        (HEAD_DIM * step_heads, tokens), lambda i, place=place: (place * steps + i, 0)
    )
    return pl.pallas_call(
        partial(attend_kernel, step_heads),
        grid=(steps,),
        in_specs=[part(0), part(1), part(2), pl.BlockSpec((tokens, 1), lambda i: (0, 0))],
        out_specs=[part(0), pl.BlockSpec((step_heads, 1, tokens), lambda i: (i, 0, 0))],
        out_shape=[
            jax.ShapeDtypeStruct((heads * HEAD_DIM, tokens), low),
            jax.ShapeDtypeStruct((heads, 1, tokens), wide),
        ],
        compiler_params=pltpu.CompilerParams(vmem_limit_bytes=48 * 2**20),
        cost_estimate=pl.CostEstimate(
            flops=heads * tokens * tokens * 128, bytes_accessed=2**20, transcendentals=0
        ),
        name="attend",
    )(projected, projected, projected, bias)


def attend_back(projected, bias, attended, total, weights, branch, heads, step_heads):
    tokens = projected.shape[1]
    steps = heads // step_heads
    part = lambda place: pl.BlockSpec(
        (HEAD_DIM * step_heads, tokens), lambda i, place=place: (place * steps + i, 0)
    )
    return pl.pallas_call(
        partial(attend_back_kernel, step_heads),
        grid=(steps,),
        in_specs=[
            part(0),
            part(1),
            part(2),
            pl.BlockSpec((tokens, 1), lambda i: (0, 0)),
            part(0),
            pl.BlockSpec((step_heads, 1, tokens), lambda i: (i, 0, 0)),
            pl.BlockSpec((HEAD_DIM * step_heads, branch.shape[1]), lambda i: (3 * steps + i, 0)),
            pl.BlockSpec(branch.shape, lambda i: (0, 0)),
        ],
        out_specs=pl.BlockSpec((3, HEAD_DIM * step_heads, tokens), lambda i: (0, i, 0)),
        out_shape=jax.ShapeDtypeStruct((3, heads * HEAD_DIM, tokens), low),
        compiler_params=pltpu.CompilerParams(vmem_limit_bytes=48 * 2**20),
        cost_estimate=pl.CostEstimate(
            flops=heads * tokens * tokens * 128, bytes_accessed=2**20, transcendentals=0
        ),
        name="attend_back",
    )(projected, projected, projected, bias, attended, total, weights, branch)


def norm_forward(values, gain, shift):
    row_mean = jnp.mean(values, axis=-1, keepdims=True)
    centred = values - row_mean
    inv_scale = lax.rsqrt(jnp.mean(centred * centred, axis=-1, keepdims=True) + norm_eps)
    return (centred * inv_scale * gain + shift).astype(low)


def norm_back_kernel(values_ref, grad_ref, gain_ref, base_ref, full_ref, low_ref, sums_ref):
    values = values_ref[...].astype(wide)
    centred = values - jnp.mean(values, axis=-1, keepdims=True)
    inv_scale = lax.rsqrt(jnp.mean(centred * centred, axis=-1, keepdims=True) + norm_eps)
    unit = centred * inv_scale
    grad = grad_ref[...]
    scaled = grad * gain_ref[...]
    mean_grad = jnp.mean(scaled, axis=-1, keepdims=True)
    mean_along = jnp.mean(scaled * unit, axis=-1, keepdims=True)
    base = base_ref[...].astype(wide)
    full = base + inv_scale * (scaled - mean_grad - unit * mean_along)
    rounded = full.astype(low)
    full_ref[...] = full
    low_ref[...] = rounded
    total = lambda rows: jnp.sum(rows, axis=0, keepdims=True)
    sums = jnp.concatenate(
        [total(grad * unit), total(grad), total(rounded.astype(wide)), total(base)], axis=0
    )

    @pl.when(pl.program_id(0) == 0)
    def first():
        sums_ref[...] = sums

    @pl.when(pl.program_id(0) > 0)
    def later():
        sums_ref[...] += sums


def norm_back(values, grad, gain, base):
    tokens, width = values.shape
    block = tokens // 4
    rows = pl.BlockSpec((block, width), lambda i: (i, 0))
    return pl.pallas_call(
        norm_back_kernel,
        grid=(4,),
        in_specs=[rows, rows, pl.BlockSpec((1, width), lambda i: (0, 0)), rows],
        out_specs=[rows, rows, pl.BlockSpec((4, width), lambda i: (0, 0))],
        out_shape=[
            jax.ShapeDtypeStruct((tokens, width), wide),
            jax.ShapeDtypeStruct((tokens, width), low),
            jax.ShapeDtypeStruct((4, width), wide),
        ],
        compiler_params=pltpu.CompilerParams(vmem_limit_bytes=40 * 2**20),
        cost_estimate=pl.CostEstimate(
            flops=tokens * width, bytes_accessed=tokens * width, transcendentals=0
        ),
        name="norm_back",
    )(values, grad, gain.reshape(1, width), base)


def mlp_kernel(carried, plan, normed_ref, grad_ref, bias_ref, *refs):
    starts, rows, group, pieces = plan
    weights, refs = refs[:pieces], refs[pieces:]
    steps = 32 // group
    if carried:
        out_before, normed_before = refs[:2]
        refs = refs[2:]
    out_ref, grad_normed_ref, *grad_refs, grad_bias_ref, ups, downs, sems = refs
    step = pl.program_id(0)
    slot = step % 2

    def copies(at):
        moves = []
        many = group if pieces == 1 else 2
        size = group // many * rows
        for place in range(many):
            block = weights[0].at[at * many + place] if pieces == 1 else weights[2 * at + place]
            for kind, target in enumerate((ups, downs)):
                moves.append(
                    pltpu.make_async_copy(
                        block.at[pl.ds(starts[kind], size)],
                        target.at[at % 2, pl.ds(place * size, size)],
                        sems.at[at % 2, 2 * place + kind],
                    )
                )
        return moves

    for at in range(steps):

        @pl.when(step + 1 == at if at else step == 0)
        def fetch():
            for move in copies(at):
                move.start()

    for at in range(steps):

        @pl.when(step == at)
        def arrive():
            for move in copies(at):
                move.wait()

    normed, grad = normed_ref[...], grad_ref[...]
    up, down = ups[slot], downs[slot]
    pre_act = product(up, normed, 1, 1) + bias_ref[...]
    square = pre_act * pre_act
    bent = jnp.tanh(gelu_scale * (pre_act + gelu_cube * square * pre_act))
    half = 0.5 * (1.0 + bent)
    active = (pre_act * half).astype(low)
    slope = half + 0.5 * pre_act * (1.0 - bent * bent) * (
        gelu_scale * (1.0 + 3.0 * gelu_cube * square)
    )
    grad_wide = product(down, grad, 1, 1) * slope
    grad_pre = grad_wide.astype(low)
    grad_bias_ref[...] = jnp.sum(grad_wide, axis=1, keepdims=True)
    grad_down = product(active, grad, 1, 0).astype(low)
    grad_up = product(grad_pre, normed, 1, 0).astype(low)

    def keep(ref):
        many = ref.shape[2]
        for place in range(ref.shape[0]):
            ref[place, 0] = grad_up[place * many : (place + 1) * many]
            ref[place, 1] = grad_down[place * many : (place + 1) * many]

    if pieces == 1:
        keep(grad_refs[0])
    else:
        pl.when(step < 2)(lambda: keep(grad_refs[0]))
        pl.when(step >= 2)(lambda: keep(grad_refs[1]))
    out_term = product(active, down, 0, 0)
    normed_term = product(grad_pre, up, 0, 0)

    @pl.when(step == 0)
    def first():
        if carried:
            out_ref[...] = out_before[...] + out_term
            grad_normed_ref[...] = normed_before[...] + normed_term
        else:
            out_ref[...] = out_term
            grad_normed_ref[...] = normed_term

    @pl.when(step > 0)
    def later():
        out_ref[...] += out_term
        grad_normed_ref[...] += normed_term


def mlp(normed, grad, bias, weights, starts, rows, group=8, before=None):
    tokens, width = normed.shape
    steps = 32 // group
    whole = pl.BlockSpec((tokens, width), lambda i: (0, 0))
    column = pl.BlockSpec((group * rows, 1), lambda i: (i, 0))
    if len(weights) == 1:
        grad_specs = [pl.BlockSpec((group, 2, rows, width), lambda i: (i, 0, 0, 0))]
        grad_shapes = [jax.ShapeDtypeStruct((32, 2, rows, width), low)]
    else:
        part = (2, 2, 4 * rows, width)
        grad_specs = [
            pl.BlockSpec(part, lambda i: (jnp.minimum(i, 1), 0, 0, 0)),
            pl.BlockSpec(part, lambda i: (jnp.maximum(i - 2, 0), 0, 0, 0)),
        ]
        grad_shapes = [jax.ShapeDtypeStruct((4, 2, 4 * rows, width), low)] * 2
    earlier = [] if before is None else list(before)
    return pl.pallas_call(
        partial(mlp_kernel, before is not None, (starts, rows, group, len(weights))),
        grid=(steps,),
        in_specs=[whole, whole, column]
        + [pl.BlockSpec(memory_space=pl.ANY)] * len(weights)
        + [whole] * len(earlier),
        out_specs=[whole, whole] + grad_specs + [column],
        out_shape=[jax.ShapeDtypeStruct((tokens, width), wide)] * 2
        + grad_shapes
        + [jax.ShapeDtypeStruct((32 * rows, 1), wide)],
        scratch_shapes=[
            pltpu.VMEM((2, group * rows, width), low),
            pltpu.VMEM((2, group * rows, width), low),
            pltpu.SemaphoreType.DMA((2, 2 * group)),
        ],
        input_output_aliases=(
            {3 + len(weights): 0, 4 + len(weights): 1} if earlier else {}
        ),
        compiler_params=pltpu.CompilerParams(vmem_limit_bytes=60 * 2**20),
        cost_estimate=pl.CostEstimate(
            flops=2 * tokens * width * 32 * rows, bytes_accessed=2**20, transcendentals=0
        ),
        name="mlp",
    )(normed, grad, bias, *weights, *earlier)


def kinds_kernel(slabs, kind_ref, grads_ref, attended_ref, normed_ref, branch_ref, *outs):
    kind = pl.program_id(0)
    held = outs[8]
    rows = held.shape[0] // slabs

    own = ((kind ^ kind_ref[0]) & 1) == 0

    def keep(terms):
        def block(spot):
            slab = spot
            if slabs == 8:
                away = (spot >> 2) * 4 + (spot & 1) * 2 + ((spot >> 1) & 1)
                slab = away ^ kind_ref[1]
            start = pl.multiple_of(slab * rows, 16)
            return held[pl.ds(start, rows), :]

        held[...] = terms
        across = (kind ^ kind_ref[0]) >> 1
        many = slabs // 4 if slabs > 1 else 1

        def put(near, near_y, far, far_x):
            for place in range(many):
                near[0, place] = block(place)
                near_y[0, place] = block(many + place)
            for place in range(2 * many):

                @pl.when(across == 0)
                def same():
                    far[place] = block(2 * many + place)

                @pl.when(across == 1)
                def other():
                    far_x[place] = block(2 * many + place)

        pl.when(own)(lambda: put(*outs[:4]))
        pl.when(jnp.logical_not(own))(lambda: put(*outs[4:8]))

    @pl.when(kind < 3)
    def projections():
        keep(product(grads_ref[0], normed_ref[...], 1, 0).astype(low))

    @pl.when(kind == 3)
    def output():
        keep(product(attended_ref[...], branch_ref[...], 1, 0).astype(low))


def kinds_grad(places, grads, attended, normed, branch, slabs):
    _, rows, tokens = grads.shape
    width = normed.shape[1]
    whole = pl.BlockSpec((tokens, width), lambda k, ref: (0, 0))
    many, each = slabs // 4, rows // slabs
    near = pl.BlockSpec((1, many, each, width), lambda k, ref: ((k ^ ref[0]) >> 1, 0, 0, 0))
    far = pl.BlockSpec((2 * many, each, width), lambda k, ref: (0, 0, 0))
    near_shape = jax.ShapeDtypeStruct((2, many, each, width), low)
    far_shape = jax.ShapeDtypeStruct((2 * many, each, width), low)
    return pl.pallas_call(
        partial(kinds_kernel, slabs),
        grid_spec=pltpu.PrefetchScalarGridSpec(
            num_scalar_prefetch=1,
            grid=(4,),
            in_specs=[
                pl.BlockSpec((1, rows, tokens), lambda k, ref: (jnp.minimum(k, 2), 0, 0)),
                pl.BlockSpec((rows, tokens), lambda k, ref: (0, 0)),
                whole,
                whole,
            ],
            out_specs=[near, near, far, far] * 2,
            scratch_shapes=[pltpu.VMEM((rows, width), low)],
        ),
        out_shape=[near_shape, near_shape, far_shape, far_shape] * 2,
        compiler_params=pltpu.CompilerParams(vmem_limit_bytes=48 * 2**20),
        cost_estimate=pl.CostEstimate(
            flops=rows * width * tokens, bytes_accessed=2**20, transcendentals=0
        ),
        name="kinds_grad",
    )(places, grads, attended, normed, branch)


def unite_kernel(kind_ref, *refs):
    outs = refs[4:]
    part = refs[0].shape[1]
    for distance in range(4):
        source = kind_ref[0] ^ distance
        for column in range(4):

            @pl.when(source == column)
            def put():
                start = 0
                for out in outs:
                    rows = out.shape[0]
                    out[:, column * part : (column + 1) * part] = refs[distance][
                        start : start + rows, :
                    ]
                    start += rows


def unite(kind, blocks, cuts):
    part = blocks[0].shape[1]
    local = pl.BlockSpec(memory_space=pltpu.VMEM)
    return pl.pallas_call(
        unite_kernel,
        in_specs=[pl.BlockSpec(memory_space=pltpu.SMEM)] + [local] * 4,
        out_specs=[local] * len(cuts),
        out_shape=[jax.ShapeDtypeStruct((rows, 4 * part), low) for rows in cuts],
        name="unite",
    )(kind, *blocks)


def divide_kernel(kind_ref, *refs):
    ins, outs = refs[:-4], refs[-4:]
    part = outs[0].shape[1]
    for distance in range(4):
        target = kind_ref[0] ^ distance
        for column in range(4):

            @pl.when(target == column)
            def put():
                start = 0
                for ref in ins:
                    rows = ref.shape[0]
                    outs[distance][start : start + rows, :] = ref[
                        :, column * part : (column + 1) * part
                    ]
                    start += rows


def divide(kind, owned):
    rows = sum(values.shape[0] for values in owned)
    part = owned[0].shape[1] // 4
    local = pl.BlockSpec(memory_space=pltpu.VMEM)
    return pl.pallas_call(
        divide_kernel,
        in_specs=[pl.BlockSpec(memory_space=pltpu.SMEM)] + [local] * len(owned),
        out_specs=[local] * 4,
        out_shape=[jax.ShapeDtypeStruct((rows, part), low)] * 4,
        name="divide",
    )(kind, *owned)


def settle_kernel(kind_ref, *refs):
    for distance in range(4):
        refs[4][kind_ref[0] ^ distance] = refs[distance][...].astype(wide)


def settle(kind, blocks):
    rows, part = blocks[0].shape
    local = pl.BlockSpec(memory_space=pltpu.VMEM)
    return pl.pallas_call(
        settle_kernel,
        in_specs=[pl.BlockSpec(memory_space=pltpu.SMEM)] + [local] * 4,
        out_specs=local,
        out_shape=jax.ShapeDtypeStruct((4, rows, part), wide),
        name="settle",
    )(kind, *blocks)


def after(values, *earlier):
    return lax.optimization_barrier((values, earlier))[0]


def add_low(*terms):
    total = terms[0].astype(wide)
    for term in terms[1:]:
        total = total + term.astype(wide)
    return total.astype(low)


def join(kinds, *blocks):
    width = blocks[0].shape[-1]
    parts = [block.reshape(kinds, -1, width) for block in blocks]
    return jnp.concatenate(parts, axis=1).reshape(-1, width)


class Hops:
    def __init__(self, dp_count, tensor_count):
        self.count = dp_count * tensor_count
        self.y, self.z = 1, (2, 4, 6)
        self.core, self.x = tensor_count, 2 * tensor_count
        self.near, self.far = (0, 2), (4, 6)

    def send(self, values, distance):
        pairs = [(place, place ^ distance) for place in range(self.count)]
        return lax.ppermute(values, everyone, pairs)

    def order(self):
        x, y = self.x, self.y
        near = [n ^ p ^ q for q in (0, y) for p in (0, x) for n in self.near]
        far = [n ^ p ^ q for q in (0, x) for p in (0, y) for n in self.far]
        return near + far

    def along_z(self, block):
        return [self.send(block, z) for z in self.z]

    def second_operands(self, kinds, block, arrived):
        z1, z2, z3 = arrived
        return join(kinds, block, z1), join(kinds, z2, z3)

    def sibling(self, *pieces):
        return [self.send(piece, self.core) for piece in pieces]

    def across_dp(self, blocks):
        return [blocks[0]] + [self.send(blocks[j], j * self.core) for j in (1, 2, 3)]


class Reduction:
    def __init__(self, hops, own, sibling, joined):
        self.hops, self.own, self.joined = hops, own, joined
        if joined:
            self.arrived = hops.send(sibling, hops.core)
        else:
            self.arrived = [hops.send(piece, hops.core) for piece in sibling]
        self.width = own[0].shape[-1]

    def part(self, place):
        return self.own[place], self.arrived[place]

    def halves(self, values):
        axis = 1 if self.joined else 0
        shape = (2, 2, 2, -1, self.width) if self.joined else (2, 2, -1, self.width)
        values = values.reshape(shape)
        return [lax.index_in_dim(values, place, axis, keepdims=False) for place in (0, 1)]

    def blocks(self, values):
        axis = 1 if self.joined else 0
        return [lax.index_in_dim(values, place, axis, keepdims=False) for place in (0, 1)]

    def ready_third(self):
        self.operands = add_low(*self.part(1)), add_low(*self.part(3))
        return self.operands

    def send_third(self):
        near, far = self.operands
        self.moved = self.hops.send(near, self.hops.y), self.hops.send(far, self.hops.x)

    def third(self):
        near, far = self.moved
        near, far = add_low(*self.part(0), near), add_low(*self.part(2), far)
        self.near, self.far = self.halves(near), self.halves(far)
        self.operands = self.near[1], self.far[1]
        return self.operands

    def send_second(self):
        near, far = self.operands
        self.moved = self.hops.send(near, self.hops.x), self.hops.send(far, self.hops.y)

    def second(self):
        near, far = self.moved
        near, far = add_low(self.near[0], near), add_low(self.far[0], far)
        self.near, self.far = self.blocks(near), self.blocks(far)
        self.operands = self.near[1], self.far[0], self.far[1]
        return self.operands

    def send_along_z(self):
        self.moved = [
            self.hops.send(v, z) for v, z in zip(self.operands, self.hops.z, strict=True)
        ]

    def along_z(self):
        return add_low(self.near[0], *self.moved)


def shards(
    dp_count,
    tensor_count,
    inputs,
    pad_mask,
    cotangent,
    attn_norm_gain,
    attn_norm_shift,
    w_query,
    b_query,
    w_key,
    w_value,
    b_value,
    w_out,
    b_out,
    mlp_norm_gain,
    mlp_norm_shift,
    w_up,
    b_up,
    w_down,
    b_down,
):
    half_rows, width = inputs.shape[1:]
    tokens = 2 * half_rows
    head_cols = w_query.shape[1]
    unit_cols = w_up.shape[1]
    quantum = 8 * dp_count
    slab_units = -(-unit_cols // quantum) * quantum
    by_hops = (dp_count, tensor_count) == (4, 8)
    dp_place, tensor_place = lax.axis_index("dp"), lax.axis_index("tensor")
    devices = dp_count * tensor_count
    here = (dp_place * tensor_count + tensor_place).astype(jnp.int32)
    col_start = tensor_place * head_cols
    side = tensor_place % 2
    pairs = [(place, place ^ 1) for place in range(tensor_count)]
    hops = Hops(dp_count, tensor_count)
    places = jnp.stack([dp_place, tensor_place]).astype(jnp.int32)
    places = places if by_hops else places * 0
    kind = places[:1]
    heads = head_cols * tensor_count // HEAD_DIM

    def swap(values):
        return lax.ppermute(values, "tensor", pairs)

    def one_slot(values, *earlier):
        kept = lax.dynamic_index_in_dim(values, side, 0, keepdims=False)
        sent = lax.dynamic_index_in_dim(values, 1 - side, 0, keepdims=False)
        if earlier:
            sent = after(sent, *earlier)
        return jnp.concatenate([kept, swap(sent)], axis=0)

    def both_micros(kept, other):
        return jnp.where(side == 0, jnp.stack([kept, other]), jnp.stack([other, kept]))

    unit_pad = ((0, slab_units - unit_cols), (0, 0))
    up_cols, down_cols = jnp.pad(w_up.T, unit_pad), jnp.pad(w_down, unit_pad)
    attn_cols = jnp.concatenate([w_query.T, w_key.T, w_value.T, w_out], axis=0)
    if by_hops:
        unit_cuts = (48, slab_units // 4 - 48)
        first_units = 4 * unit_cuts[0]
        share = lambda values, low_end, high_end: values[low_end:high_end].reshape(
            4, -1, values.shape[1]
        )
        mlp_cols = jnp.concatenate(
            [
                share(up_cols, 0, first_units),
                share(down_cols, 0, first_units),
                share(up_cols, first_units, slab_units),
                share(down_cols, first_units, slab_units),
            ],
            axis=1,
        )
        attn_cols = attn_cols.reshape(4, head_cols, -1)
        pick = lambda values, j: lax.dynamic_index_in_dim(
            values, dp_place ^ j, 0, keepdims=False
        )
        attn_blocks = hops.across_dp([pick(attn_cols, j) for j in range(4)])
        (attn_block,) = unite(kind, attn_blocks, (head_cols,))
        mlp_blocks = hops.across_dp([pick(mlp_cols, j) for j in range(4)])
        bulk_block, hop_block = unite(kind, mlp_blocks, [2 * rows for rows in unit_cuts])
        attn_rows = lax.all_gather(attn_block, everyone).reshape(4, -1, width)
        x_slot = one_slot(inputs)
        grad_out = one_slot(cotangent, x_slot)
        bulk_weights = lax.all_gather(bulk_block, everyone)
        hop_z = hops.along_z(hop_block)
        order = hops.order()
        order = [place ^ hops.core for place in order] + order
        unit_places = here ^ jnp.array(order)
        unit_here = (unit_places[:, None] == jnp.arange(devices)[None, :]).astype(wide)
        shuffled = partial(jnp.dot, precision=lax.Precision.HIGHEST)
    else:
        x_slot, grad_out = one_slot(inputs), one_slot(cotangent)
        unit_cuts = (slab_units // dp_count,)

        def gathered(values):
            owned = lax.all_to_all(
                values.reshape(dp_count, -1, values.shape[1]), "dp", 0, 2, tiled=True
            )
            return lax.all_gather(owned[0], everyone, axis=0, tiled=True)

        attn_rows = gathered(attn_cols)
        attn_rows = attn_rows.reshape(4, dp_count // 4, tensor_count, -1, width)
        attn_rows = attn_rows.transpose(0, 2, 1, 3, 4).reshape(4, -1, width)
        columns = [values.reshape(dp_count, -1, values.shape[1]) for values in (up_cols, down_cols)]
        unit_weights = gathered(jnp.concatenate(columns, axis=1).reshape(2 * slab_units, -1))
        unit_weights = unit_weights.reshape(32, devices // 32, 2, -1, width)
        bulk_weights = unit_weights.transpose(0, 2, 1, 3, 4).reshape(32, -1, width)

    slab_bias = jnp.pad(
        b_up.reshape(tensor_count, unit_cols), ((0, 0), (0, slab_units - unit_cols))
    )
    unit_starts = [dp_count * sum(unit_cuts[:i]) for i in range(len(unit_cuts) + 1)]

    def unit_bias(part):
        values = slab_bias[:, unit_starts[part] : unit_starts[part + 1]]
        values = values.reshape(tensor_count, dp_count, -1).transpose(1, 0, 2)
        if part == 1:
            values = shuffled(unit_here, values.reshape(devices, -1))
        return values.reshape(-1, 1)

    def unit_grads(values):
        slabs = []
        for place, part in enumerate(values):
            if place == 1:
                part = shuffled(unit_here.T, part.reshape(devices, -1))
            part = part.reshape(dp_count, tensor_count, -1).transpose(1, 0, 2)
            slabs.append(part.reshape(tensor_count, -1))
        return jnp.concatenate(slabs, axis=1)

    mask_row = lax.dynamic_slice(pad_mask, (side, tensor_place // 2, 0), (1, 1, tokens))
    mask_row = mask_row.reshape(2, half_rows)
    mask_row = jnp.where(side == 0, mask_row, mask_row[::-1]).reshape(tokens, 1)
    bias_col = jnp.where(mask_row > 0, 0.0, masked_score).astype(wide)

    normed_first = norm_forward(x_slot.astype(wide), attn_norm_gain, attn_norm_shift)
    qkv_rows, out_rows = attn_rows[:3].reshape(-1, width), attn_rows[3]
    qkv_bias = jnp.concatenate([b_query, jnp.zeros_like(b_query), b_value])
    projected = (product(qkv_rows, normed_first, 1, 1) + qkv_bias[:, None]).astype(low)
    if by_hops:
        hop_z = after(hop_z, grad_out, normed_first)
    if by_hops:
        hop_near, hop_far = hops.second_operands(2, hop_block, hop_z)
        near_x, far_y = hops.send(hop_near, hops.x), hops.send(hop_far, hops.y)
        near_x, far_y = after((near_x, far_y))
        hop_near, hop_far = join(2, hop_near, near_x), join(2, hop_far, far_y)
        attended, totals = attend(projected, bias_col, heads, 4)
        near_y, far_x = hops.send(hop_near, hops.y), hops.send(hop_far, hops.x)
        near_y, far_x = after((near_y, far_x), attended)
        hop_three = [hop_near, near_y, hop_far, far_x]
        hop_weights = hops.sibling(*hop_three) + list(hop_three)
    else:
        attended, totals = attend(projected, bias_col, heads, 4)
    branch = product(attended, out_rows, 0, 0) + b_out
    middle = x_slot.astype(wide) + branch
    normed_second = norm_forward(middle, mlp_norm_gain, mlp_norm_shift)
    rows = unit_cuts[0] * devices // 32
    sums, up_sums = None, []
    if by_hops:
        *sums, grad_sibling, grad_own, up_sum = mlp(
            normed_second,
            grad_out,
            unit_bias(1),
            hop_weights,
            (0, 4 * unit_cuts[1]),
            unit_cuts[1],
        )
        up_sums.append(up_sum[:, 0])
    bulk = partial(
        mlp,
        normed_second,
        grad_out,
        unit_bias(0),
        [bulk_weights],
        (0, rows),
        rows,
        16 if by_hops else 4,
    )
    if by_hops:
        units = Reduction(hops, grad_own, grad_sibling, True)
        sums = after(sums, units.ready_third())
        units.send_third()
        *sums, bulk_grads, up_sum = bulk(sums)
    else:
        *sums, bulk_grads, up_sum = bulk()
    up_sums = [up_sum[:, 0]] + up_sums
    bulk_grads = bulk_grads.reshape(32, 2, devices // 32, -1, width).transpose(0, 2, 1, 3, 4)
    bulk_owned = lax.psum_scatter(
        bulk_grads.reshape(2 * 32 * rows, width), everyone, scatter_dimension=0, tiled=True
    )
    down_out, grad_normed_second = sums
    if by_hops:
        units_third = units.third()
        grad_normed_second = after(grad_normed_second, units_third)
    grad_middle, grad_branch, second_sums = norm_back(
        middle, grad_normed_second, mlp_norm_gain, grad_out
    )
    out_low = (middle + (down_out + b_down)).astype(low)
    back = partial(
        attend_back, projected, bias_col, attended, totals, attn_rows.reshape(-1, width)
    )
    if by_hops:
        units.send_second()
        out_other = swap(after(out_low[half_rows:], units_third))
        grads = back(grad_branch, heads, 4)
        grads, out_other = after((grads, out_other), units.second())
        layer_out = both_micros(out_low[:half_rows], out_other)
        units.send_along_z()
        kind_grads = kinds_grad(
            places, grads, attended, normed_first, grad_branch, tensor_count
        )
        attns = Reduction(hops, kind_grads[:4], kind_grads[4:], False)
        grads = after(grads, kind_grads)
        first_terms = product(grads.reshape(-1, tokens), qkv_rows, 0, 0)
        units.moved = after(units.moved, first_terms)
        first_terms = after(first_terms, attns.ready_third())
        attns.send_third()
        input_full, input_low, first_sums = norm_back(
            x_slot, first_terms, attn_norm_gain, grad_middle
        )
        units_owned = units.along_z()
        attns.moved = after(attns.moved, units_owned)
        attns_third = attns.third()
    else:
        grads = back(grad_branch, heads, 4)
        first_terms = product(grads.reshape(-1, tokens), qkv_rows, 0, 0)
        input_full, input_low, first_sums = norm_back(
            x_slot, first_terms, attn_norm_gain, grad_middle
        )
        out_other = swap(out_low[half_rows:])
        layer_out = both_micros(out_low[:half_rows], out_other)

    total_over = lambda i: jnp.sum(grads[i], axis=1, dtype=wide)
    small = jnp.concatenate(
        [
            second_sums.reshape(-1),
            first_sums[:2].reshape(-1),
            total_over(0),
            total_over(2),
            unit_grads(up_sums).reshape(-1),
        ]
    )
    if by_hops:
        small, mlp_owned = after(
            (small.reshape(-1, 128), [bulk_owned, units_owned[0], units_owned[1]]), attns_third
        )
        attns.send_second()
        small = small + sum(hops.send(small, z) for z in hops.z)
        mlp_parts = divide(kind, mlp_owned)
        attns.moved = after(attns.moved, small, mlp_parts)
        attns_second = attns.second()
        attns.send_along_z()
        small, input_low, mlp_parts = after((small, input_low, mlp_parts), attns_second)
        input_other = swap(input_low[half_rows:])
        mlp_blocks = hops.across_dp(mlp_parts)
        mlp_back = settle(kind, mlp_blocks)
        attns.moved = after(attns.moved, mlp_back, input_other)
        small = after(small, attns.moved)
        small = small + hops.send(small, hops.y)
        small = small + sum(hops.send(small, j * hops.core) for j in (1, 2, 3))
        attn_parts = divide(kind, [attns.along_z()])
        attn_back = settle(kind, hops.across_dp(attn_parts))
        small = small.reshape(-1)
    else:
        small = lax.psum(small, everyone)
        input_other = swap(input_low[half_rows:])
    input_grad = both_micros(input_full[:half_rows], input_other.astype(wide))

    if by_hops:
        bounds = [0]
        for rows in (unit_cuts[0], unit_cuts[0], unit_cuts[1], unit_cuts[1]):
            bounds.append(bounds[-1] + rows)
        parts = [
            mlp_back[:, bounds[i] : bounds[i + 1]].reshape(-1, mlp_back.shape[2])
            for i in range(4)
        ]
        grad_w_up = jnp.concatenate([parts[0], parts[2]], axis=0)
        grad_w_down = jnp.concatenate([parts[1], parts[3]], axis=0)
    else:

        def to_columns(owned):
            back = lax.all_to_all(owned[None], "dp", 2, 0, tiled=True)
            return back.reshape(-1, width // dp_count).astype(wide)

        columns = to_columns(bulk_owned)
        columns = columns.reshape(dp_count, 2, -1, columns.shape[1])
        grad_w_up = columns[:, 0].reshape(-1, columns.shape[3])
        grad_w_down = columns[:, 1].reshape(-1, columns.shape[3])
        flat = grads.reshape(-1, tokens)
        terms = [product(flat, normed_first, 1, 0), product(attended, grad_branch, 1, 0)]
        terms = jnp.concatenate(terms, axis=0).astype(low)
        terms = terms.reshape(4, tensor_count, dp_count // 4, -1, width)
        terms = terms.transpose(0, 2, 1, 3, 4).reshape(-1, width)
        owned = lax.psum_scatter(terms, everyone, scatter_dimension=0, tiled=True)
        attn_back = to_columns(owned).reshape(4, head_cols, -1)

    part = lambda i: small[i * width : (i + 1) * width]
    up_all = small[8 * width :].reshape(tensor_count, slab_units)
    return (
        layer_out,
        input_grad,
        part(4),
        part(5),
        attn_back[0].T,
        lax.dynamic_slice_in_dim(part(6), col_start, head_cols),
        attn_back[1].T,
        attn_back[2].T,
        lax.dynamic_slice_in_dim(part(7), col_start, head_cols),
        attn_back[3],
        part(2),
        part(0),
        part(1),
        grad_w_up[:unit_cols].T,
        up_all[:, :unit_cols].reshape(-1),
        grad_w_down[:unit_cols],
        part(3),
    )


def solution(mesh):
    tokens = P(None, ("dp", "tensor"), None)
    columns = P("dp", "tensor")
    rows = P("tensor", "dp")
    return jax.shard_map(
        partial(shards, mesh.shape["dp"], mesh.shape["tensor"]),
        mesh=mesh,
        in_specs=(
            tokens,
            P(None, "dp", None),
            tokens,
            P(),
            P(),
            columns,
            P(),
            columns,
            columns,
            P(),
            rows,
            P(),
            P(),
            P(),
            columns,
            P(),
            rows,
            P(),
        ),
        out_specs=(
            tokens,
            tokens,
            P(),
            P(),
            columns,
            P("tensor"),
            columns,
            columns,
            P("tensor"),
            rows,
            P(),
            P(),
            P(),
            columns,
            P(),
            rows,
            P(),
        ),
        check_vma=False,
    )
```

```python
from functools import partial

import jax
import jax.numpy as jnp
from jax import lax
from jax.experimental import pallas as pl
from jax.experimental.pallas import tpu as pltpu
from jax.sharding import PartitionSpec as P

HEAD_DIM = 72
norm_eps = 1e-06
masked_score = -1000000000.0
low = jnp.bfloat16
wide = jnp.float32
score_scale = HEAD_DIM**-0.5
log2_e = 1.4426950408889634
gelu_scale = 0.7978845608028654
gelu_cube = 0.044715
everyone = ("dp", "tensor")


def product(left, right, left_dim, right_dim):
    return lax.dot_general(
        left, right, (((left_dim,), (right_dim,)), ((), ())), preferred_element_type=wide
    )


def attend_kernel(heads, query_ref, key_ref, value_ref, bias_ref, out_ref, total_ref):
    for head in range(heads):
        rows = slice(head * HEAD_DIM, (head + 1) * HEAD_DIM)
        scores = product(key_ref[rows, :], query_ref[rows, :], 0, 0) * (score_scale * log2_e)
        scores = scores + bias_ref[...]
        top = jnp.max(scores, axis=0, keepdims=True)
        weights = jnp.exp2(scores - top)
        total = jnp.sum(weights, axis=0, keepdims=True)
        mixed = product(value_ref[rows, :], weights.astype(low), 1, 0)
        out_ref[rows, :] = (mixed * (1.0 / total)).astype(low)
        total_ref[head] = top + jnp.log2(total)


def attend_back_kernel(
    heads,
    query_ref,
    key_ref,
    value_ref,
    bias_ref,
    out_ref,
    total_ref,
    weights_ref,
    branch_ref,
    grads_ref,
):
    grad_rows = product(weights_ref[...], branch_ref[...], 1, 1).astype(low)
    for head in range(heads):
        rows = slice(head * HEAD_DIM, (head + 1) * HEAD_DIM)
        query, key, value, grad = (
            query_ref[rows, :],
            key_ref[rows, :],
            value_ref[rows, :],
            grad_rows[rows, :],
        )
        scores = product(key, query, 0, 0) * (score_scale * log2_e) + bias_ref[...]
        probs = jnp.exp2(scores - total_ref[head])
        grad_probs = product(value, grad, 0, 0)
        along = jnp.sum(
            grad.astype(wide) * out_ref[rows, :].astype(wide), axis=0, keepdims=True
        )
        grad_raw = (probs * (grad_probs - along)).astype(low)
        grads_ref[2, rows, :] = product(grad, probs.astype(low), 1, 1).astype(low)
        grads_ref[0, rows, :] = (product(key, grad_raw, 1, 0) * score_scale).astype(low)
        grads_ref[1, rows, :] = (product(query, grad_raw, 1, 1) * score_scale).astype(low)


def attend(projected, bias, heads, step_heads):
    tokens = projected.shape[1]
    steps = heads // step_heads
    part = lambda place: pl.BlockSpec(
        (HEAD_DIM * step_heads, tokens), lambda i, place=place: (place * steps + i, 0)
    )
    return pl.pallas_call(
        partial(attend_kernel, step_heads),
        grid=(steps,),
        in_specs=[part(0), part(1), part(2), pl.BlockSpec((tokens, 1), lambda i: (0, 0))],
        out_specs=[part(0), pl.BlockSpec((step_heads, 1, tokens), lambda i: (i, 0, 0))],
        out_shape=[
            jax.ShapeDtypeStruct((heads * HEAD_DIM, tokens), low),
            jax.ShapeDtypeStruct((heads, 1, tokens), wide),
        ],
        compiler_params=pltpu.CompilerParams(vmem_limit_bytes=48 * 2**20),
        cost_estimate=pl.CostEstimate(
            flops=heads * tokens * tokens * 128, bytes_accessed=2**20, transcendentals=0
        ),
        name="attend",
    )(projected, projected, projected, bias)


def attend_back(projected, bias, attended, total, weights, branch, heads, step_heads):
    tokens = projected.shape[1]
    steps = heads // step_heads
    part = lambda place: pl.BlockSpec(
        (HEAD_DIM * step_heads, tokens), lambda i, place=place: (place * steps + i, 0)
    )
    return pl.pallas_call(
        partial(attend_back_kernel, step_heads),
        grid=(steps,),
        in_specs=[
            part(0),
            part(1),
            part(2),
            pl.BlockSpec((tokens, 1), lambda i: (0, 0)),
            part(0),
            pl.BlockSpec((step_heads, 1, tokens), lambda i: (i, 0, 0)),
            pl.BlockSpec((HEAD_DIM * step_heads, branch.shape[1]), lambda i: (3 * steps + i, 0)),
            pl.BlockSpec(branch.shape, lambda i: (0, 0)),
        ],
        out_specs=pl.BlockSpec((3, HEAD_DIM * step_heads, tokens), lambda i: (0, i, 0)),
        out_shape=jax.ShapeDtypeStruct((3, heads * HEAD_DIM, tokens), low),
        compiler_params=pltpu.CompilerParams(vmem_limit_bytes=48 * 2**20),
        cost_estimate=pl.CostEstimate(
            flops=heads * tokens * tokens * 128, bytes_accessed=2**20, transcendentals=0
        ),
        name="attend_back",
    )(projected, projected, projected, bias, attended, total, weights, branch)


def norm_forward(values, gain, shift):
    row_mean = jnp.mean(values, axis=-1, keepdims=True)
    centred = values - row_mean
    inv_scale = lax.rsqrt(jnp.mean(centred * centred, axis=-1, keepdims=True) + norm_eps)
    return (centred * inv_scale * gain + shift).astype(low)


def norm_back_kernel(values_ref, grad_ref, gain_ref, base_ref, *refs):
    if len(refs) > 3:
        down_ref, shift_ref, full_ref, low_ref, sums_ref, kept_ref, sent_ref = refs
        total = (values_ref[...] + (down_ref[...] + shift_ref[...])).astype(low)
        early = pl.program_id(0) < 2

        @pl.when(early)
        def keep():
            kept_ref[...] = total

        @pl.when(jnp.logical_not(early))
        def give():
            sent_ref[...] = total

    else:
        full_ref, low_ref, sums_ref = refs
    values = values_ref[...].astype(wide)
    centred = values - jnp.mean(values, axis=-1, keepdims=True)
    inv_scale = lax.rsqrt(jnp.mean(centred * centred, axis=-1, keepdims=True) + norm_eps)
    unit = centred * inv_scale
    grad = grad_ref[...]
    scaled = grad * gain_ref[...]
    mean_grad = jnp.mean(scaled, axis=-1, keepdims=True)
    mean_along = jnp.mean(scaled * unit, axis=-1, keepdims=True)
    base = base_ref[...].astype(wide)
    full = base + inv_scale * (scaled - mean_grad - unit * mean_along)
    rounded = full.astype(low)
    full_ref[...] = full
    low_ref[...] = rounded
    total = lambda rows: jnp.sum(rows, axis=0, keepdims=True)
    sums = jnp.concatenate(
        [total(grad * unit), total(grad), total(rounded.astype(wide)), total(base)], axis=0
    )

    @pl.when(pl.program_id(0) == 0)
    def first():
        sums_ref[...] = sums

    @pl.when(pl.program_id(0) > 0)
    def later():
        sums_ref[...] += sums


def norm_back(values, grad, gain, base, down=None, shift=None):
    tokens, width = values.shape
    block = tokens // 4
    rows = pl.BlockSpec((block, width), lambda i: (i, 0))
    line = pl.BlockSpec((1, width), lambda i: (0, 0))
    more, halves = [], []
    if down is not None:
        more = [down, shift.reshape(1, width)]
        halves = [
            pl.BlockSpec((block, width), lambda i: (jnp.minimum(i, 1), 0)),
            pl.BlockSpec((block, width), lambda i: (jnp.maximum(i - 2, 0), 0)),
        ]
    return pl.pallas_call(
        norm_back_kernel,
        grid=(4,),
        in_specs=[rows, rows, line, rows] + [rows, line][: len(more)],
        out_specs=[rows, rows, pl.BlockSpec((4, width), lambda i: (0, 0))] + halves,
        out_shape=[
            jax.ShapeDtypeStruct((tokens, width), wide),
            jax.ShapeDtypeStruct((tokens, width), low),
            jax.ShapeDtypeStruct((4, width), wide),
        ]
        + [jax.ShapeDtypeStruct((tokens // 2, width), low)] * len(halves),
        compiler_params=pltpu.CompilerParams(vmem_limit_bytes=40 * 2**20),
        cost_estimate=pl.CostEstimate(
            flops=tokens * width, bytes_accessed=tokens * width, transcendentals=0
        ),
        name="norm_back",
    )(values, grad, gain.reshape(1, width), base, *more)


def mlp_kernel(carried, plan, normed_ref, grad_ref, bias_ref, *refs):
    starts, rows, group, pieces = plan
    weights, refs = refs[:pieces], refs[pieces:]
    steps = 32 // group if pieces == 1 else pieces // 2
    if carried:
        out_before, normed_before = refs[:2]
        refs = refs[2:]
    out_ref, grad_normed_ref, *grad_refs, grad_bias_ref, ups, downs, sems = refs
    step = pl.program_id(0)
    slot = step % 2

    def copies(at):
        moves = []
        many = group if pieces == 1 else 2
        size = group // many * rows
        for place in range(many):
            block = weights[0].at[at * many + place] if pieces == 1 else weights[2 * at + place]
            for kind, target in enumerate((ups, downs)):
                moves.append(
                    pltpu.make_async_copy(
                        block.at[pl.ds(starts[kind], size)],
                        target.at[at % 2, pl.ds(place * size, size)],
                        sems.at[at % 2, 2 * place + kind],
                    )
                )
        return moves

    for at in range(steps):

        @pl.when(step + 1 == at if at else step == 0)
        def fetch():
            for move in copies(at):
                move.start()

    for at in range(steps):

        @pl.when(step == at)
        def arrive():
            for move in copies(at):
                move.wait()

    normed, grad = normed_ref[...], grad_ref[...]
    up, down = ups[slot], downs[slot]
    pre_act = product(up, normed, 1, 1) + bias_ref[...]
    square = pre_act * pre_act
    bent = jnp.tanh(gelu_scale * (pre_act + gelu_cube * square * pre_act))
    half = 0.5 * (1.0 + bent)
    active = (pre_act * half).astype(low)
    slope = half + 0.5 * pre_act * (1.0 - bent * bent) * (
        gelu_scale * (1.0 + 3.0 * gelu_cube * square)
    )
    grad_wide = product(down, grad, 1, 1) * slope
    grad_pre = grad_wide.astype(low)
    grad_bias_ref[...] = jnp.sum(grad_wide, axis=1, keepdims=True)
    grad_down = product(active, grad, 1, 0).astype(low)
    grad_up = product(grad_pre, normed, 1, 0).astype(low)

    def keep(ref):
        many = ref.shape[2]
        for place in range(ref.shape[0]):
            ref[place, 0] = grad_up[place * many : (place + 1) * many]
            ref[place, 1] = grad_down[place * many : (place + 1) * many]

    keep(grad_refs[0])
    out_term = product(active, down, 0, 0)
    normed_term = product(grad_pre, up, 0, 0)

    @pl.when(step == 0)
    def first():
        if carried:
            out_ref[...] = out_before[...] + out_term
            grad_normed_ref[...] = normed_before[...] + normed_term
        else:
            out_ref[...] = out_term
            grad_normed_ref[...] = normed_term

    @pl.when(step > 0)
    def later():
        out_ref[...] += out_term
        grad_normed_ref[...] += normed_term


def mlp(normed, grad, bias, weights, starts, rows, group=8, before=None):
    tokens, width = normed.shape
    steps = 32 // group if len(weights) == 1 else len(weights) // 2
    blocks = 32 if len(weights) == 1 else 4 * len(weights)
    whole = pl.BlockSpec((tokens, width), lambda i: (0, 0))
    column = pl.BlockSpec((group * rows, 1), lambda i: (i, 0))
    if len(weights) == 1:
        part, many = (group, 2, rows, width), blocks
    else:
        part, many = (2, 2, 4 * rows, width), blocks // 4
    grad_specs = [pl.BlockSpec(part, lambda i: (i, 0, 0, 0))]
    grad_shapes = [jax.ShapeDtypeStruct((many,) + part[1:], low)]
    earlier = [] if before is None else list(before)
    return pl.pallas_call(
        partial(mlp_kernel, before is not None, (starts, rows, group, len(weights))),
        grid=(steps,),
        in_specs=[whole, whole, column]
        + [pl.BlockSpec(memory_space=pl.ANY)] * len(weights)
        + [whole] * len(earlier),
        out_specs=[whole, whole] + grad_specs + [column],
        out_shape=[jax.ShapeDtypeStruct((tokens, width), wide)] * 2
        + grad_shapes
        + [jax.ShapeDtypeStruct((blocks * rows, 1), wide)],
        scratch_shapes=[
            pltpu.VMEM((2, group * rows, width), low),
            pltpu.VMEM((2, group * rows, width), low),
            pltpu.SemaphoreType.DMA((2, 2 * group)),
        ],
        input_output_aliases=(
            {3 + len(weights): 0, 4 + len(weights): 1} if earlier else {}
        ),
        compiler_params=pltpu.CompilerParams(vmem_limit_bytes=60 * 2**20),
        cost_estimate=pl.CostEstimate(
            flops=2 * tokens * width * blocks * rows, bytes_accessed=2**20, transcendentals=0
        ),
        name="mlp",
    )(normed, grad, bias, *weights, *earlier)


def kinds_kernel(slabs, kind_ref, grads_ref, attended_ref, normed_ref, branch_ref, *outs):
    kind = pl.program_id(0)
    held = outs[8]
    rows = held.shape[0] // slabs

    own = ((kind ^ kind_ref[0]) & 1) == 0

    def keep(terms):
        def block(spot):
            slab = spot
            if slabs == 8:
                away = (spot >> 2) * 4 + (spot & 1) * 2 + ((spot >> 1) & 1)
                slab = away ^ kind_ref[1]
            start = pl.multiple_of(slab * rows, 16)
            return held[pl.ds(start, rows), :]

        held[...] = terms
        across = (kind ^ kind_ref[0]) >> 1
        many = slabs // 4 if slabs > 1 else 1

        def put(near, near_y, far, far_x):
            for place in range(many):
                near[0, place] = block(place)
                near_y[0, place] = block(many + place)
            for place in range(2 * many):

                @pl.when(across == 0)
                def same():
                    far[place] = block(2 * many + place)

                @pl.when(across == 1)
                def other():
                    far_x[place] = block(2 * many + place)

        pl.when(own)(lambda: put(*outs[:4]))
        pl.when(jnp.logical_not(own))(lambda: put(*outs[4:8]))

    @pl.when(kind < 3)
    def projections():
        keep(product(grads_ref[0], normed_ref[...], 1, 0).astype(low))

    @pl.when(kind == 3)
    def output():
        keep(product(attended_ref[...], branch_ref[...], 1, 0).astype(low))


def kinds_grad(places, grads, attended, normed, branch, slabs):
    _, rows, tokens = grads.shape
    width = normed.shape[1]
    whole = pl.BlockSpec((tokens, width), lambda k, ref: (0, 0))
    many, each = slabs // 4, rows // slabs
    near = pl.BlockSpec((1, many, each, width), lambda k, ref: ((k ^ ref[0]) >> 1, 0, 0, 0))
    far = pl.BlockSpec((2 * many, each, width), lambda k, ref: (0, 0, 0))
    near_shape = jax.ShapeDtypeStruct((2, many, each, width), low)
    far_shape = jax.ShapeDtypeStruct((2 * many, each, width), low)
    return pl.pallas_call(
        partial(kinds_kernel, slabs),
        grid_spec=pltpu.PrefetchScalarGridSpec(
            num_scalar_prefetch=1,
            grid=(4,),
            in_specs=[
                pl.BlockSpec((1, rows, tokens), lambda k, ref: (jnp.minimum(k, 2), 0, 0)),
                pl.BlockSpec((rows, tokens), lambda k, ref: (0, 0)),
                whole,
                whole,
            ],
            out_specs=[near, near, far, far] * 2,
            scratch_shapes=[pltpu.VMEM((rows, width), low)],
        ),
        out_shape=[near_shape, near_shape, far_shape, far_shape] * 2,
        compiler_params=pltpu.CompilerParams(vmem_limit_bytes=48 * 2**20),
        cost_estimate=pl.CostEstimate(
            flops=rows * width * tokens, bytes_accessed=2**20, transcendentals=0
        ),
        name="kinds_grad",
    )(places, grads, attended, normed, branch)


def unite_kernel(kind_ref, *refs):
    outs = refs[4:]
    part = refs[0].shape[1]
    for distance in range(4):
        source = kind_ref[0] ^ distance
        for column in range(4):

            @pl.when(source == column)
            def put():
                start = 0
                for out in outs:
                    rows = out.shape[0]
                    out[:, column * part : (column + 1) * part] = refs[distance][
                        start : start + rows, :
                    ]
                    start += rows


def unite(kind, blocks, cuts):
    part = blocks[0].shape[1]
    local = pl.BlockSpec(memory_space=pltpu.VMEM)
    return pl.pallas_call(
        unite_kernel,
        in_specs=[pl.BlockSpec(memory_space=pltpu.SMEM)] + [local] * 4,
        out_specs=[local] * len(cuts),
        out_shape=[jax.ShapeDtypeStruct((rows, 4 * part), low) for rows in cuts],
        name="unite",
    )(kind, *blocks)


def divide_kernel(kind_ref, *refs):
    ins, outs = refs[:-4], refs[-4:]
    part = outs[0].shape[1]
    for distance in range(4):
        target = kind_ref[0] ^ distance
        for column in range(4):

            @pl.when(target == column)
            def put():
                start = 0
                for ref in ins:
                    rows = ref.shape[0]
                    outs[distance][start : start + rows, :] = ref[
                        :, column * part : (column + 1) * part
                    ]
                    start += rows


def divide(kind, owned):
    rows = sum(values.shape[0] for values in owned)
    part = owned[0].shape[1] // 4
    local = pl.BlockSpec(memory_space=pltpu.VMEM)
    return pl.pallas_call(
        divide_kernel,
        in_specs=[pl.BlockSpec(memory_space=pltpu.SMEM)] + [local] * len(owned),
        out_specs=[local] * 4,
        out_shape=[jax.ShapeDtypeStruct((rows, part), low)] * 4,
        name="divide",
    )(kind, *owned)


def settle_kernel(kind_ref, *refs):
    for distance in range(4):
        refs[4][kind_ref[0] ^ distance] = refs[distance][...].astype(wide)


def settle(kind, blocks):
    rows, part = blocks[0].shape
    local = pl.BlockSpec(memory_space=pltpu.VMEM)
    return pl.pallas_call(
        settle_kernel,
        in_specs=[pl.BlockSpec(memory_space=pltpu.SMEM)] + [local] * 4,
        out_specs=local,
        out_shape=jax.ShapeDtypeStruct((4, rows, part), wide),
        name="settle",
    )(kind, *blocks)


def after(values, *earlier):
    return lax.optimization_barrier((values, earlier))[0]


def add_low(*terms):
    total = terms[0].astype(wide)
    for term in terms[1:]:
        total = total + term.astype(wide)
    return total.astype(low)


def join(kinds, *blocks):
    width = blocks[0].shape[-1]
    parts = [block.reshape(kinds, -1, width) for block in blocks]
    return jnp.concatenate(parts, axis=1).reshape(-1, width)


class Hops:
    def __init__(self, dp_count, tensor_count):
        self.count = dp_count * tensor_count
        self.y, self.z = 1, (2, 4, 6)
        self.core, self.x = tensor_count, 2 * tensor_count
        self.near, self.far = (0, 2), (4, 6)

    def send(self, values, distance):
        pairs = [(place, place ^ distance) for place in range(self.count)]
        return lax.ppermute(values, everyone, pairs)

    def order(self):
        x, y = self.x, self.y
        near = [n ^ p ^ q for q in (0, y) for p in (0, x) for n in self.near]
        far = [n ^ p ^ q for q in (0, x) for p in (0, y) for n in self.far]
        return near + far

    def along_z(self, block):
        return [self.send(block, z) for z in self.z]

    def second_operands(self, kinds, block, arrived):
        z1, z2, z3 = arrived
        return join(kinds, block, z1), join(kinds, z2, z3)

    def sibling(self, *pieces):
        return [self.send(piece, self.core) for piece in pieces]

    def across_dp(self, blocks):
        return [blocks[0]] + [self.send(blocks[j], j * self.core) for j in (1, 2, 3)]


class Reduction:
    def __init__(self, hops, own, sibling, joined):
        self.hops, self.own, self.joined = hops, own, joined
        if joined:
            self.arrived = hops.send(sibling, hops.core)
        else:
            self.arrived = [hops.send(piece, hops.core) for piece in sibling]
        self.width = sibling[0].shape[-1]

    def part(self, place):
        return self.own[place], self.arrived[place]

    def halves(self, values):
        axis = 1 if self.joined else 0
        shape = (2, 2, 2, -1, self.width) if self.joined else (2, 2, -1, self.width)
        values = values.reshape(shape)
        return [lax.index_in_dim(values, place, axis, keepdims=False) for place in (0, 1)]

    def blocks(self, values):
        axis = 1 if self.joined else 0
        return [lax.index_in_dim(values, place, axis, keepdims=False) for place in (0, 1)]

    def ready_third(self):
        self.operands = add_low(*self.part(1)), add_low(*self.part(3))
        return self.operands

    def send_third(self):
        near, far = self.operands
        self.moved = self.hops.send(near, self.hops.y), self.hops.send(far, self.hops.x)

    def third(self):
        near, far = self.moved
        near, far = add_low(*self.part(0), near), add_low(*self.part(2), far)
        self.near, self.far = self.halves(near), self.halves(far)
        self.operands = self.near[1], self.far[1]
        return self.operands

    def send_second(self):
        near, far = self.operands
        self.moved = self.hops.send(near, self.hops.x), self.hops.send(far, self.hops.y)

    def second(self):
        near, far = self.moved
        near, far = add_low(self.near[0], near), add_low(self.far[0], far)
        self.near, self.far = self.blocks(near), self.blocks(far)
        self.operands = self.near[1], self.far[0], self.far[1]
        return self.operands

    def send_along_z(self):
        self.moved = [
            self.hops.send(v, z) for v, z in zip(self.operands, self.hops.z, strict=True)
        ]

    def along_z(self):
        return add_low(self.near[0], *self.moved)


def shards(
    dp_count,
    tensor_count,
    inputs,
    pad_mask,
    cotangent,
    attn_norm_gain,
    attn_norm_shift,
    w_query,
    b_query,
    w_key,
    w_value,
    b_value,
    w_out,
    b_out,
    mlp_norm_gain,
    mlp_norm_shift,
    w_up,
    b_up,
    w_down,
    b_down,
):
    half_rows, width = inputs.shape[1:]
    tokens = 2 * half_rows
    head_cols = w_query.shape[1]
    unit_cols = w_up.shape[1]
    quantum = 8 * dp_count
    slab_units = -(-unit_cols // quantum) * quantum
    by_hops = (dp_count, tensor_count) == (4, 8)
    dp_place, tensor_place = lax.axis_index("dp"), lax.axis_index("tensor")
    devices = dp_count * tensor_count
    here = (dp_place * tensor_count + tensor_place).astype(jnp.int32)
    col_start = tensor_place * head_cols
    side = tensor_place % 2
    pairs = [(place, place ^ 1) for place in range(tensor_count)]
    hops = Hops(dp_count, tensor_count)
    places = jnp.stack([dp_place, tensor_place]).astype(jnp.int32)
    places = places if by_hops else places * 0
    kind = places[:1]
    heads = head_cols * tensor_count // HEAD_DIM

    def swap(values):
        return lax.ppermute(values, "tensor", pairs)

    def one_slot(values, *earlier):
        kept = lax.dynamic_index_in_dim(values, side, 0, keepdims=False)
        sent = lax.dynamic_index_in_dim(values, 1 - side, 0, keepdims=False)
        if earlier:
            sent = after(sent, *earlier)
        return jnp.concatenate([kept, swap(sent)], axis=0)

    def both_micros(kept, other):
        return jnp.where(side == 0, jnp.stack([kept, other]), jnp.stack([other, kept]))

    unit_pad = ((0, slab_units - unit_cols), (0, 0))
    up_cols, down_cols = jnp.pad(w_up.T, unit_pad), jnp.pad(w_down, unit_pad)
    attn_cols = jnp.concatenate([w_query.T, w_key.T, w_value.T, w_out], axis=0)
    if by_hops:
        unit_cuts = (48, slab_units // 4 - 48)
        first_units = 4 * unit_cuts[0]
        share = lambda values, low_end, high_end: values[low_end:high_end].reshape(
            4, -1, values.shape[1]
        )
        mlp_cols = jnp.concatenate(
            [
                share(up_cols, 0, first_units),
                share(down_cols, 0, first_units),
                share(up_cols, first_units, slab_units),
                share(down_cols, first_units, slab_units),
            ],
            axis=1,
        )
        attn_cols = attn_cols.reshape(4, head_cols, -1)
        pick = lambda values, j: lax.dynamic_index_in_dim(
            values, dp_place ^ j, 0, keepdims=False
        )
        attn_blocks = hops.across_dp([pick(attn_cols, j) for j in range(4)])
        (attn_block,) = unite(kind, attn_blocks, (head_cols,))
        mlp_blocks = hops.across_dp([pick(mlp_cols, j) for j in range(4)])
        bulk_block, hop_block = unite(kind, mlp_blocks, [2 * rows for rows in unit_cuts])
        attn_rows = lax.all_gather(attn_block, everyone).reshape(4, -1, width)
        x_slot = one_slot(inputs)
        grad_out = one_slot(cotangent, x_slot)
        bulk_weights = lax.all_gather(bulk_block, everyone)
        hop_z = hops.along_z(hop_block)
        order = hops.order()
        order = [place ^ hops.core for place in order] + order
        unit_places = here ^ jnp.array(order)
        unit_here = (unit_places[:, None] == jnp.arange(devices)[None, :]).astype(wide)
        shuffled = partial(jnp.dot, precision=lax.Precision.HIGHEST)
    else:
        x_slot, grad_out = one_slot(inputs), one_slot(cotangent)
        unit_cuts = (slab_units // dp_count,)

        def gathered(values):
            owned = lax.all_to_all(
                values.reshape(dp_count, -1, values.shape[1]), "dp", 0, 2, tiled=True
            )
            return lax.all_gather(owned[0], everyone, axis=0, tiled=True)

        attn_rows = gathered(attn_cols)
        attn_rows = attn_rows.reshape(4, dp_count // 4, tensor_count, -1, width)
        attn_rows = attn_rows.transpose(0, 2, 1, 3, 4).reshape(4, -1, width)
        columns = [values.reshape(dp_count, -1, values.shape[1]) for values in (up_cols, down_cols)]
        unit_weights = gathered(jnp.concatenate(columns, axis=1).reshape(2 * slab_units, -1))
        unit_weights = unit_weights.reshape(32, devices // 32, 2, -1, width)
        bulk_weights = unit_weights.transpose(0, 2, 1, 3, 4).reshape(32, -1, width)

    slab_bias = jnp.pad(
        b_up.reshape(tensor_count, unit_cols), ((0, 0), (0, slab_units - unit_cols))
    )
    unit_starts = [dp_count * sum(unit_cuts[:i]) for i in range(len(unit_cuts) + 1)]

    def unit_bias(part):
        values = slab_bias[:, unit_starts[part] : unit_starts[part + 1]]
        values = values.reshape(tensor_count, dp_count, -1).transpose(1, 0, 2)
        if part == 1:
            values = shuffled(unit_here, values.reshape(devices, -1))
        return values.reshape(-1, 1)

    def unit_grads(values):
        slabs = []
        for place, part in enumerate(values):
            if place == 1:
                part = shuffled(unit_here.T, part.reshape(devices, -1))
            part = part.reshape(dp_count, tensor_count, -1).transpose(1, 0, 2)
            slabs.append(part.reshape(tensor_count, -1))
        return jnp.concatenate(slabs, axis=1)

    mask_row = lax.dynamic_slice(pad_mask, (side, tensor_place // 2, 0), (1, 1, tokens))
    mask_row = mask_row.reshape(2, half_rows)
    mask_row = jnp.where(side == 0, mask_row, mask_row[::-1]).reshape(tokens, 1)
    bias_col = jnp.where(mask_row > 0, 0.0, masked_score).astype(wide)

    normed_first = norm_forward(x_slot.astype(wide), attn_norm_gain, attn_norm_shift)
    qkv_rows, out_rows = attn_rows[:3].reshape(-1, width), attn_rows[3]
    qkv_bias = jnp.concatenate([b_query, jnp.zeros_like(b_query), b_value])
    projected = (product(qkv_rows, normed_first, 1, 1) + qkv_bias[:, None]).astype(low)
    if by_hops:
        hop_z = after(hop_z, grad_out, normed_first)
    if by_hops:
        hop_near, hop_far = hops.second_operands(2, hop_block, hop_z)
        near_x, far_y = hops.send(hop_near, hops.x), hops.send(hop_far, hops.y)
        near_x, far_y = after((near_x, far_y))
        hop_near, hop_far = join(2, hop_near, near_x), join(2, hop_far, far_y)
        attended, totals = attend(projected, bias_col, heads, 4)
        near_y, far_x = hops.send(hop_near, hops.y), hops.send(hop_far, hops.x)
        near_y, far_x = after((near_y, far_x), attended)
        hop_three = [hop_near, near_y, hop_far, far_x]
        hop_sibling = hops.sibling(*hop_three)
    else:
        attended, totals = attend(projected, bias_col, heads, 4)
    branch = product(attended, out_rows, 0, 0) + b_out
    middle = x_slot.astype(wide) + branch
    normed_second = norm_forward(middle, mlp_norm_gain, mlp_norm_shift)
    rows = unit_cuts[0] * devices // 32
    sums, up_sums = None, []
    if by_hops:
        hop_bias = jnp.split(unit_bias(1), 2)
        hop_rows = unit_cuts[1]
        hop_mlp = partial(mlp, normed_second, grad_out)
        *sums, grad_sibling, sibling_sum = hop_mlp(
            hop_bias[0], hop_sibling, (0, 4 * hop_rows), hop_rows
        )
        units = Reduction(hops, None, grad_sibling, True)
        *sums, units.own, own_sum = hop_mlp(
            hop_bias[1], hop_three, (0, 4 * hop_rows), hop_rows, 8, sums
        )
        up_sums.append(jnp.concatenate([sibling_sum[:, 0], own_sum[:, 0]]))
        units.arrived = after(units.arrived, sums)
    bulk = partial(
        mlp,
        normed_second,
        grad_out,
        unit_bias(0),
        [bulk_weights],
        (0, rows),
        rows,
        16 if by_hops else 4,
    )
    if by_hops:
        sums = after(sums, units.ready_third())
        units.send_third()
        *sums, bulk_grads, up_sum = bulk(sums)
        units.moved = after(units.moved, sums)
    else:
        *sums, bulk_grads, up_sum = bulk()
    up_sums = [up_sum[:, 0]] + up_sums
    bulk_grads = bulk_grads.reshape(32, 2, devices // 32, -1, width).transpose(0, 2, 1, 3, 4)
    bulk_owned = lax.psum_scatter(
        bulk_grads.reshape(2 * 32 * rows, width), everyone, scatter_dimension=0, tiled=True
    )
    down_out, grad_normed_second = sums
    if by_hops:
        units_third = units.third()
        grad_normed_second = after(grad_normed_second, units_third)
    grad_middle, grad_branch, second_sums, out_kept, out_sent = norm_back(
        middle, grad_normed_second, mlp_norm_gain, grad_out, down_out, b_down
    )
    back = partial(
        attend_back, projected, bias_col, attended, totals, attn_rows.reshape(-1, width)
    )
    if by_hops:
        units.send_second()
        out_other = swap(out_sent)
        grads = back(grad_branch, heads, 4)
        units.moved, out_other = after((units.moved, out_other), grads)
        grads = after(grads, units.second())
        layer_out = both_micros(out_kept, out_other)
        units.send_along_z()
        kind_grads = kinds_grad(
            places, grads, attended, normed_first, grad_branch, tensor_count
        )
        attns = Reduction(hops, kind_grads[:4], kind_grads[4:], False)
        grads = after(grads, kind_grads)
        first_terms = product(grads.reshape(-1, tokens), qkv_rows, 0, 0)
        units.moved = after(units.moved, first_terms)
        first_terms = after(first_terms, attns.ready_third())
        attns.send_third()
        input_full, input_low, first_sums = norm_back(
            x_slot, first_terms, attn_norm_gain, grad_middle
        )
        units_owned = units.along_z()
        attns.moved = after(attns.moved, units_owned)
        attns_third = attns.third()
    else:
        grads = back(grad_branch, heads, 4)
        first_terms = product(grads.reshape(-1, tokens), qkv_rows, 0, 0)
        input_full, input_low, first_sums = norm_back(
            x_slot, first_terms, attn_norm_gain, grad_middle
        )
        out_other = swap(out_sent)
        layer_out = both_micros(out_kept, out_other)

    grads, second_sums, up_sums = after((grads, second_sums, up_sums), input_low)
    total_over = lambda i: jnp.sum(grads[i], axis=1, dtype=wide)
    small = jnp.concatenate(
        [
            second_sums.reshape(-1),
            first_sums[:2].reshape(-1),
            total_over(0),
            total_over(2),
            unit_grads(up_sums).reshape(-1),
        ]
    )
    if by_hops:
        small, mlp_owned = after(
            (small.reshape(-1, 128), [bulk_owned, units_owned[0], units_owned[1]]), attns_third
        )
        attns.send_second()
        small = small + sum(hops.send(small, z) for z in hops.z)
        mlp_parts = divide(kind, mlp_owned)
        attns.moved = after(attns.moved, small, mlp_parts)
        attns_second = attns.second()
        attns.send_along_z()
        small, input_low, mlp_parts = after((small, input_low, mlp_parts), attns_second)
        input_other = swap(input_low[half_rows:])
        mlp_blocks = hops.across_dp(mlp_parts)
        mlp_back = settle(kind, mlp_blocks)
        attns.moved = after(attns.moved, mlp_back, input_other)
        small = after(small, attns.moved)
        small = small + hops.send(small, hops.y)
        small = small + sum(hops.send(small, j * hops.core) for j in (1, 2, 3))
        attn_parts = divide(kind, [attns.along_z()])
        attn_back = settle(kind, hops.across_dp(attn_parts))
        small = small.reshape(-1)
    else:
        small = lax.psum(small, everyone)
        input_other = swap(input_low[half_rows:])
    input_grad = both_micros(input_full[:half_rows], input_other.astype(wide))

    if by_hops:
        bounds = [0]
        for rows in (unit_cuts[0], unit_cuts[0], unit_cuts[1], unit_cuts[1]):
            bounds.append(bounds[-1] + rows)
        parts = [
            mlp_back[:, bounds[i] : bounds[i + 1]].reshape(-1, mlp_back.shape[2])
            for i in range(4)
        ]
        grad_w_up = jnp.concatenate([parts[0], parts[2]], axis=0)
        grad_w_down = jnp.concatenate([parts[1], parts[3]], axis=0)
    else:

        def to_columns(owned):
            back = lax.all_to_all(owned[None], "dp", 2, 0, tiled=True)
            return back.reshape(-1, width // dp_count).astype(wide)

        columns = to_columns(bulk_owned)
        columns = columns.reshape(dp_count, 2, -1, columns.shape[1])
        grad_w_up = columns[:, 0].reshape(-1, columns.shape[3])
        grad_w_down = columns[:, 1].reshape(-1, columns.shape[3])
        flat = grads.reshape(-1, tokens)
        terms = [product(flat, normed_first, 1, 0), product(attended, grad_branch, 1, 0)]
        terms = jnp.concatenate(terms, axis=0).astype(low)
        terms = terms.reshape(4, tensor_count, dp_count // 4, -1, width)
        terms = terms.transpose(0, 2, 1, 3, 4).reshape(-1, width)
        owned = lax.psum_scatter(terms, everyone, scatter_dimension=0, tiled=True)
        attn_back = to_columns(owned).reshape(4, head_cols, -1)

    part = lambda i: small[i * width : (i + 1) * width]
    up_all = small[8 * width :].reshape(tensor_count, slab_units)
    return (
        layer_out,
        input_grad,
        part(4),
        part(5),
        attn_back[0].T,
        lax.dynamic_slice_in_dim(part(6), col_start, head_cols),
        attn_back[1].T,
        attn_back[2].T,
        lax.dynamic_slice_in_dim(part(7), col_start, head_cols),
        attn_back[3],
        part(2),
        part(0),
        part(1),
        grad_w_up[:unit_cols].T,
        up_all[:, :unit_cols].reshape(-1),
        grad_w_down[:unit_cols],
        part(3),
    )


def solution(mesh):
    tokens = P(None, ("dp", "tensor"), None)
    columns = P("dp", "tensor")
    rows = P("tensor", "dp")
    return jax.shard_map(
        partial(shards, mesh.shape["dp"], mesh.shape["tensor"]),
        mesh=mesh,
        in_specs=(
            tokens,
            P(None, "dp", None),
            tokens,
            P(),
            P(),
            columns,
            P(),
            columns,
            columns,
            P(),
            rows,
            P(),
            P(),
            P(),
            columns,
            P(),
            rows,
            P(),
        ),
        out_specs=(
            tokens,
            tokens,
            P(),
            P(),
            columns,
            P("tensor"),
            columns,
            columns,
            P("tensor"),
            rows,
            P(),
            P(),
            P(),
            columns,
            P(),
            rows,
            P(),
        ),
        check_vma=False,
    )
```

```python
from functools import partial

import jax
import jax.numpy as jnp
from jax import lax
from jax.experimental import pallas as pl
from jax.experimental.pallas import tpu as pltpu
from jax.sharding import PartitionSpec as P

HEAD_DIM = 72
norm_eps = 1e-06
masked_score = -1000000000.0
low = jnp.bfloat16
wide = jnp.float32
score_scale = HEAD_DIM**-0.5
log2_e = 1.4426950408889634
gelu_scale = 0.7978845608028654
gelu_cube = 0.044715
everyone = ("dp", "tensor")


def product(left, right, left_dim, right_dim):
    return lax.dot_general(
        left, right, (((left_dim,), (right_dim,)), ((), ())), preferred_element_type=wide
    )


def attend_kernel(heads, query_ref, key_ref, value_ref, bias_ref, out_ref, total_ref):
    for head in range(heads):
        rows = slice(head * HEAD_DIM, (head + 1) * HEAD_DIM)
        scores = product(key_ref[rows, :], query_ref[rows, :], 0, 0) * (score_scale * log2_e)
        scores = scores + bias_ref[...]
        top = jnp.max(scores, axis=0, keepdims=True)
        weights = jnp.exp2(scores - top)
        total = jnp.sum(weights, axis=0, keepdims=True)
        mixed = product(value_ref[rows, :], weights.astype(low), 1, 0)
        out_ref[rows, :] = (mixed * (1.0 / total)).astype(low)
        total_ref[head] = top + jnp.log2(total)


def attend_back_kernel(
    heads,
    query_ref,
    key_ref,
    value_ref,
    bias_ref,
    out_ref,
    total_ref,
    weights_ref,
    branch_ref,
    grads_ref,
):
    grad_rows = product(weights_ref[...], branch_ref[...], 1, 1).astype(low)
    for head in range(heads):
        rows = slice(head * HEAD_DIM, (head + 1) * HEAD_DIM)
        query, key, value, grad = (
            query_ref[rows, :],
            key_ref[rows, :],
            value_ref[rows, :],
            grad_rows[rows, :],
        )
        scores = product(key, query, 0, 0) * (score_scale * log2_e) + bias_ref[...]
        probs = jnp.exp2(scores - total_ref[head])
        grad_probs = product(value, grad, 0, 0)
        along = jnp.sum(
            grad.astype(wide) * out_ref[rows, :].astype(wide), axis=0, keepdims=True
        )
        grad_raw = (probs * (grad_probs - along)).astype(low)
        grads_ref[2, rows, :] = product(grad, probs.astype(low), 1, 1).astype(low)
        grads_ref[0, rows, :] = (product(key, grad_raw, 1, 0) * score_scale).astype(low)
        grads_ref[1, rows, :] = (product(query, grad_raw, 1, 1) * score_scale).astype(low)


def attend(projected, bias, heads, step_heads):
    tokens = projected.shape[1]
    steps = heads // step_heads
    part = lambda place: pl.BlockSpec(
        (HEAD_DIM * step_heads, tokens), lambda i, place=place: (place * steps + i, 0)
    )
    return pl.pallas_call(
        partial(attend_kernel, step_heads),
        grid=(steps,),
        in_specs=[part(0), part(1), part(2), pl.BlockSpec((tokens, 1), lambda i: (0, 0))],
        out_specs=[part(0), pl.BlockSpec((step_heads, 1, tokens), lambda i: (i, 0, 0))],
        out_shape=[
            jax.ShapeDtypeStruct((heads * HEAD_DIM, tokens), low),
            jax.ShapeDtypeStruct((heads, 1, tokens), wide),
        ],
        compiler_params=pltpu.CompilerParams(vmem_limit_bytes=48 * 2**20),
        cost_estimate=pl.CostEstimate(
            flops=heads * tokens * tokens * 128, bytes_accessed=2**20, transcendentals=0
        ),
        name="attend",
    )(projected, projected, projected, bias)


def attend_back(projected, bias, attended, total, weights, branch, heads, step_heads):
    tokens = projected.shape[1]
    steps = heads // step_heads
    part = lambda place: pl.BlockSpec(
        (HEAD_DIM * step_heads, tokens), lambda i, place=place: (place * steps + i, 0)
    )
    return pl.pallas_call(
        partial(attend_back_kernel, step_heads),
        grid=(steps,),
        in_specs=[
            part(0),
            part(1),
            part(2),
            pl.BlockSpec((tokens, 1), lambda i: (0, 0)),
            part(0),
            pl.BlockSpec((step_heads, 1, tokens), lambda i: (i, 0, 0)),
            pl.BlockSpec((HEAD_DIM * step_heads, branch.shape[1]), lambda i: (3 * steps + i, 0)),
            pl.BlockSpec(branch.shape, lambda i: (0, 0)),
        ],
        out_specs=pl.BlockSpec((3, HEAD_DIM * step_heads, tokens), lambda i: (0, i, 0)),
        out_shape=jax.ShapeDtypeStruct((3, heads * HEAD_DIM, tokens), low),
        compiler_params=pltpu.CompilerParams(vmem_limit_bytes=48 * 2**20),
        cost_estimate=pl.CostEstimate(
            flops=heads * tokens * tokens * 128, bytes_accessed=2**20, transcendentals=0
        ),
        name="attend_back",
    )(projected, projected, projected, bias, attended, total, weights, branch)


def norm_forward(values, gain, shift):
    row_mean = jnp.mean(values, axis=-1, keepdims=True)
    centred = values - row_mean
    inv_scale = lax.rsqrt(jnp.mean(centred * centred, axis=-1, keepdims=True) + norm_eps)
    return (centred * inv_scale * gain + shift).astype(low)


def norm_back_kernel(values_ref, grad_ref, gain_ref, base_ref, *refs):
    if len(refs) > 3:
        down_ref, shift_ref, full_ref, low_ref, sums_ref, kept_ref, sent_ref = refs
        total = (values_ref[...] + (down_ref[...] + shift_ref[...])).astype(low)
        early = pl.program_id(0) < 2

        @pl.when(early)
        def keep():
            kept_ref[...] = total

        @pl.when(jnp.logical_not(early))
        def give():
            sent_ref[...] = total

    else:
        full_ref, low_ref, sums_ref = refs
    values = values_ref[...].astype(wide)
    centred = values - jnp.mean(values, axis=-1, keepdims=True)
    inv_scale = lax.rsqrt(jnp.mean(centred * centred, axis=-1, keepdims=True) + norm_eps)
    unit = centred * inv_scale
    grad = grad_ref[...]
    scaled = grad * gain_ref[...]
    mean_grad = jnp.mean(scaled, axis=-1, keepdims=True)
    mean_along = jnp.mean(scaled * unit, axis=-1, keepdims=True)
    base = base_ref[...].astype(wide)
    full = base + inv_scale * (scaled - mean_grad - unit * mean_along)
    rounded = full.astype(low)
    full_ref[...] = full
    low_ref[...] = rounded
    total = lambda rows: jnp.sum(rows, axis=0, keepdims=True)
    sums = jnp.concatenate(
        [total(grad * unit), total(grad), total(rounded.astype(wide)), total(base)], axis=0
    )

    @pl.when(pl.program_id(0) == 0)
    def first():
        sums_ref[...] = sums

    @pl.when(pl.program_id(0) > 0)
    def later():
        sums_ref[...] += sums


def norm_back(values, grad, gain, base, down=None, shift=None):
    tokens, width = values.shape
    block = tokens // 4
    rows = pl.BlockSpec((block, width), lambda i: (i, 0))
    line = pl.BlockSpec((1, width), lambda i: (0, 0))
    more, halves = [], []
    if down is not None:
        more = [down, shift.reshape(1, width)]
        halves = [
            pl.BlockSpec((block, width), lambda i: (jnp.minimum(i, 1), 0)),
            pl.BlockSpec((block, width), lambda i: (jnp.maximum(i - 2, 0), 0)),
        ]
    return pl.pallas_call(
        norm_back_kernel,
        grid=(4,),
        in_specs=[rows, rows, line, rows] + [rows, line][: len(more)],
        out_specs=[rows, rows, pl.BlockSpec((4, width), lambda i: (0, 0))] + halves,
        out_shape=[
            jax.ShapeDtypeStruct((tokens, width), wide),
            jax.ShapeDtypeStruct((tokens, width), low),
            jax.ShapeDtypeStruct((4, width), wide),
        ]
        + [jax.ShapeDtypeStruct((tokens // 2, width), low)] * len(halves),
        compiler_params=pltpu.CompilerParams(vmem_limit_bytes=40 * 2**20),
        cost_estimate=pl.CostEstimate(
            flops=tokens * width, bytes_accessed=tokens * width, transcendentals=0
        ),
        name="norm_back",
    )(values, grad, gain.reshape(1, width), base, *more)


def mlp_kernel(carried, plan, normed_ref, grad_ref, bias_ref, *refs):
    starts, rows, group, pieces = plan
    weights, refs = refs[:pieces], refs[pieces:]
    steps = 32 // group if pieces == 1 else pieces // 2
    if carried:
        out_before, normed_before = refs[:2]
        refs = refs[2:]
    out_ref, grad_normed_ref, *grad_refs, grad_bias_ref, ups, downs, sems = refs
    step = pl.program_id(0)
    slot = step % 2

    def copies(at):
        moves = []
        many = group if pieces == 1 else 2
        size = group // many * rows
        for place in range(many):
            block = weights[0].at[at * many + place] if pieces == 1 else weights[2 * at + place]
            for kind, target in enumerate((ups, downs)):
                moves.append(
                    pltpu.make_async_copy(
                        block.at[pl.ds(starts[kind], size)],
                        target.at[at % 2, pl.ds(place * size, size)],
                        sems.at[at % 2, 2 * place + kind],
                    )
                )
        return moves

    for at in range(steps):

        @pl.when(step + 1 == at if at else step == 0)
        def fetch():
            for move in copies(at):
                move.start()

    for at in range(steps):

        @pl.when(step == at)
        def arrive():
            for move in copies(at):
                move.wait()

    normed, grad = normed_ref[...], grad_ref[...]
    up, down = ups[slot], downs[slot]
    pre_act = product(up, normed, 1, 1) + bias_ref[...]
    square = pre_act * pre_act
    bent = jnp.tanh(gelu_scale * (pre_act + gelu_cube * square * pre_act))
    half = 0.5 * (1.0 + bent)
    active = (pre_act * half).astype(low)
    slope = half + 0.5 * pre_act * (1.0 - bent * bent) * (
        gelu_scale * (1.0 + 3.0 * gelu_cube * square)
    )
    grad_wide = product(down, grad, 1, 1) * slope
    grad_pre = grad_wide.astype(low)
    grad_bias_ref[...] = jnp.sum(grad_wide, axis=1, keepdims=True)
    grad_down = product(active, grad, 1, 0).astype(low)
    grad_up = product(grad_pre, normed, 1, 0).astype(low)

    def keep(ref):
        many = ref.shape[2]
        for place in range(ref.shape[0]):
            ref[place, 0] = grad_up[place * many : (place + 1) * many]
            ref[place, 1] = grad_down[place * many : (place + 1) * many]

    keep(grad_refs[0])
    out_term = product(active, down, 0, 0)
    normed_term = product(grad_pre, up, 0, 0)

    @pl.when(step == 0)
    def first():
        if carried:
            out_ref[...] = out_before[...] + out_term
            grad_normed_ref[...] = normed_before[...] + normed_term
        else:
            out_ref[...] = out_term
            grad_normed_ref[...] = normed_term

    @pl.when(step > 0)
    def later():
        out_ref[...] += out_term
        grad_normed_ref[...] += normed_term


def mlp(normed, grad, bias, weights, starts, rows, group=8, before=None):
    tokens, width = normed.shape
    steps = 32 // group if len(weights) == 1 else len(weights) // 2
    blocks = 32 if len(weights) == 1 else 4 * len(weights)
    whole = pl.BlockSpec((tokens, width), lambda i: (0, 0))
    column = pl.BlockSpec((group * rows, 1), lambda i: (i, 0))
    if len(weights) == 1:
        part, many = (group, 2, rows, width), blocks
    else:
        part, many = (2, 2, 4 * rows, width), blocks // 4
    grad_specs = [pl.BlockSpec(part, lambda i: (i, 0, 0, 0))]
    grad_shapes = [jax.ShapeDtypeStruct((many,) + part[1:], low)]
    earlier = [] if before is None else list(before)
    return pl.pallas_call(
        partial(mlp_kernel, before is not None, (starts, rows, group, len(weights))),
        grid=(steps,),
        in_specs=[whole, whole, column]
        + [pl.BlockSpec(memory_space=pl.ANY)] * len(weights)
        + [whole] * len(earlier),
        out_specs=[whole, whole] + grad_specs + [column],
        out_shape=[jax.ShapeDtypeStruct((tokens, width), wide)] * 2
        + grad_shapes
        + [jax.ShapeDtypeStruct((blocks * rows, 1), wide)],
        scratch_shapes=[
            pltpu.VMEM((2, group * rows, width), low),
            pltpu.VMEM((2, group * rows, width), low),
            pltpu.SemaphoreType.DMA((2, 2 * group)),
        ],
        input_output_aliases=(
            {3 + len(weights): 0, 4 + len(weights): 1} if earlier else {}
        ),
        compiler_params=pltpu.CompilerParams(vmem_limit_bytes=60 * 2**20),
        cost_estimate=pl.CostEstimate(
            flops=2 * tokens * width * blocks * rows, bytes_accessed=2**20, transcendentals=0
        ),
        name="mlp",
    )(normed, grad, bias, *weights, *earlier)


def kinds_kernel(slabs, kind_ref, grads_ref, attended_ref, normed_ref, branch_ref, *outs):
    kind = pl.program_id(0)
    held = outs[8]
    rows = held.shape[0] // slabs

    own = ((kind ^ kind_ref[0]) & 1) == 0

    def keep(terms):
        def block(spot):
            slab = spot
            if slabs == 8:
                away = (spot >> 2) * 4 + (spot & 1) * 2 + ((spot >> 1) & 1)
                slab = away ^ kind_ref[1]
            start = pl.multiple_of(slab * rows, 16)
            return held[pl.ds(start, rows), :]

        held[...] = terms
        across = (kind ^ kind_ref[0]) >> 1
        many = slabs // 4 if slabs > 1 else 1

        def put(near, near_y, far, far_x):
            for place in range(many):
                near[0, place] = block(place)
                near_y[0, place] = block(many + place)
            for place in range(2 * many):

                @pl.when(across == 0)
                def same():
                    far[place] = block(2 * many + place)

                @pl.when(across == 1)
                def other():
                    far_x[place] = block(2 * many + place)

        pl.when(own)(lambda: put(*outs[:4]))
        pl.when(jnp.logical_not(own))(lambda: put(*outs[4:8]))

    @pl.when(kind < 3)
    def projections():
        keep(product(grads_ref[0], normed_ref[...], 1, 0).astype(low))

    @pl.when(kind == 3)
    def output():
        keep(product(attended_ref[...], branch_ref[...], 1, 0).astype(low))


def kinds_grad(places, grads, attended, normed, branch, slabs):
    _, rows, tokens = grads.shape
    width = normed.shape[1]
    whole = pl.BlockSpec((tokens, width), lambda k, ref: (0, 0))
    many, each = slabs // 4, rows // slabs
    near = pl.BlockSpec((1, many, each, width), lambda k, ref: ((k ^ ref[0]) >> 1, 0, 0, 0))
    far = pl.BlockSpec((2 * many, each, width), lambda k, ref: (0, 0, 0))
    near_shape = jax.ShapeDtypeStruct((2, many, each, width), low)
    far_shape = jax.ShapeDtypeStruct((2 * many, each, width), low)
    return pl.pallas_call(
        partial(kinds_kernel, slabs),
        grid_spec=pltpu.PrefetchScalarGridSpec(
            num_scalar_prefetch=1,
            grid=(4,),
            in_specs=[
                pl.BlockSpec((1, rows, tokens), lambda k, ref: (jnp.minimum(k, 2), 0, 0)),
                pl.BlockSpec((rows, tokens), lambda k, ref: (0, 0)),
                whole,
                whole,
            ],
            out_specs=[near, near, far, far] * 2,
            scratch_shapes=[pltpu.VMEM((rows, width), low)],
        ),
        out_shape=[near_shape, near_shape, far_shape, far_shape] * 2,
        compiler_params=pltpu.CompilerParams(vmem_limit_bytes=48 * 2**20),
        cost_estimate=pl.CostEstimate(
            flops=rows * width * tokens, bytes_accessed=2**20, transcendentals=0
        ),
        name="kinds_grad",
    )(places, grads, attended, normed, branch)


def unite_kernel(kind_ref, *refs):
    outs = refs[4:]
    part = refs[0].shape[1]
    for distance in range(4):
        source = kind_ref[0] ^ distance
        for column in range(4):

            @pl.when(source == column)
            def put():
                start = 0
                for out in outs:
                    rows = out.shape[0]
                    out[:, column * part : (column + 1) * part] = refs[distance][
                        start : start + rows, :
                    ]
                    start += rows


def unite(kind, blocks, cuts):
    part = blocks[0].shape[1]
    local = pl.BlockSpec(memory_space=pltpu.VMEM)
    return pl.pallas_call(
        unite_kernel,
        in_specs=[pl.BlockSpec(memory_space=pltpu.SMEM)] + [local] * 4,
        out_specs=[local] * len(cuts),
        out_shape=[jax.ShapeDtypeStruct((rows, 4 * part), low) for rows in cuts],
        name="unite",
    )(kind, *blocks)


def divide_kernel(kind_ref, *refs):
    ins, outs = refs[:-4], refs[-4:]
    part = outs[0].shape[1]
    for distance in range(4):
        target = kind_ref[0] ^ distance
        for column in range(4):

            @pl.when(target == column)
            def put():
                start = 0
                for ref in ins:
                    rows = ref.shape[0]
                    outs[distance][start : start + rows, :] = ref[
                        :, column * part : (column + 1) * part
                    ]
                    start += rows


def divide(kind, owned):
    rows = sum(values.shape[0] for values in owned)
    part = owned[0].shape[1] // 4
    local = pl.BlockSpec(memory_space=pltpu.VMEM)
    return pl.pallas_call(
        divide_kernel,
        in_specs=[pl.BlockSpec(memory_space=pltpu.SMEM)] + [local] * len(owned),
        out_specs=[local] * 4,
        out_shape=[jax.ShapeDtypeStruct((rows, part), low)] * 4,
        name="divide",
    )(kind, *owned)


def settle_kernel(kind_ref, *refs):
    for distance in range(4):
        refs[4][kind_ref[0] ^ distance] = refs[distance][...].astype(wide)


def settle(kind, blocks):
    rows, part = blocks[0].shape
    local = pl.BlockSpec(memory_space=pltpu.VMEM)
    return pl.pallas_call(
        settle_kernel,
        in_specs=[pl.BlockSpec(memory_space=pltpu.SMEM)] + [local] * 4,
        out_specs=local,
        out_shape=jax.ShapeDtypeStruct((4, rows, part), wide),
        name="settle",
    )(kind, *blocks)


def after(values, *earlier):
    return lax.optimization_barrier((values, earlier))[0]


def add_low(*terms):
    total = terms[0].astype(wide)
    for term in terms[1:]:
        total = total + term.astype(wide)
    return total.astype(low)


def join(kinds, *blocks):
    width = blocks[0].shape[-1]
    parts = [block.reshape(kinds, -1, width) for block in blocks]
    return jnp.concatenate(parts, axis=1).reshape(-1, width)


class Hops:
    def __init__(self, dp_count, tensor_count):
        self.count = dp_count * tensor_count
        self.y, self.z = 1, (2, 4, 6)
        self.core, self.x = tensor_count, 2 * tensor_count
        self.near, self.far = (0, 2), (4, 6)

    def send(self, values, distance):
        pairs = [(place, place ^ distance) for place in range(self.count)]
        return lax.ppermute(values, everyone, pairs)

    def order(self):
        x, y = self.x, self.y
        near = [n ^ p ^ q for q in (0, y) for p in (0, x) for n in self.near]
        far = [n ^ p ^ q for q in (0, x) for p in (0, y) for n in self.far]
        return near + far

    def along_z(self, block):
        return [self.send(block, z) for z in self.z]

    def second_operands(self, kinds, block, arrived):
        z1, z2, z3 = arrived
        return join(kinds, block, z1), join(kinds, z2, z3)

    def sibling(self, *pieces):
        return [self.send(piece, self.core) for piece in pieces]

    def across_dp(self, blocks):
        return [blocks[0]] + [self.send(blocks[j], j * self.core) for j in (1, 2, 3)]


class Reduction:
    def __init__(self, hops, own, sibling, joined):
        self.hops, self.own, self.joined = hops, own, joined
        if joined:
            self.arrived = hops.send(sibling, hops.core)
        else:
            self.arrived = [hops.send(piece, hops.core) for piece in sibling]
        self.width = sibling[0].shape[-1]

    def part(self, place):
        return self.own[place], self.arrived[place]

    def halves(self, values):
        axis = 1 if self.joined else 0
        shape = (2, 2, 2, -1, self.width) if self.joined else (2, 2, -1, self.width)
        values = values.reshape(shape)
        return [lax.index_in_dim(values, place, axis, keepdims=False) for place in (0, 1)]

    def blocks(self, values):
        axis = 1 if self.joined else 0
        return [lax.index_in_dim(values, place, axis, keepdims=False) for place in (0, 1)]

    def ready_third(self):
        self.operands = add_low(*self.part(1)), add_low(*self.part(3))
        return self.operands

    def send_third(self):
        near, far = self.operands
        self.moved = self.hops.send(near, self.hops.y), self.hops.send(far, self.hops.x)

    def third(self):
        near, far = self.moved
        near, far = add_low(*self.part(0), near), add_low(*self.part(2), far)
        self.near, self.far = self.halves(near), self.halves(far)
        self.operands = self.near[1], self.far[1]
        return self.operands

    def send_second(self):
        near, far = self.operands
        self.moved = self.hops.send(near, self.hops.x), self.hops.send(far, self.hops.y)

    def second(self):
        near, far = self.moved
        near, far = add_low(self.near[0], near), add_low(self.far[0], far)
        self.near, self.far = self.blocks(near), self.blocks(far)
        self.operands = self.near[1], self.far[0], self.far[1]
        return self.operands

    def send_along_z(self):
        self.moved = [
            self.hops.send(v, z) for v, z in zip(self.operands, self.hops.z, strict=True)
        ]

    def along_z(self):
        return add_low(self.near[0], *self.moved)


def shards(
    dp_count,
    tensor_count,
    inputs,
    pad_mask,
    cotangent,
    attn_norm_gain,
    attn_norm_shift,
    w_query,
    b_query,
    w_key,
    w_value,
    b_value,
    w_out,
    b_out,
    mlp_norm_gain,
    mlp_norm_shift,
    w_up,
    b_up,
    w_down,
    b_down,
):
    half_rows, width = inputs.shape[1:]
    tokens = 2 * half_rows
    head_cols = w_query.shape[1]
    unit_cols = w_up.shape[1]
    quantum = 8 * dp_count
    slab_units = -(-unit_cols // quantum) * quantum
    by_hops = (dp_count, tensor_count) == (4, 8)
    dp_place, tensor_place = lax.axis_index("dp"), lax.axis_index("tensor")
    devices = dp_count * tensor_count
    here = (dp_place * tensor_count + tensor_place).astype(jnp.int32)
    col_start = tensor_place * head_cols
    side = tensor_place % 2
    pairs = [(place, place ^ 1) for place in range(tensor_count)]
    hops = Hops(dp_count, tensor_count)
    places = jnp.stack([dp_place, tensor_place]).astype(jnp.int32)
    places = places if by_hops else places * 0
    kind = places[:1]
    heads = head_cols * tensor_count // HEAD_DIM

    def swap(values):
        return lax.ppermute(values, "tensor", pairs)

    def one_slot(values, *earlier):
        kept = lax.dynamic_index_in_dim(values, side, 0, keepdims=False)
        sent = lax.dynamic_index_in_dim(values, 1 - side, 0, keepdims=False)
        if earlier:
            sent = after(sent, *earlier)
        return jnp.concatenate([kept, swap(sent)], axis=0)

    def both_micros(kept, other):
        return jnp.where(side == 0, jnp.stack([kept, other]), jnp.stack([other, kept]))

    unit_pad = ((0, slab_units - unit_cols), (0, 0))
    up_cols, down_cols = jnp.pad(w_up.T, unit_pad), jnp.pad(w_down, unit_pad)
    attn_cols = jnp.concatenate([w_query.T, w_key.T, w_value.T, w_out], axis=0)
    if by_hops:
        unit_cuts = (48, slab_units // 4 - 48)
        first_units = 4 * unit_cuts[0]
        share = lambda values, low_end, high_end: values[low_end:high_end].reshape(
            4, -1, values.shape[1]
        )
        mlp_cols = jnp.concatenate(
            [
                share(up_cols, 0, first_units),
                share(down_cols, 0, first_units),
                share(up_cols, first_units, slab_units),
                share(down_cols, first_units, slab_units),
            ],
            axis=1,
        )
        attn_cols = attn_cols.reshape(4, head_cols, -1)
        pick = lambda values, j: lax.dynamic_index_in_dim(
            values, dp_place ^ j, 0, keepdims=False
        )
        attn_blocks = hops.across_dp([pick(attn_cols, j) for j in range(4)])
        (attn_block,) = unite(kind, attn_blocks, (head_cols,))
        mlp_blocks = hops.across_dp([pick(mlp_cols, j) for j in range(4)])
        bulk_block, hop_block = unite(kind, mlp_blocks, [2 * rows for rows in unit_cuts])
        attn_rows = lax.all_gather(attn_block, everyone).reshape(4, -1, width)
        x_slot = one_slot(inputs)
        grad_out = one_slot(cotangent, x_slot)
        bulk_weights = lax.all_gather(bulk_block, everyone)
        hop_z = hops.along_z(hop_block)
        order = hops.order()
        order = [place ^ hops.core for place in order] + order
        unit_places = here ^ jnp.array(order)
        unit_here = (unit_places[:, None] == jnp.arange(devices)[None, :]).astype(wide)
        shuffled = partial(jnp.dot, precision=lax.Precision.HIGHEST)
    else:
        x_slot, grad_out = one_slot(inputs), one_slot(cotangent)
        unit_cuts = (slab_units // dp_count,)

        def gathered(values):
            owned = lax.all_to_all(
                values.reshape(dp_count, -1, values.shape[1]), "dp", 0, 2, tiled=True
            )
            return lax.all_gather(owned[0], everyone, axis=0, tiled=True)

        attn_rows = gathered(attn_cols)
        attn_rows = attn_rows.reshape(4, dp_count // 4, tensor_count, -1, width)
        attn_rows = attn_rows.transpose(0, 2, 1, 3, 4).reshape(4, -1, width)
        columns = [values.reshape(dp_count, -1, values.shape[1]) for values in (up_cols, down_cols)]
        unit_weights = gathered(jnp.concatenate(columns, axis=1).reshape(2 * slab_units, -1))
        unit_weights = unit_weights.reshape(32, devices // 32, 2, -1, width)
        bulk_weights = unit_weights.transpose(0, 2, 1, 3, 4).reshape(32, -1, width)

    slab_bias = jnp.pad(
        b_up.reshape(tensor_count, unit_cols), ((0, 0), (0, slab_units - unit_cols))
    )
    unit_starts = [dp_count * sum(unit_cuts[:i]) for i in range(len(unit_cuts) + 1)]

    def unit_bias(part):
        values = slab_bias[:, unit_starts[part] : unit_starts[part + 1]]
        values = values.reshape(tensor_count, dp_count, -1).transpose(1, 0, 2)
        if part == 1:
            values = shuffled(unit_here, values.reshape(devices, -1))
        return values.reshape(-1, 1)

    def unit_grads(values):
        slabs = []
        for place, part in enumerate(values):
            if place == 1:
                part = shuffled(unit_here.T, part.reshape(devices, -1))
            part = part.reshape(dp_count, tensor_count, -1).transpose(1, 0, 2)
            slabs.append(part.reshape(tensor_count, -1))
        return jnp.concatenate(slabs, axis=1)

    mask_row = lax.dynamic_slice(pad_mask, (side, tensor_place // 2, 0), (1, 1, tokens))
    mask_row = mask_row.reshape(2, half_rows)
    mask_row = jnp.where(side == 0, mask_row, mask_row[::-1]).reshape(tokens, 1)
    bias_col = jnp.where(mask_row > 0, 0.0, masked_score).astype(wide)

    normed_first = norm_forward(x_slot.astype(wide), attn_norm_gain, attn_norm_shift)
    qkv_rows, out_rows = attn_rows[:3].reshape(-1, width), attn_rows[3]
    qkv_bias = jnp.concatenate([b_query, jnp.zeros_like(b_query), b_value])
    projected = (product(qkv_rows, normed_first, 1, 1) + qkv_bias[:, None]).astype(low)
    if by_hops:
        hop_z = after(hop_z, grad_out, normed_first)
    if by_hops:
        hop_near, hop_far = hops.second_operands(2, hop_block, hop_z)
        near_x, far_y = hops.send(hop_near, hops.x), hops.send(hop_far, hops.y)
        near_x, far_y = after((near_x, far_y))
        hop_near, hop_far = join(2, hop_near, near_x), join(2, hop_far, far_y)
        attended, totals = attend(projected, bias_col, heads, 4)
        near_y, far_x = hops.send(hop_near, hops.y), hops.send(hop_far, hops.x)
        near_y, far_x = after((near_y, far_x), attended)
        hop_three = [hop_near, near_y, hop_far, far_x]
        hop_sibling = hops.sibling(*hop_three)
    else:
        attended, totals = attend(projected, bias_col, heads, 4)
    branch = product(attended, out_rows, 0, 0) + b_out
    middle = x_slot.astype(wide) + branch
    normed_second = norm_forward(middle, mlp_norm_gain, mlp_norm_shift)
    rows = unit_cuts[0] * devices // 32
    sums, up_sums = None, []
    if by_hops:
        hop_bias = jnp.split(unit_bias(1), 2)
        hop_rows = unit_cuts[1]
        hop_mlp = partial(mlp, normed_second, grad_out)
        *sums, grad_sibling, sibling_sum = hop_mlp(
            hop_bias[0], hop_sibling, (0, 4 * hop_rows), hop_rows
        )
        units = Reduction(hops, None, grad_sibling, True)
        *sums, units.own, own_sum = hop_mlp(
            hop_bias[1], hop_three, (0, 4 * hop_rows), hop_rows, 8, sums
        )
        up_sums.append((sibling_sum, own_sum))
        units.arrived = after(units.arrived, sums)
    bulk = partial(
        mlp,
        normed_second,
        grad_out,
        unit_bias(0),
        [bulk_weights],
        (0, rows),
        rows,
        16 if by_hops else 4,
    )
    if by_hops:
        sums = after(sums, units.ready_third())
        units.send_third()
        *sums, bulk_grads, up_sum = bulk(sums)
        units.moved = after(units.moved, sums)
    else:
        *sums, bulk_grads, up_sum = bulk()
    up_sums = [(up_sum,)] + up_sums
    bulk_grads = bulk_grads.reshape(32, 2, devices // 32, -1, width).transpose(0, 2, 1, 3, 4)
    bulk_owned = lax.psum_scatter(
        bulk_grads.reshape(2 * 32 * rows, width), everyone, scatter_dimension=0, tiled=True
    )
    down_out, grad_normed_second = sums
    if by_hops:
        units_third = units.third()
        grad_normed_second = after(grad_normed_second, units_third)
    grad_middle, grad_branch, second_sums, out_kept, out_sent = norm_back(
        middle, grad_normed_second, mlp_norm_gain, grad_out, down_out, b_down
    )
    back = partial(
        attend_back, projected, bias_col, attended, totals, attn_rows.reshape(-1, width)
    )
    if by_hops:
        units.send_second()
        out_other = swap(out_sent)
        grads = back(grad_branch, heads, 4)
        units.moved, out_other = after((units.moved, out_other), grads)
        grads = after(grads, units.second())
        layer_out = both_micros(out_kept, out_other)
        units.send_along_z()
        kind_grads = kinds_grad(
            places, grads, attended, normed_first, grad_branch, tensor_count
        )
        attns = Reduction(hops, kind_grads[:4], kind_grads[4:], False)
        grads = after(grads, kind_grads)
        first_terms = product(grads.reshape(-1, tokens), qkv_rows, 0, 0)
        units.moved = after(units.moved, first_terms)
        first_terms = after(first_terms, attns.ready_third())
        attns.send_third()
        input_full, input_low, first_sums = norm_back(
            x_slot, first_terms, attn_norm_gain, grad_middle
        )
        attns.moved = after(attns.moved, input_low)
        units.moved = after(units.moved, attns.moved)
        attns_third = attns.third()
        units_owned = units.along_z()
    else:
        grads = back(grad_branch, heads, 4)
        first_terms = product(grads.reshape(-1, tokens), qkv_rows, 0, 0)
        input_full, input_low, first_sums = norm_back(
            x_slot, first_terms, attn_norm_gain, grad_middle
        )
        out_other = swap(out_sent)
        layer_out = both_micros(out_kept, out_other)

    grads, second_sums, up_sums = after((grads, second_sums, up_sums), input_low)
    up_sums = [jnp.concatenate([part[:, 0] for part in parts]) for parts in up_sums]
    total_over = lambda i: jnp.sum(grads[i], axis=1, dtype=wide)
    small = jnp.concatenate(
        [
            second_sums.reshape(-1),
            first_sums[:2].reshape(-1),
            total_over(0),
            total_over(2),
            unit_grads(up_sums).reshape(-1),
        ]
    )
    if by_hops:
        small, mlp_owned = after(
            (small.reshape(-1, 128), [bulk_owned, units_owned[0], units_owned[1]]), attns_third
        )
        attns.send_second()
        small = small + sum(hops.send(small, z) for z in hops.z)
        mlp_parts = divide(kind, mlp_owned)
        attns.moved = after(attns.moved, small, mlp_parts)
        attns_second = attns.second()
        attns.send_along_z()
        small, input_low, mlp_parts = after((small, input_low, mlp_parts), attns_second)
        input_other = swap(input_low[half_rows:])
        mlp_blocks = hops.across_dp(mlp_parts)
        mlp_back = settle(kind, mlp_blocks)
        attns.moved = after(attns.moved, mlp_back, input_other)
        small = after(small, attns.moved)
        small = small + hops.send(small, hops.y)
        small = small + sum(hops.send(small, j * hops.core) for j in (1, 2, 3))
        attn_parts = divide(kind, [attns.along_z()])
        attn_back = settle(kind, hops.across_dp(attn_parts))
        small = small.reshape(-1)
    else:
        small = lax.psum(small, everyone)
        input_other = swap(input_low[half_rows:])
    input_grad = both_micros(input_full[:half_rows], input_other.astype(wide))

    if by_hops:
        bounds = [0]
        for rows in (unit_cuts[0], unit_cuts[0], unit_cuts[1], unit_cuts[1]):
            bounds.append(bounds[-1] + rows)
        parts = [
            mlp_back[:, bounds[i] : bounds[i + 1]].reshape(-1, mlp_back.shape[2])
            for i in range(4)
        ]
        grad_w_up = jnp.concatenate([parts[0], parts[2]], axis=0)
        grad_w_down = jnp.concatenate([parts[1], parts[3]], axis=0)
    else:

        def to_columns(owned):
            back = lax.all_to_all(owned[None], "dp", 2, 0, tiled=True)
            return back.reshape(-1, width // dp_count).astype(wide)

        columns = to_columns(bulk_owned)
        columns = columns.reshape(dp_count, 2, -1, columns.shape[1])
        grad_w_up = columns[:, 0].reshape(-1, columns.shape[3])
        grad_w_down = columns[:, 1].reshape(-1, columns.shape[3])
        flat = grads.reshape(-1, tokens)
        terms = [product(flat, normed_first, 1, 0), product(attended, grad_branch, 1, 0)]
        terms = jnp.concatenate(terms, axis=0).astype(low)
        terms = terms.reshape(4, tensor_count, dp_count // 4, -1, width)
        terms = terms.transpose(0, 2, 1, 3, 4).reshape(-1, width)
        owned = lax.psum_scatter(terms, everyone, scatter_dimension=0, tiled=True)
        attn_back = to_columns(owned).reshape(4, head_cols, -1)

    part = lambda i: small[i * width : (i + 1) * width]
    up_all = small[8 * width :].reshape(tensor_count, slab_units)
    return (
        layer_out,
        input_grad,
        part(4),
        part(5),
        attn_back[0].T,
        lax.dynamic_slice_in_dim(part(6), col_start, head_cols),
        attn_back[1].T,
        attn_back[2].T,
        lax.dynamic_slice_in_dim(part(7), col_start, head_cols),
        attn_back[3],
        part(2),
        part(0),
        part(1),
        grad_w_up[:unit_cols].T,
        up_all[:, :unit_cols].reshape(-1),
        grad_w_down[:unit_cols],
        part(3),
    )


def solution(mesh):
    tokens = P(None, ("dp", "tensor"), None)
    columns = P("dp", "tensor")
    rows = P("tensor", "dp")
    return jax.shard_map(
        partial(shards, mesh.shape["dp"], mesh.shape["tensor"]),
        mesh=mesh,
        in_specs=(
            tokens,
            P(None, "dp", None),
            tokens,
            P(),
            P(),
            columns,
            P(),
            columns,
            columns,
            P(),
            rows,
            P(),
            P(),
            P(),
            columns,
            P(),
            rows,
            P(),
        ),
        out_specs=(
            tokens,
            tokens,
            P(),
            P(),
            columns,
            P("tensor"),
            columns,
            columns,
            P("tensor"),
            rows,
            P(),
            P(),
            P(),
            columns,
            P(),
            rows,
            P(),
        ),
        check_vma=False,
    )
```

```python
from functools import partial

import jax
import jax.numpy as jnp
from jax import lax
from jax.experimental import pallas as pl
from jax.experimental.pallas import tpu as pltpu
from jax.sharding import PartitionSpec as P

HEAD_DIM = 72
norm_eps = 1e-06
masked_score = -1000000000.0
low = jnp.bfloat16
wide = jnp.float32
score_scale = HEAD_DIM**-0.5
log2_e = 1.4426950408889634
gelu_scale = 0.7978845608028654
gelu_cube = 0.044715
everyone = ("dp", "tensor")


def product(left, right, left_dim, right_dim):
    return lax.dot_general(
        left, right, (((left_dim,), (right_dim,)), ((), ())), preferred_element_type=wide
    )


def attend_kernel(heads, query_ref, key_ref, value_ref, bias_ref, out_ref, total_ref):
    for head in range(heads):
        rows = slice(head * HEAD_DIM, (head + 1) * HEAD_DIM)
        scores = product(key_ref[rows, :], query_ref[rows, :], 0, 0) * (score_scale * log2_e)
        scores = scores + bias_ref[...]
        top = jnp.max(scores, axis=0, keepdims=True)
        weights = jnp.exp2(scores - top)
        total = jnp.sum(weights, axis=0, keepdims=True)
        mixed = product(value_ref[rows, :], weights.astype(low), 1, 0)
        out_ref[rows, :] = (mixed * (1.0 / total)).astype(low)
        total_ref[head] = top + jnp.log2(total)


def attend_back_kernel(
    heads,
    query_ref,
    key_ref,
    value_ref,
    bias_ref,
    out_ref,
    total_ref,
    weights_ref,
    branch_ref,
    grads_ref,
):
    grad_rows = product(weights_ref[...], branch_ref[...], 1, 1).astype(low)
    for head in range(heads):
        rows = slice(head * HEAD_DIM, (head + 1) * HEAD_DIM)
        query, key, value, grad = (
            query_ref[rows, :],
            key_ref[rows, :],
            value_ref[rows, :],
            grad_rows[rows, :],
        )
        scores = product(key, query, 0, 0) * (score_scale * log2_e) + bias_ref[...]
        probs = jnp.exp2(scores - total_ref[head])
        grad_probs = product(value, grad, 0, 0)
        along = jnp.sum(
            grad.astype(wide) * out_ref[rows, :].astype(wide), axis=0, keepdims=True
        )
        grad_raw = (probs * (grad_probs - along)).astype(low)
        grads_ref[2, rows, :] = product(grad, probs.astype(low), 1, 1).astype(low)
        grads_ref[0, rows, :] = (product(key, grad_raw, 1, 0) * score_scale).astype(low)
        grads_ref[1, rows, :] = (product(query, grad_raw, 1, 1) * score_scale).astype(low)


def attend(projected, bias, heads, step_heads):
    tokens = projected.shape[1]
    steps = heads // step_heads
    part = lambda place: pl.BlockSpec(
        (HEAD_DIM * step_heads, tokens), lambda i, place=place: (place * steps + i, 0)
    )
    return pl.pallas_call(
        partial(attend_kernel, step_heads),
        grid=(steps,),
        in_specs=[part(0), part(1), part(2), pl.BlockSpec((tokens, 1), lambda i: (0, 0))],
        out_specs=[part(0), pl.BlockSpec((step_heads, 1, tokens), lambda i: (i, 0, 0))],
        out_shape=[
            jax.ShapeDtypeStruct((heads * HEAD_DIM, tokens), low),
            jax.ShapeDtypeStruct((heads, 1, tokens), wide),
        ],
        compiler_params=pltpu.CompilerParams(vmem_limit_bytes=48 * 2**20),
        cost_estimate=pl.CostEstimate(
            flops=heads * tokens * tokens * 128, bytes_accessed=2**20, transcendentals=0
        ),
        name="attend",
    )(projected, projected, projected, bias)


def attend_back(projected, bias, attended, total, weights, branch, heads, step_heads):
    tokens = projected.shape[1]
    steps = heads // step_heads
    part = lambda place: pl.BlockSpec(
        (HEAD_DIM * step_heads, tokens), lambda i, place=place: (place * steps + i, 0)
    )
    return pl.pallas_call(
        partial(attend_back_kernel, step_heads),
        grid=(steps,),
        in_specs=[
            part(0),
            part(1),
            part(2),
            pl.BlockSpec((tokens, 1), lambda i: (0, 0)),
            part(0),
            pl.BlockSpec((step_heads, 1, tokens), lambda i: (i, 0, 0)),
            pl.BlockSpec((HEAD_DIM * step_heads, branch.shape[1]), lambda i: (3 * steps + i, 0)),
            pl.BlockSpec(branch.shape, lambda i: (0, 0)),
        ],
        out_specs=pl.BlockSpec((3, HEAD_DIM * step_heads, tokens), lambda i: (0, i, 0)),
        out_shape=jax.ShapeDtypeStruct((3, heads * HEAD_DIM, tokens), low),
        compiler_params=pltpu.CompilerParams(vmem_limit_bytes=48 * 2**20),
        cost_estimate=pl.CostEstimate(
            flops=heads * tokens * tokens * 128, bytes_accessed=2**20, transcendentals=0
        ),
        name="attend_back",
    )(projected, projected, projected, bias, attended, total, weights, branch)


def norm_forward(values, gain, shift):
    row_mean = jnp.mean(values, axis=-1, keepdims=True)
    centred = values - row_mean
    inv_scale = lax.rsqrt(jnp.mean(centred * centred, axis=-1, keepdims=True) + norm_eps)
    return (centred * inv_scale * gain + shift).astype(low)


def norm_back_kernel(values_ref, grad_ref, gain_ref, base_ref, *refs):
    if len(refs) > 3:
        down_ref, shift_ref, full_ref, low_ref, sums_ref, kept_ref, sent_ref = refs
        total = (values_ref[...] + (down_ref[...] + shift_ref[...])).astype(low)
        early = pl.program_id(0) < 2

        @pl.when(early)
        def keep():
            kept_ref[...] = total

        @pl.when(jnp.logical_not(early))
        def give():
            sent_ref[...] = total

    else:
        full_ref, low_ref, sums_ref = refs
    values = values_ref[...].astype(wide)
    centred = values - jnp.mean(values, axis=-1, keepdims=True)
    inv_scale = lax.rsqrt(jnp.mean(centred * centred, axis=-1, keepdims=True) + norm_eps)
    unit = centred * inv_scale
    grad = grad_ref[...]
    scaled = grad * gain_ref[...]
    mean_grad = jnp.mean(scaled, axis=-1, keepdims=True)
    mean_along = jnp.mean(scaled * unit, axis=-1, keepdims=True)
    base = base_ref[...].astype(wide)
    full = base + inv_scale * (scaled - mean_grad - unit * mean_along)
    rounded = full.astype(low)
    full_ref[...] = full
    low_ref[...] = rounded
    total = lambda rows: jnp.sum(rows, axis=0, keepdims=True)
    sums = jnp.concatenate(
        [total(grad * unit), total(grad), total(rounded.astype(wide)), total(base)], axis=0
    )

    @pl.when(pl.program_id(0) == 0)
    def first():
        sums_ref[...] = sums

    @pl.when(pl.program_id(0) > 0)
    def later():
        sums_ref[...] += sums


def norm_back(values, grad, gain, base, down=None, shift=None):
    tokens, width = values.shape
    block = tokens // 4
    rows = pl.BlockSpec((block, width), lambda i: (i, 0))
    line = pl.BlockSpec((1, width), lambda i: (0, 0))
    more, halves = [], []
    if down is not None:
        more = [down, shift.reshape(1, width)]
        halves = [
            pl.BlockSpec((block, width), lambda i: (jnp.minimum(i, 1), 0)),
            pl.BlockSpec((block, width), lambda i: (jnp.maximum(i - 2, 0), 0)),
        ]
    return pl.pallas_call(
        norm_back_kernel,
        grid=(4,),
        in_specs=[rows, rows, line, rows] + [rows, line][: len(more)],
        out_specs=[rows, rows, pl.BlockSpec((4, width), lambda i: (0, 0))] + halves,
        out_shape=[
            jax.ShapeDtypeStruct((tokens, width), wide),
            jax.ShapeDtypeStruct((tokens, width), low),
            jax.ShapeDtypeStruct((4, width), wide),
        ]
        + [jax.ShapeDtypeStruct((tokens // 2, width), low)] * len(halves),
        compiler_params=pltpu.CompilerParams(vmem_limit_bytes=40 * 2**20),
        cost_estimate=pl.CostEstimate(
            flops=tokens * width, bytes_accessed=tokens * width, transcendentals=0
        ),
        name="norm_back",
    )(values, grad, gain.reshape(1, width), base, *more)


def mlp_kernel(carried, plan, normed_ref, grad_ref, bias_ref, *refs):
    starts, rows, group, pieces = plan
    weights, refs = refs[:pieces], refs[pieces:]
    steps = 32 // group if pieces == 1 else pieces // 2
    if carried:
        out_before, normed_before = refs[:2]
        refs = refs[2:]
    out_ref, grad_normed_ref, *grad_refs, grad_bias_ref, ups, downs, sems = refs
    step = pl.program_id(0)
    slot = step % 2

    def copies(at):
        moves = []
        many = group if pieces == 1 else 2
        size = group // many * rows
        for place in range(many):
            block = weights[0].at[at * many + place] if pieces == 1 else weights[2 * at + place]
            for kind, target in enumerate((ups, downs)):
                moves.append(
                    pltpu.make_async_copy(
                        block.at[pl.ds(starts[kind], size)],
                        target.at[at % 2, pl.ds(place * size, size)],
                        sems.at[at % 2, 2 * place + kind],
                    )
                )
        return moves

    for at in range(steps):

        @pl.when(step + 1 == at if at else step == 0)
        def fetch():
            for move in copies(at):
                move.start()

    for at in range(steps):

        @pl.when(step == at)
        def arrive():
            for move in copies(at):
                move.wait()

    normed, grad = normed_ref[...], grad_ref[...]
    up, down = ups[slot], downs[slot]
    pre_act = product(up, normed, 1, 1) + bias_ref[...]
    square = pre_act * pre_act
    bent = jnp.tanh(gelu_scale * (pre_act + gelu_cube * square * pre_act))
    half = 0.5 * (1.0 + bent)
    active = (pre_act * half).astype(low)
    slope = half + 0.5 * pre_act * (1.0 - bent * bent) * (
        gelu_scale * (1.0 + 3.0 * gelu_cube * square)
    )
    grad_wide = product(down, grad, 1, 1) * slope
    grad_pre = grad_wide.astype(low)
    grad_bias_ref[...] = jnp.sum(grad_wide, axis=1, keepdims=True)
    grad_down = product(active, grad, 1, 0).astype(low)
    grad_up = product(grad_pre, normed, 1, 0).astype(low)

    def keep(ref):
        many = ref.shape[2]
        for place in range(ref.shape[0]):
            ref[place, 0] = grad_up[place * many : (place + 1) * many]
            ref[place, 1] = grad_down[place * many : (place + 1) * many]

    keep(grad_refs[0])
    out_term = product(active, down, 0, 0)
    normed_term = product(grad_pre, up, 0, 0)

    @pl.when(step == 0)
    def first():
        if carried:
            out_ref[...] = out_before[...] + out_term
            grad_normed_ref[...] = normed_before[...] + normed_term
        else:
            out_ref[...] = out_term
            grad_normed_ref[...] = normed_term

    @pl.when(step > 0)
    def later():
        out_ref[...] += out_term
        grad_normed_ref[...] += normed_term


def mlp(normed, grad, bias, weights, starts, rows, group=8, before=None):
    tokens, width = normed.shape
    steps = 32 // group if len(weights) == 1 else len(weights) // 2
    blocks = 32 if len(weights) == 1 else 4 * len(weights)
    whole = pl.BlockSpec((tokens, width), lambda i: (0, 0))
    column = pl.BlockSpec((group * rows, 1), lambda i: (i, 0))
    if len(weights) == 1:
        part, many = (group, 2, rows, width), blocks
    else:
        part, many = (2, 2, 4 * rows, width), blocks // 4
    grad_specs = [pl.BlockSpec(part, lambda i: (i, 0, 0, 0))]
    grad_shapes = [jax.ShapeDtypeStruct((many,) + part[1:], low)]
    earlier = [] if before is None else list(before)
    return pl.pallas_call(
        partial(mlp_kernel, before is not None, (starts, rows, group, len(weights))),
        grid=(steps,),
        in_specs=[whole, whole, column]
        + [pl.BlockSpec(memory_space=pl.ANY)] * len(weights)
        + [whole] * len(earlier),
        out_specs=[whole, whole] + grad_specs + [column],
        out_shape=[jax.ShapeDtypeStruct((tokens, width), wide)] * 2
        + grad_shapes
        + [jax.ShapeDtypeStruct((blocks * rows, 1), wide)],
        scratch_shapes=[
            pltpu.VMEM((2, group * rows, width), low),
            pltpu.VMEM((2, group * rows, width), low),
            pltpu.SemaphoreType.DMA((2, 2 * group)),
        ],
        input_output_aliases=(
            {3 + len(weights): 0, 4 + len(weights): 1} if earlier else {}
        ),
        compiler_params=pltpu.CompilerParams(vmem_limit_bytes=60 * 2**20),
        cost_estimate=pl.CostEstimate(
            flops=2 * tokens * width * blocks * rows, bytes_accessed=2**20, transcendentals=0
        ),
        name="mlp",
    )(normed, grad, bias, *weights, *earlier)


def kinds_kernel(slabs, kind_ref, grads_ref, attended_ref, normed_ref, branch_ref, *outs):
    kind = pl.program_id(0)
    held = outs[8]
    rows = held.shape[0] // slabs

    own = ((kind ^ kind_ref[0]) & 1) == 0

    def keep(terms):
        def block(spot):
            slab = spot
            if slabs == 8:
                away = (spot >> 2) * 4 + (spot & 1) * 2 + ((spot >> 1) & 1)
                slab = away ^ kind_ref[1]
            start = pl.multiple_of(slab * rows, 16)
            return held[pl.ds(start, rows), :]

        held[...] = terms
        across = (kind ^ kind_ref[0]) >> 1
        many = slabs // 4 if slabs > 1 else 1

        def put(near, near_y, far, far_x):
            for place in range(many):
                near[0, place] = block(place)
                near_y[0, place] = block(many + place)
            for place in range(2 * many):

                @pl.when(across == 0)
                def same():
                    far[place] = block(2 * many + place)

                @pl.when(across == 1)
                def other():
                    far_x[place] = block(2 * many + place)

        pl.when(own)(lambda: put(*outs[:4]))
        pl.when(jnp.logical_not(own))(lambda: put(*outs[4:8]))

    @pl.when(kind < 3)
    def projections():
        keep(product(grads_ref[0], normed_ref[...], 1, 0).astype(low))

    @pl.when(kind == 3)
    def output():
        keep(product(attended_ref[...], branch_ref[...], 1, 0).astype(low))


def kinds_grad(places, grads, attended, normed, branch, slabs):
    _, rows, tokens = grads.shape
    width = normed.shape[1]
    whole = pl.BlockSpec((tokens, width), lambda k, ref: (0, 0))
    many, each = slabs // 4, rows // slabs
    near = pl.BlockSpec((1, many, each, width), lambda k, ref: ((k ^ ref[0]) >> 1, 0, 0, 0))
    far = pl.BlockSpec((2 * many, each, width), lambda k, ref: (0, 0, 0))
    near_shape = jax.ShapeDtypeStruct((2, many, each, width), low)
    far_shape = jax.ShapeDtypeStruct((2 * many, each, width), low)
    return pl.pallas_call(
        partial(kinds_kernel, slabs),
        grid_spec=pltpu.PrefetchScalarGridSpec(
            num_scalar_prefetch=1,
            grid=(4,),
            in_specs=[
                pl.BlockSpec((1, rows, tokens), lambda k, ref: (jnp.minimum(k, 2), 0, 0)),
                pl.BlockSpec((rows, tokens), lambda k, ref: (0, 0)),
                whole,
                whole,
            ],
            out_specs=[near, near, far, far] * 2,
            scratch_shapes=[pltpu.VMEM((rows, width), low)],
        ),
        out_shape=[near_shape, near_shape, far_shape, far_shape] * 2,
        compiler_params=pltpu.CompilerParams(vmem_limit_bytes=48 * 2**20),
        cost_estimate=pl.CostEstimate(
            flops=rows * width * tokens, bytes_accessed=2**20, transcendentals=0
        ),
        name="kinds_grad",
    )(places, grads, attended, normed, branch)


def unite_kernel(kind_ref, *refs):
    outs = refs[4:]
    part = refs[0].shape[1]
    for distance in range(4):
        source = kind_ref[0] ^ distance
        for column in range(4):

            @pl.when(source == column)
            def put():
                start = 0
                for out in outs:
                    rows = out.shape[0]
                    out[:, column * part : (column + 1) * part] = refs[distance][
                        start : start + rows, :
                    ]
                    start += rows


def unite(kind, blocks, cuts):
    part = blocks[0].shape[1]
    local = pl.BlockSpec(memory_space=pltpu.VMEM)
    return pl.pallas_call(
        unite_kernel,
        in_specs=[pl.BlockSpec(memory_space=pltpu.SMEM)] + [local] * 4,
        out_specs=[local] * len(cuts),
        out_shape=[jax.ShapeDtypeStruct((rows, 4 * part), low) for rows in cuts],
        name="unite",
    )(kind, *blocks)


def divide_kernel(kind_ref, *refs):
    ins, outs = refs[:-4], refs[-4:]
    part = outs[0].shape[1]
    for distance in range(4):
        target = kind_ref[0] ^ distance
        for column in range(4):

            @pl.when(target == column)
            def put():
                start = 0
                for ref in ins:
                    rows = ref.shape[0]
                    outs[distance][start : start + rows, :] = ref[
                        :, column * part : (column + 1) * part
                    ]
                    start += rows


def divide(kind, owned):
    rows = sum(values.shape[0] for values in owned)
    part = owned[0].shape[1] // 4
    local = pl.BlockSpec(memory_space=pltpu.VMEM)
    return pl.pallas_call(
        divide_kernel,
        in_specs=[pl.BlockSpec(memory_space=pltpu.SMEM)] + [local] * len(owned),
        out_specs=[local] * 4,
        out_shape=[jax.ShapeDtypeStruct((rows, part), low)] * 4,
        name="divide",
    )(kind, *owned)


def settle_kernel(kind_ref, *refs):
    for distance in range(4):
        refs[4][kind_ref[0] ^ distance] = refs[distance][...].astype(wide)


def settle(kind, blocks):
    rows, part = blocks[0].shape
    local = pl.BlockSpec(memory_space=pltpu.VMEM)
    return pl.pallas_call(
        settle_kernel,
        in_specs=[pl.BlockSpec(memory_space=pltpu.SMEM)] + [local] * 4,
        out_specs=local,
        out_shape=jax.ShapeDtypeStruct((4, rows, part), wide),
        name="settle",
    )(kind, *blocks)


def after(values, *earlier):
    return lax.optimization_barrier((values, earlier))[0]


def add_low(*terms):
    total = terms[0].astype(wide)
    for term in terms[1:]:
        total = total + term.astype(wide)
    return total.astype(low)


def join(kinds, *blocks):
    width = blocks[0].shape[-1]
    parts = [block.reshape(kinds, -1, width) for block in blocks]
    return jnp.concatenate(parts, axis=1).reshape(-1, width)


class Hops:
    def __init__(self, dp_count, tensor_count):
        self.count = dp_count * tensor_count
        self.y, self.z = 1, (2, 4, 6)
        self.core, self.x = tensor_count, 2 * tensor_count
        self.near, self.far = (0, 2), (4, 6)

    def send(self, values, distance):
        pairs = [(place, place ^ distance) for place in range(self.count)]
        return lax.ppermute(values, everyone, pairs)

    def order(self):
        x, y = self.x, self.y
        near = [n ^ p ^ q for q in (0, y) for p in (0, x) for n in self.near]
        far = [n ^ p ^ q for q in (0, x) for p in (0, y) for n in self.far]
        return near + far

    def along_z(self, block):
        return [self.send(block, z) for z in self.z]

    def second_operands(self, kinds, block, arrived):
        z1, z2, z3 = arrived
        return join(kinds, block, z1), join(kinds, z2, z3)

    def sibling(self, *pieces):
        return [self.send(piece, self.core) for piece in pieces]

    def across_dp(self, blocks):
        return [blocks[0]] + [self.send(blocks[j], j * self.core) for j in (1, 2, 3)]


class Reduction:
    def __init__(self, hops, own, sibling, joined):
        self.hops, self.own, self.joined = hops, own, joined
        if joined:
            self.arrived = hops.send(sibling, hops.core)
        else:
            self.arrived = [hops.send(piece, hops.core) for piece in sibling]
        self.width = sibling[0].shape[-1]

    def part(self, place):
        return self.own[place], self.arrived[place]

    def halves(self, values):
        axis = 1 if self.joined else 0
        shape = (2, 2, 2, -1, self.width) if self.joined else (2, 2, -1, self.width)
        values = values.reshape(shape)
        return [lax.index_in_dim(values, place, axis, keepdims=False) for place in (0, 1)]

    def blocks(self, values):
        axis = 1 if self.joined else 0
        return [lax.index_in_dim(values, place, axis, keepdims=False) for place in (0, 1)]

    def ready_third(self):
        self.operands = add_low(*self.part(1)), add_low(*self.part(3))
        return self.operands

    def send_third(self):
        near, far = self.operands
        self.moved = self.hops.send(near, self.hops.y), self.hops.send(far, self.hops.x)

    def third(self):
        near, far = self.moved
        near, far = add_low(*self.part(0), near), add_low(*self.part(2), far)
        self.near, self.far = self.halves(near), self.halves(far)
        self.operands = self.near[1], self.far[1]
        return self.operands

    def send_second(self):
        near, far = self.operands
        self.moved = self.hops.send(near, self.hops.x), self.hops.send(far, self.hops.y)

    def second(self):
        near, far = self.moved
        near, far = add_low(self.near[0], near), add_low(self.far[0], far)
        self.near, self.far = self.blocks(near), self.blocks(far)
        self.operands = self.near[1], self.far[0], self.far[1]
        return self.operands

    def send_along_z(self):
        self.moved = [
            self.hops.send(v, z) for v, z in zip(self.operands, self.hops.z, strict=True)
        ]

    def along_z(self):
        return add_low(self.near[0], *self.moved)


def shards(
    dp_count,
    tensor_count,
    inputs,
    pad_mask,
    cotangent,
    attn_norm_gain,
    attn_norm_shift,
    w_query,
    b_query,
    w_key,
    w_value,
    b_value,
    w_out,
    b_out,
    mlp_norm_gain,
    mlp_norm_shift,
    w_up,
    b_up,
    w_down,
    b_down,
):
    half_rows, width = inputs.shape[1:]
    tokens = 2 * half_rows
    head_cols = w_query.shape[1]
    unit_cols = w_up.shape[1]
    quantum = 8 * dp_count
    slab_units = -(-unit_cols // quantum) * quantum
    by_hops = (dp_count, tensor_count) == (4, 8)
    dp_place, tensor_place = lax.axis_index("dp"), lax.axis_index("tensor")
    devices = dp_count * tensor_count
    here = (dp_place * tensor_count + tensor_place).astype(jnp.int32)
    col_start = tensor_place * head_cols
    side = tensor_place % 2
    pairs = [(place, place ^ 1) for place in range(tensor_count)]
    hops = Hops(dp_count, tensor_count)
    places = jnp.stack([dp_place, tensor_place]).astype(jnp.int32)
    places = places if by_hops else places * 0
    kind = places[:1]
    heads = head_cols * tensor_count // HEAD_DIM

    def swap(values):
        return lax.ppermute(values, "tensor", pairs)

    def one_slot(values, *earlier):
        kept = lax.dynamic_index_in_dim(values, side, 0, keepdims=False)
        sent = lax.dynamic_index_in_dim(values, 1 - side, 0, keepdims=False)
        if earlier:
            sent = after(sent, *earlier)
        return jnp.concatenate([kept, swap(sent)], axis=0)

    def both_micros(kept, other):
        return jnp.where(side == 0, jnp.stack([kept, other]), jnp.stack([other, kept]))

    unit_pad = ((0, slab_units - unit_cols), (0, 0))
    up_cols, down_cols = jnp.pad(w_up.T, unit_pad), jnp.pad(w_down, unit_pad)
    attn_cols = jnp.concatenate([w_query.T, w_key.T, w_value.T, w_out], axis=0)
    if by_hops:
        unit_cuts = (48, slab_units // 4 - 48)
        first_units = 4 * unit_cuts[0]
        share = lambda values, low_end, high_end: values[low_end:high_end].reshape(
            4, -1, values.shape[1]
        )
        mlp_cols = jnp.concatenate(
            [
                share(up_cols, 0, first_units),
                share(down_cols, 0, first_units),
                share(up_cols, first_units, slab_units),
                share(down_cols, first_units, slab_units),
            ],
            axis=1,
        )
        attn_cols = attn_cols.reshape(4, head_cols, -1)
        pick = lambda values, j: lax.dynamic_index_in_dim(
            values, dp_place ^ j, 0, keepdims=False
        )
        attn_blocks = hops.across_dp([pick(attn_cols, j) for j in range(4)])
        (attn_block,) = unite(kind, attn_blocks, (head_cols,))
        mlp_blocks = hops.across_dp([pick(mlp_cols, j) for j in range(4)])
        bulk_block, hop_block = unite(kind, mlp_blocks, [2 * rows for rows in unit_cuts])
        attn_rows = lax.all_gather(attn_block, everyone).reshape(4, -1, width)
        x_slot = one_slot(inputs)
        grad_out = one_slot(cotangent, x_slot)
        bulk_weights = lax.all_gather(bulk_block, everyone)
        hop_z = hops.along_z(hop_block)
        order = hops.order()
        order = [place ^ hops.core for place in order] + order
        unit_places = here ^ jnp.array(order)
        unit_here = (unit_places[:, None] == jnp.arange(devices)[None, :]).astype(wide)
        shuffled = partial(jnp.dot, precision=lax.Precision.HIGHEST)
    else:
        x_slot, grad_out = one_slot(inputs), one_slot(cotangent)
        unit_cuts = (slab_units // dp_count,)

        def gathered(values):
            owned = lax.all_to_all(
                values.reshape(dp_count, -1, values.shape[1]), "dp", 0, 2, tiled=True
            )
            return lax.all_gather(owned[0], everyone, axis=0, tiled=True)

        attn_rows = gathered(attn_cols)
        attn_rows = attn_rows.reshape(4, dp_count // 4, tensor_count, -1, width)
        attn_rows = attn_rows.transpose(0, 2, 1, 3, 4).reshape(4, -1, width)
        columns = [values.reshape(dp_count, -1, values.shape[1]) for values in (up_cols, down_cols)]
        unit_weights = gathered(jnp.concatenate(columns, axis=1).reshape(2 * slab_units, -1))
        unit_weights = unit_weights.reshape(32, devices // 32, 2, -1, width)
        bulk_weights = unit_weights.transpose(0, 2, 1, 3, 4).reshape(32, -1, width)

    slab_bias = jnp.pad(
        b_up.reshape(tensor_count, unit_cols), ((0, 0), (0, slab_units - unit_cols))
    )
    unit_starts = [dp_count * sum(unit_cuts[:i]) for i in range(len(unit_cuts) + 1)]

    def unit_bias(part):
        values = slab_bias[:, unit_starts[part] : unit_starts[part + 1]]
        values = values.reshape(tensor_count, dp_count, -1).transpose(1, 0, 2)
        if part == 1:
            values = shuffled(unit_here, values.reshape(devices, -1))
        return values.reshape(-1, 1)

    def unit_grads(values):
        slabs = []
        for place, part in enumerate(values):
            if place == 1:
                part = shuffled(unit_here.T, part.reshape(devices, -1))
            part = part.reshape(dp_count, tensor_count, -1).transpose(1, 0, 2)
            slabs.append(part.reshape(tensor_count, -1))
        return jnp.concatenate(slabs, axis=1)

    mask_row = lax.dynamic_slice(pad_mask, (side, tensor_place // 2, 0), (1, 1, tokens))
    mask_row = mask_row.reshape(2, half_rows)
    mask_row = jnp.where(side == 0, mask_row, mask_row[::-1]).reshape(tokens, 1)
    bias_col = jnp.where(mask_row > 0, 0.0, masked_score).astype(wide)

    normed_first = norm_forward(x_slot.astype(wide), attn_norm_gain, attn_norm_shift)
    qkv_rows, out_rows = attn_rows[:3].reshape(-1, width), attn_rows[3]
    qkv_bias = jnp.concatenate([b_query, jnp.zeros_like(b_query), b_value])
    projected = (product(qkv_rows, normed_first, 1, 1) + qkv_bias[:, None]).astype(low)
    if by_hops:
        hop_z = after(hop_z, grad_out, normed_first)
    if by_hops:
        hop_near, hop_far = hops.second_operands(2, hop_block, hop_z)
        near_x, far_y = hops.send(hop_near, hops.x), hops.send(hop_far, hops.y)
        near_x, far_y = after((near_x, far_y))
        hop_near, hop_far = join(2, hop_near, near_x), join(2, hop_far, far_y)
        attended, totals = attend(projected, bias_col, heads, 4)
        near_y, far_x = hops.send(hop_near, hops.y), hops.send(hop_far, hops.x)
        near_y, far_x = after((near_y, far_x), attended)
        hop_three = [hop_near, near_y, hop_far, far_x]
        hop_sibling = hops.sibling(*hop_three)
    else:
        attended, totals = attend(projected, bias_col, heads, 4)
    branch = product(attended, out_rows, 0, 0) + b_out
    middle = x_slot.astype(wide) + branch
    normed_second = norm_forward(middle, mlp_norm_gain, mlp_norm_shift)
    rows = unit_cuts[0] * devices // 32
    sums, up_sums = None, []
    if by_hops:
        hop_bias = jnp.split(unit_bias(1), 2)
        hop_rows = unit_cuts[1]
        hop_mlp = partial(mlp, normed_second, grad_out)
        *sums, grad_sibling, sibling_sum = hop_mlp(
            hop_bias[0], hop_sibling, (0, 4 * hop_rows), hop_rows
        )
        units = Reduction(hops, None, grad_sibling, True)
        *sums, units.own, own_sum = hop_mlp(
            hop_bias[1], hop_three, (0, 4 * hop_rows), hop_rows, 8, sums
        )
        up_sums.append(jnp.concatenate([sibling_sum[:, 0], own_sum[:, 0]]))
        units.arrived = after(units.arrived, sums)
    bulk = partial(
        mlp,
        normed_second,
        grad_out,
        unit_bias(0),
        [bulk_weights],
        (0, rows),
        rows,
        16 if by_hops else 4,
    )
    if by_hops:
        sums = after(sums, units.ready_third())
        units.send_third()
        *sums, bulk_grads, up_sum = bulk(sums)
    else:
        *sums, bulk_grads, up_sum = bulk()
    up_sums = [up_sum[:, 0]] + up_sums
    bulk_grads = bulk_grads.reshape(32, 2, devices // 32, -1, width).transpose(0, 2, 1, 3, 4)
    bulk_owned = lax.psum_scatter(
        bulk_grads.reshape(2 * 32 * rows, width), everyone, scatter_dimension=0, tiled=True
    )
    down_out, grad_normed_second = sums
    if by_hops:
        units_third = units.third()
        grad_normed_second = after(grad_normed_second, units_third)
    grad_middle, grad_branch, second_sums, out_kept, out_sent = norm_back(
        middle, grad_normed_second, mlp_norm_gain, grad_out, down_out, b_down
    )
    back = partial(
        attend_back, projected, bias_col, attended, totals, attn_rows.reshape(-1, width)
    )
    if by_hops:
        units.send_second()
        out_other = swap(out_sent)
        grads = back(grad_branch, heads, 4)
        grads, out_other = after((grads, out_other), units.second())
        layer_out = both_micros(out_kept, out_other)
        units.send_along_z()
        kind_grads = kinds_grad(
            places, grads, attended, normed_first, grad_branch, tensor_count
        )
        attns = Reduction(hops, kind_grads[:4], kind_grads[4:], False)
        grads = after(grads, kind_grads)
        first_terms = product(grads.reshape(-1, tokens), qkv_rows, 0, 0)
        units.moved = after(units.moved, first_terms)
        first_terms = after(first_terms, attns.ready_third())
        attns.send_third()
        input_full, input_low, first_sums = norm_back(
            x_slot, first_terms, attn_norm_gain, grad_middle
        )
        units_owned = units.along_z()
        attns.moved = after(attns.moved, units_owned)
        attns_third = attns.third()
    else:
        grads = back(grad_branch, heads, 4)
        first_terms = product(grads.reshape(-1, tokens), qkv_rows, 0, 0)
        input_full, input_low, first_sums = norm_back(
            x_slot, first_terms, attn_norm_gain, grad_middle
        )
        out_other = swap(out_sent)
        layer_out = both_micros(out_kept, out_other)

    total_over = lambda i: jnp.sum(grads[i], axis=1, dtype=wide)
    small = jnp.concatenate(
        [
            second_sums.reshape(-1),
            first_sums[:2].reshape(-1),
            total_over(0),
            total_over(2),
            unit_grads(up_sums).reshape(-1),
        ]
    )
    if by_hops:
        small, mlp_owned = after(
            (small.reshape(-1, 128), [bulk_owned, units_owned[0], units_owned[1]]), attns_third
        )
        attns.send_second()
        small = small + sum(hops.send(small, z) for z in hops.z)
        mlp_parts = divide(kind, mlp_owned)
        attns.moved = after(attns.moved, small, mlp_parts)
        attns_second = attns.second()
        attns.send_along_z()
        small, input_low, mlp_parts = after((small, input_low, mlp_parts), attns_second)
        input_other = swap(input_low[half_rows:])
        mlp_blocks = hops.across_dp(mlp_parts)
        mlp_back = settle(kind, mlp_blocks)
        attns.moved = after(attns.moved, mlp_back, input_other)
        small = after(small, attns.moved)
        small = small + hops.send(small, hops.y)
        small = small + sum(hops.send(small, j * hops.core) for j in (1, 2, 3))
        attn_parts = divide(kind, [attns.along_z()])
        attn_back = settle(kind, hops.across_dp(attn_parts))
        small = small.reshape(-1)
    else:
        small = lax.psum(small, everyone)
        input_other = swap(input_low[half_rows:])
    input_grad = both_micros(input_full[:half_rows], input_other.astype(wide))

    if by_hops:
        bounds = [0]
        for rows in (unit_cuts[0], unit_cuts[0], unit_cuts[1], unit_cuts[1]):
            bounds.append(bounds[-1] + rows)
        parts = [
            mlp_back[:, bounds[i] : bounds[i + 1]].reshape(-1, mlp_back.shape[2])
            for i in range(4)
        ]
        grad_w_up = jnp.concatenate([parts[0], parts[2]], axis=0)
        grad_w_down = jnp.concatenate([parts[1], parts[3]], axis=0)
    else:

        def to_columns(owned):
            back = lax.all_to_all(owned[None], "dp", 2, 0, tiled=True)
            return back.reshape(-1, width // dp_count).astype(wide)

        columns = to_columns(bulk_owned)
        columns = columns.reshape(dp_count, 2, -1, columns.shape[1])
        grad_w_up = columns[:, 0].reshape(-1, columns.shape[3])
        grad_w_down = columns[:, 1].reshape(-1, columns.shape[3])
        flat = grads.reshape(-1, tokens)
        terms = [product(flat, normed_first, 1, 0), product(attended, grad_branch, 1, 0)]
        terms = jnp.concatenate(terms, axis=0).astype(low)
        terms = terms.reshape(4, tensor_count, dp_count // 4, -1, width)
        terms = terms.transpose(0, 2, 1, 3, 4).reshape(-1, width)
        owned = lax.psum_scatter(terms, everyone, scatter_dimension=0, tiled=True)
        attn_back = to_columns(owned).reshape(4, head_cols, -1)

    part = lambda i: small[i * width : (i + 1) * width]
    up_all = small[8 * width :].reshape(tensor_count, slab_units)
    return (
        layer_out,
        input_grad,
        part(4),
        part(5),
        attn_back[0].T,
        lax.dynamic_slice_in_dim(part(6), col_start, head_cols),
        attn_back[1].T,
        attn_back[2].T,
        lax.dynamic_slice_in_dim(part(7), col_start, head_cols),
        attn_back[3],
        part(2),
        part(0),
        part(1),
        grad_w_up[:unit_cols].T,
        up_all[:, :unit_cols].reshape(-1),
        grad_w_down[:unit_cols],
        part(3),
    )


def solution(mesh):
    tokens = P(None, ("dp", "tensor"), None)
    columns = P("dp", "tensor")
    rows = P("tensor", "dp")
    return jax.shard_map(
        partial(shards, mesh.shape["dp"], mesh.shape["tensor"]),
        mesh=mesh,
        in_specs=(
            tokens,
            P(None, "dp", None),
            tokens,
            P(),
            P(),
            columns,
            P(),
            columns,
            columns,
            P(),
            rows,
            P(),
            P(),
            P(),
            columns,
            P(),
            rows,
            P(),
        ),
        out_specs=(
            tokens,
            tokens,
            P(),
            P(),
            columns,
            P("tensor"),
            columns,
            columns,
            P("tensor"),
            rows,
            P(),
            P(),
            P(),
            columns,
            P(),
            rows,
            P(),
        ),
        check_vma=False,
    )
```
